512 devices in a mesh: scene: 64 (over z_lo, x, core), tile: 8 (over z_hi, y).
Axes of the slice: x: 4, y: 4, z: 16 (z_hi: 2, z_lo: 8; z = z_hi * 8 + z_lo), core: 2. Of those that a mesh axis runs over, the one named last changes fastest.
Arguments:
- radiance: bfloat16 [512, 8, 10, 8192], P(('scene', 'tile')), may hold values from -8 to 8
- cloud_weight: int32 [512, 8, 8192], P(('scene', 'tile')), may hold values from 0 to 15
- footprint: int32 [512, 8], replicated, may hold values from 0 to 63, as said below
Outputs:
- composite: bfloat16 [64, 10, 8192], P('tile', None, 'scene')
- overview_one: bfloat16 [64, 10, 64, 32], P('tile')
- overview_two: bfloat16 [64, 10, 32, 16], P('tile')
- overview_three: bfloat16 [64, 10, 16, 8], P('tile')
- overview_four: bfloat16 [64, 10, 8, 4], P('tile')
- overview_five: bfloat16 [64, 10, 4, 2], P('tile')
The draws below stay inside these ranges and needn't reach their ends.
Inputs may be any that keep to these rules, and one draw needn't show every extreme that they name: `footprint`: each row names 8 different tiles; at most 2 tiles of a row share the value of tile // 8, and in every row some such group holds exactly 2 tiles.
All inputs are finite; a program needn't handle non-finite values.
Results may differ from the reference program's by a relative error of at most 0.012.
Values may be sent and summed in bfloat16 or wider, within the bound.
A program may use at most 128 MiB of HBM per device.

```python
import jax
import jax.numpy as jnp
from jax import lax

BANDS = 10
K = 8
TILE_DEV = 8
COLS = 64
CAP = 2
SCENES = 512
TILES = 64
ROWS = 128
PIX = 8192


def footprint_table(key):
    owners = TILES // TILE_DEV
    base_key = jax.random.fold_in(key, 11)
    scene_keys = jax.random.split(jax.random.fold_in(base_key, 2), SCENES)
    first_flags = jnp.arange(SCENES) == 0
    owner_of = jnp.repeat(jnp.arange(owners), CAP)
    positions = jnp.arange(TILE_DEV)

    def pick_local(inner_key, forced):
        order = jax.random.permutation(inner_key, TILE_DEV)
        head = order[0]
        moved = jnp.where(order == TILE_DEV - 1, head, order)
        moved = jnp.where(positions == 0, TILE_DEV - 1, moved)
        chosen = jnp.where(forced, moved, order)
        return chosen[:CAP]

    def one_scene(scene_key, is_first):
        first_key, second_key, third_key = jax.random.split(scene_key, 3)
        favored = jax.random.randint(third_key, (), 0, owners)
        favored = jnp.where(is_first, owners - 1, favored)
        local_keys = jax.random.split(first_key, owners)
        forced = jnp.logical_and(is_first, jnp.arange(owners) == owners - 1)
        local_pick = jax.vmap(pick_local)(local_keys, forced)
        candidate = (jnp.arange(owners)[:, None] * TILE_DEV + local_pick).reshape(-1)
        scores = jax.random.permutation(second_key, owners * CAP)
        scores = scores + jnp.where(owner_of == favored, owners * CAP, 0)
        ranking = jnp.argsort(-scores, stable=True)
        return candidate[ranking[:K]]
    return jax.vmap(one_scene)(scene_keys, first_flags).astype(jnp.int32)


def draw_footprint(key, part):
    return footprint_table(key)


def draw_cloud_weight(key, part):
    table = footprint_table(key)
    gaps = jax.random.randint(jax.random.fold_in(key, 23), (TILES, PIX), 0, 48) == 0
    clouds = jnp.maximum(jax.random.randint(jax.random.fold_in(key, 29), (SCENES, K, PIX), -6, 16), 0)
    return jnp.where(gaps[table], 0, clouds).astype(jnp.int32)


def block_scale(rng, shape, cuts, smallest, top_value):
    gain = 1.0
    for position, blocks in cuts:
        draws = jax.random.uniform(jax.random.fold_in(jax.random.fold_in(rng, 6), position), (blocks,), jnp.float32, smallest / len(cuts), top_value / len(cuts))
        gain = gain * jnp.repeat(jnp.exp(draws), shape[position] // blocks).reshape((-1,) + (1,) * (len(shape) - 1 - position))
    return gain


def gaussian(stream_key, extent, spread, limit, pieces=(), kind=jnp.bfloat16):
    entries = spread * jax.random.normal(stream_key, extent, jnp.float32)
    if pieces:
        entries = entries * block_scale(stream_key, extent, pieces, -0.22, 0.18)
    return jnp.clip(entries, -limit, limit).astype(kind)


def setup_inputs(seed: int = 0) -> dict:
    seeds = jax.random.split(jax.random.key(seed), 4)
    return {
        "radiance": gaussian(seeds[0], (SCENES, K, BANDS, PIX), 2.0, 8.0, ((0, 512),)),
        "cloud_weight": draw_cloud_weight(jax.random.fold_in(seeds[3], 71), 0),
        "footprint": draw_footprint(jax.random.fold_in(seeds[3], 71), 0),
    }


def average_pool(values):
    height = values.shape[-2]
    width = values.shape[-1]
    shaped = values.astype(jnp.float32).reshape(values.shape[:-2] + (height // 2, 2, width // 2, 2))
    return jnp.mean(shaped, axis=(-3, -1)).astype(jnp.bfloat16)


def reference(radiance, cloud_weight, footprint):
    group = 16
    blocks = SCENES // group
    rad_blocks = radiance.reshape(blocks, group, K, BANDS, PIX)
    weight_blocks = cloud_weight.reshape(blocks, group, K, PIX)
    tile_blocks = footprint.reshape(blocks, group * K).astype(jnp.int32)

    def accumulate(carry, inputs):
        weighted_sums, weight_totals = carry
        rad_part, weight_part, tile_part = inputs
        weight_float = weight_part.astype(jnp.float32)
        product = weight_float[:, :, None, :] * rad_part.astype(jnp.float32)
        weighted_sums = weighted_sums.at[tile_part].add(product.reshape(group * K, BANDS, PIX))
        weight_totals = weight_totals.at[tile_part].add(weight_float.reshape(group * K, PIX))
        return (weighted_sums, weight_totals), None

    start = (jnp.zeros((TILES, BANDS, PIX), jnp.float32), jnp.zeros((TILES, PIX), jnp.float32))
    (weighted_sums, weight_totals), _ = lax.scan(accumulate, start, (rad_blocks, weight_blocks, tile_blocks))
    composite = (weighted_sums / jnp.maximum(weight_totals, 1.0)[:, None, :]).astype(jnp.bfloat16)
    grid = composite.reshape(TILES, BANDS, ROWS, COLS)
    overview_one = average_pool(grid)
    overview_two = average_pool(overview_one)
    overview_three = average_pool(overview_two)
    overview_four = average_pool(overview_three)
    overview_five = average_pool(overview_four)
    return (composite, overview_one, overview_two, overview_three, overview_four, overview_five)
```

```python
import functools

import jax
import jax.numpy as jnp
from jax import lax
from jax.experimental import pallas as pl
from jax.experimental.pallas import tpu as pltpu
from jax.sharding import PartitionSpec as P

MESH = pl.DeviceIdType.MESH
K = 8
BANDS = 10
TILES = 64
PIX = 8192
LANES = 128
MSG = 96
BOX = 64
F32 = jnp.float32
BF16 = jnp.bfloat16


def offsets(i):
    dx = lax.rem(i, 4)
    dy = lax.rem(lax.div(i, 4) + i, 4)
    dc = lax.rem(lax.div(i, 16), 2)
    dz = lax.div(i, 32)
    return dx, dy, dc, dz


def position():
    scene = lax.axis_index("scene")
    tile = lax.axis_index("tile")
    z_lo = lax.div(scene, 8)
    x = lax.rem(lax.div(scene, 2), 4)
    core = lax.rem(scene, 2)
    z_hi = lax.div(tile, 4)
    y = lax.rem(tile, 4)
    return z_lo, x, core, z_hi, y


def exchange_kernel(
    rad_ref, weight_ref, foot_ref, rows_ref, comp_ref,
    rad, weight, foot, turn, send, recv, assign, acc, send3, recv3, line,
    in_sem, send_sem, recv_sem, send3_sem, recv3_sem, sg1_sem, rg1_sem, sg2_sem, rg2_sem,
):
    z_lo, x, core, z_hi, y = position()
    tile = z_hi * 4 + y
    xc = x * 2 + core
    pair = lax.div(z_lo, 2)
    odd = lax.rem(z_lo, 2)

    load_foot = pltpu.make_async_copy(foot_ref.at[pl.ds(pl.multiple_of(pair * 128, 128), 128)], foot, in_sem.at[2])
    load_weight = pltpu.make_async_copy(weight_ref.at[0], weight, in_sem.at[1])
    load_rad = pltpu.make_async_copy(rad_ref.at[0], rad, in_sem.at[0])
    load_weight.start()
    load_rad.start()
    load_foot.start()

    def box_device(i):
        dx, dy, dc, dz = offsets(i)
        x2 = lax.rem(x + dx, 4)
        y2 = lax.rem(y + dy, 4)
        c2 = lax.rem(core + dc, 2)
        o2 = lax.rem(odd + dz, 2)
        block = (2 * y2 + o2) * 8 + x2 * 2 + c2
        return block, ((2 * pair + o2) * 8 + x2 * 2 + c2, z_hi * 4 + y2)

    def owner_device(o):
        return ((2 * y + odd) * 8 + xc, o)

    def source_device(s):
        return ((2 * lax.rem(s, 4) + odd) * 8 + xc, lax.div(s, 4) * 4 + pair)

    my_source = z_hi * 4 + pair
    at_home = pair == y

    barrier = pltpu.get_barrier_semaphore()

    def greet_box(i, _):
        _, device = box_device(i)
        pl.semaphore_signal(barrier, inc=1, device_id=device, device_id_type=MESH)
        return 0

    lax.fori_loop(1, BOX, greet_box, 0)

    def greet_source(s, _):
        @pl.when(jnp.logical_not(jnp.logical_and(at_home, s == my_source)))
        def _():
            pl.semaphore_signal(barrier, inc=1, device_id=source_device(s), device_id_type=MESH)
        return 0

    lax.fori_loop(0, 8, greet_source, 0)

    def line_device(i):
        z2 = lax.rem(z_lo + i, 8)
        return z2, (z2 * 8 + xc, tile)

    def greet_line(i, _):
        pl.semaphore_signal(barrier, inc=1, device_id=line_device(i)[1], device_id_type=MESH)
        return 0

    lax.fori_loop(1, 8, greet_line, 0)

    load_foot.wait()
    lane = lax.broadcasted_iota(jnp.int32, (128, 16 * BOX), 1)
    row = lax.broadcasted_iota(jnp.int32, (128, 16 * BOX), 0)
    slot = lax.div(lane, 16)
    dx, dy, dc, dz = offsets(slot)
    source_row = (
        lax.rem(odd + dz, 2) * 64
        + lax.rem(x + 4 - dx, 4) * 16
        + lax.rem(core + dc, 2) * 8
        + z_hi * 4
        + lax.rem(y + 4 - dy, 4)
    )
    pick = jnp.where(row == source_row, 1.0, 0.0).astype(BF16)
    named = lax.dot_general(
        foot[...].astype(F32).astype(BF16), pick, (((0,), (0,)), ((), ())), preferred_element_type=F32
    )
    own = lax.broadcasted_iota(jnp.int32, (K, 16 * BOX), 0) == lax.rem(
        lax.broadcasted_iota(jnp.int32, (K, 16 * BOX), 1), 8
    )
    target = jnp.sum(jnp.where(own, named, 0.0), axis=0, keepdims=True)
    half = lax.rem(lax.div(lane, 8), 2)
    wanted = jnp.where(lax.div(row, 64) == half, lax.rem(row, 64).astype(F32), -1.0)
    assign[...] = jnp.where(wanted == target, 1.0, 0.0).astype(BF16)

    load_weight.wait()
    load_rad.wait()
    pl.semaphore_wait(barrier, BOX - 1 + 7 + 8 - jnp.where(at_home, 1, 0))

    def fill(block, out):
        pixels = pl.ds(pl.multiple_of(block * LANES, LANES), LANES)
        for k in range(K):
            turn[16 * k : 16 * k + BANDS, :] = rad[k, :, pixels].astype(F32)
        w = weight[:, pixels].astype(F32)
        for j in range(5):
            low = turn[pl.ds(2 * j, K, stride=16), :] * w
            high = turn[pl.ds(2 * j + 1, K, stride=16), :] * w
            out[16 * j : 16 * j + 16, :] = jnp.concatenate([low, high], axis=0).astype(BF16)
        out[80:96, :] = jnp.concatenate([w, jnp.zeros_like(w)], axis=0).astype(BF16)

    def box_copy(i):
        block, device = box_device(i)
        copy = pltpu.make_async_remote_copy(
            src_ref=send.at[i], dst_ref=recv.at[i], send_sem=send_sem.at[i], recv_sem=recv_sem.at[i],
            device_id=device, device_id_type=MESH,
        )
        return block, copy

    def send_box(i, _):
        block, copy = box_copy(i)
        fill(block, send.at[i])
        copy.start()
        return 0

    lax.fori_loop(1, BOX, send_box, 0)
    fill((2 * y + odd) * 8 + xc, recv.at[0])

    def wait_box(i, _):
        box_copy(i)[1].wait_recv()
        return 0

    for g in range(4):
        lax.fori_loop(max(16 * g, 1), 16 * g + 16, wait_box, 0)
        left = assign[:, 256 * g : 256 * g + 256]
        for j in range(0, 6, 2):
            right = jnp.concatenate(
                [recv[16 * g : 16 * g + 16, 16 * h : 16 * h + 16, :].reshape(256, LANES) for h in (j, j + 1)], axis=1
            )
            part = jnp.dot(left, right, preferred_element_type=F32)
            if g == 0:
                acc[:, LANES * j : LANES * j + 2 * LANES] = part
            else:
                acc[:, LANES * j : LANES * j + 2 * LANES] += part

    for o in range(8):
        for j in range(6):
            lanes = slice(LANES * j, LANES * j + LANES)
            both = jnp.concatenate([acc[8 * o : 8 * o + 8, lanes], acc[64 + 8 * o : 72 + 8 * o, lanes]], axis=0)
            send3[o, 16 * j : 16 * j + 16, :] = both.astype(BF16)

    def owner_copy(o):
        return pltpu.make_async_remote_copy(
            src_ref=send3.at[o], dst_ref=recv3.at[my_source], send_sem=send3_sem.at[o], recv_sem=recv3_sem.at[my_source],
            device_id=owner_device(o), device_id_type=MESH,
        )

    def stays(o):
        return jnp.logical_and(at_home, o == tile)

    def send_owner(i, _):
        o = lax.rem(tile + i, 8)

        @pl.when(jnp.logical_not(stays(o)))
        def _():
            owner_copy(o).start()
        return 0

    lax.fori_loop(0, 8, send_owner, 0)

    @pl.when(at_home)
    def _():
        recv3[my_source] = send3[tile]

    def wait_source(s, _):
        @pl.when(jnp.logical_not(jnp.logical_and(at_home, s == my_source)))
        def _():
            pltpu.make_async_remote_copy(
                src_ref=send3.at[s], dst_ref=recv3.at[s], send_sem=send3_sem.at[s], recv_sem=recv3_sem.at[s],
                device_id=source_device(s), device_id_type=MESH,
            ).wait_recv()
        return 0

    lax.fori_loop(0, 8, wait_source, 0)

    total = recv3[0].astype(F32)
    for s in range(1, 8):
        total = total + recv3[s].astype(F32)
    scale = jnp.maximum(total[80:88, :], 1.0)
    mean = [(total[8 * b : 8 * b + 8, :] / scale).astype(BF16).astype(F32) for b in range(BANDS)]
    comp_ref[...] = jnp.concatenate(mean, axis=0)

    blank = jnp.zeros((8, LANES), F32)
    mean = mean + [blank] * 3
    pixel = lax.broadcasted_iota(jnp.int32, (LANES, LANES), 0)
    spot = lax.broadcasted_iota(jnp.int32, (LANES, LANES), 1)
    pooled = None
    for g in range(4):
        left = jnp.concatenate([mean[3 * g + b] if b < 3 else blank for b in range(4)], axis=0).astype(BF16)
        mix = jnp.where(spot == 32 * g + lax.div(lax.rem(pixel, 64), 2), 0.25, 0.0).astype(BF16)
        part = jnp.dot(left, mix, preferred_element_type=F32)
        pooled = part if pooled is None else pooled + part
    line[z_lo] = pooled.astype(BF16)

    def line_copy(i):
        return pltpu.make_async_remote_copy(
            src_ref=line.at[z_lo], dst_ref=line.at[z_lo], send_sem=sg1_sem.at[i], recv_sem=rg1_sem.at[z_lo],
            device_id=line_device(i)[1], device_id_type=MESH,
        )

    def send_line(i, _):
        line_copy(i).start()
        return 0

    lax.fori_loop(1, 8, send_line, 0)

    def wait_line(i, _):
        z2, device = line_device(i)
        pltpu.make_async_remote_copy(
            src_ref=line.at[z2], dst_ref=line.at[z2], send_sem=sg1_sem.at[i], recv_sem=rg1_sem.at[z2],
            device_id=device, device_id_type=MESH,
        ).wait_recv()
        return 0

    lax.fori_loop(1, 8, wait_line, 0)

    def plane_device(i):
        xc2 = lax.rem(xc + i, 8)
        return xc2, (z_lo * 8 + xc2, tile)

    def plane_copy(i):
        return pltpu.make_async_remote_copy(
            src_ref=line, dst_ref=rows_ref.at[xc], send_sem=sg2_sem.at[i], recv_sem=rg2_sem.at[xc],
            device_id=plane_device(i)[1], device_id_type=MESH,
        )

    def send_plane(i, _):
        plane_copy(i).start()
        return 0

    lax.fori_loop(1, 8, send_plane, 0)
    rows_ref[xc] = line[...]

    def wait_plane(i, _):
        xc2, device = plane_device(i)
        pltpu.make_async_remote_copy(
            src_ref=line, dst_ref=rows_ref.at[xc2], send_sem=sg2_sem.at[i], recv_sem=rg2_sem.at[xc2],
            device_id=device, device_id_type=MESH,
        ).wait_recv()
        return 0

    lax.fori_loop(1, 8, wait_plane, 0)

    def drain_box(i, _):
        box_copy(i)[1].wait_send()
        return 0

    lax.fori_loop(1, BOX, drain_box, 0)

    def drain_owner(o, _):
        @pl.when(jnp.logical_not(stays(o)))
        def _():
            owner_copy(o).wait_send()
        return 0

    lax.fori_loop(0, 8, drain_owner, 0)

    def drain_rows(i, _):
        line_copy(i).wait_send()
        plane_copy(i).wait_send()
        return 0

    lax.fori_loop(1, 8, drain_rows, 0)


def exchange(radiance, cloud_weight, footprint):
    any_space = pl.BlockSpec(memory_space=pl.ANY)
    vmem = pl.BlockSpec(memory_space=pltpu.VMEM)
    dma = pltpu.SemaphoreType.DMA
    return pl.pallas_call(
        exchange_kernel,
        out_shape=(
            jax.ShapeDtypeStruct((8, 8, 32, LANES), BF16),
            jax.ShapeDtypeStruct((80, LANES), F32),
        ),
        in_specs=[any_space] * 3,
        out_specs=(vmem, vmem),
        scratch_shapes=[
            pltpu.VMEM((K, BANDS, PIX), BF16),
            pltpu.VMEM((K, PIX), jnp.int32),
            pltpu.VMEM((128, K), jnp.int32),
            pltpu.VMEM((128, LANES), F32),
            pltpu.VMEM((BOX, MSG, LANES), BF16),
            pltpu.VMEM((BOX, MSG, LANES), BF16),
            pltpu.VMEM((128, 16 * BOX), BF16),
            pltpu.VMEM((128, 6 * LANES), F32),
            pltpu.VMEM((8, MSG, LANES), BF16),
            pltpu.VMEM((8, MSG, LANES), BF16),
            pltpu.VMEM((8, 32, LANES), BF16),
            dma((3,)),
            dma((BOX,)),
            dma((BOX,)),
            dma((8,)),
            dma((8,)),
            dma((8,)),
            dma((8,)),
            dma((8,)),
            dma((8,)),
        ],
        compiler_params=pltpu.CompilerParams(
            collective_id=0, has_side_effects=True, vmem_limit_bytes=40 * 1024 * 1024
        ),
        name="exchange",
    )(radiance, cloud_weight, footprint)


def pyramid_kernel(rows_ref, comp_ref, composite, one, two, three, four, five, t1, t2, t3, t4, t5):
    for t in range(8):
        composite[t] = comp_ref[pl.ds(t, BANDS, stride=8), :].astype(BF16)

    before = lax.broadcasted_iota(jnp.int32, (LANES, LANES), 0)
    after = lax.broadcasted_iota(jnp.int32, (LANES, LANES), 1)
    same = lax.div(before, 32) == lax.div(after, 32)
    mix = jnp.where(
        jnp.logical_and(same, lax.div(lax.rem(before, 32), 2) == lax.rem(after, 32)), 0.25, 0.0
    ).astype(BF16)

    def halve(values):
        n = values.shape[0]
        flat = values.reshape(-1, LANES)
        wide = jnp.dot(flat, mix, preferred_element_type=F32).reshape(n, -1, LANES)
        return wide

    def keep(scratch, row, values):
        for i in range(8):
            at = row(i) * 24
            scratch[at : at + 24, :] = values[i, 0:24, :].astype(F32)

    level = [rows_ref[xc] for xc in range(8)]
    for xc in range(8):
        keep(t1, lambda i, xc=xc: i * 8 + xc, level[xc])
    for scratch, m in ((t2, 4), (t3, 2), (t4, 1)):
        level = [(halve(level[2 * q]) + halve(level[2 * q + 1])).astype(BF16) for q in range(m)]
        for q in range(m):
            keep(scratch, lambda i, q=q, m=m: i * m + q, level[q])
    last = halve(level[0])
    for i in range(4):
        both = (last[2 * i] + last[2 * i + 1]).astype(BF16)
        t5[24 * i : 24 * i + 24, :] = both[0:24, :].astype(F32)

    for scratch, out, height, width in (
        (t1, one, 64, 32), (t2, two, 32, 16), (t3, three, 16, 8), (t4, four, 8, 4), (t5, five, 4, 2)
    ):
        for r in range(24):
            lines = scratch[pl.ds(r, height, stride=24), :].astype(BF16)
            for g in range(4):
                b = 3 * g + r // 8
                if b < BANDS:
                    out[r % 8, b] = lines[:, 32 * g : 32 * g + width]


def pyramid(rows, comp):
    vmem = pl.BlockSpec(memory_space=pltpu.VMEM)
    shapes = [(8, BANDS, LANES)] + [(8, BANDS, 64 >> i, 32 >> i) for i in range(5)]
    return pl.pallas_call(
        pyramid_kernel,
        out_shape=[jax.ShapeDtypeStruct(s, BF16) for s in shapes],
        in_specs=[vmem] * 2,
        out_specs=[vmem] * 6,
        scratch_shapes=[pltpu.VMEM((24 * (64 >> i), LANES), F32) for i in range(5)],
        compiler_params=pltpu.CompilerParams(vmem_limit_bytes=40 * 1024 * 1024),
        name="pyramid",
    )(rows, comp)


def on_device(radiance, cloud_weight, footprint):
    rows, comp = exchange(radiance, cloud_weight, footprint)
    return tuple(pyramid(rows, comp))


def solution(mesh):
    in_specs = (P(("scene", "tile"), None, None, None), P(("scene", "tile"), None, None), P())
    out_specs = (
        P("tile", None, "scene"),
        P("tile", None, None, None),
        P("tile", None, None, None),
        P("tile", None, None, None),
        P("tile", None, None, None),
        P("tile", None, None, None),
    )
    return jax.shard_map(
        on_device, mesh=mesh, in_specs=in_specs, out_specs=out_specs, check_vma=False
    )
```

```python
import functools

import jax
import jax.numpy as jnp
from jax import lax
from jax.experimental import pallas as pl
from jax.experimental.pallas import tpu as pltpu
from jax.sharding import PartitionSpec as P

MESH = pl.DeviceIdType.MESH
K = 8
BANDS = 10
TILES = 64
PIX = 8192
LANES = 128
HALF = 48
BOX = 64
F32 = jnp.float32
BF16 = jnp.bfloat16


STEPS = (
    (2, 2), (2, 1), (1, 2), (2, 3), (3, 2), (2, 0), (1, 1), (0, 2), (3, 3), (1, 3), (3, 1), (1, 0), (0, 1), (3, 0), (0, 3),
)
STEPS_X = sum(step[0] * 4**n for n, step in enumerate(STEPS))
STEPS_Y = sum(step[1] * 4**n for n, step in enumerate(STEPS))


def each_partner(visit):
    def inner(u, carry):
        n, dx, dy = carry
        visit(4 * n + u, dx, dy, 1 - lax.rem(u, 2), 1 - lax.div(u, 2))
        return carry

    def outer(n, carry):
        in_x, in_y = carry
        lax.fori_loop(0, 4, inner, (n, lax.rem(in_x, 4), lax.rem(in_y, 4)))
        return lax.div(in_x, 4), lax.div(in_y, 4)

    lax.fori_loop(0, 15, outer, (jnp.int32(STEPS_X), jnp.int32(STEPS_Y)))
    lax.fori_loop(0, 3, inner, (jnp.int32(15), jnp.int32(0), jnp.int32(0)))


def position():
    scene = lax.axis_index("scene")
    tile = lax.axis_index("tile")
    z_lo = lax.div(scene, 8)
    x = lax.rem(lax.div(scene, 2), 4)
    core = lax.rem(scene, 2)
    z_hi = lax.div(tile, 4)
    y = lax.rem(tile, 4)
    return z_lo, x, core, z_hi, y


def exchange_kernel(
    rad_ref, weight_ref, foot_ref, rows_ref, comp_ref,
    rad, weight, foot, send, recv, assign, acc, send3, recv3, line,
    ring_sem, in_sem, send_sem, recv_sem, send3_sem, recv3_sem, sg1_sem, rg1_sem, sg2_sem, rg2_sem,
):
    z_lo, x, core, z_hi, y = position()
    tile = z_hi * 4 + y
    xc = x * 2 + core
    pair = lax.div(z_lo, 2)
    odd = lax.rem(z_lo, 2)

    load_foot = pltpu.make_async_copy(foot_ref.at[:, pl.ds(pl.multiple_of(pair * 128, 128), 128)], foot, in_sem.at[2])
    load_weight = pltpu.make_async_copy(weight_ref.at[0], weight, in_sem.at[1])
    load_rad = pltpu.make_async_copy(rad_ref.at[0], rad, in_sem.at[0])
    load_weight.start()
    load_rad.start()
    load_foot.start()

    def box_device(dx, dy, dc, dz):
        x2 = lax.rem(x + dx, 4)
        y2 = lax.rem(y + dy, 4)
        c2 = lax.rem(core + dc, 2)
        o2 = lax.rem(odd + dz, 2)
        block = (2 * y2 + o2) * 8 + x2 * 2 + c2
        return block, ((2 * pair + o2) * 8 + x2 * 2 + c2, z_hi * 4 + y2)

    ring = z_hi * 4 + pair

    def ring_device(step):
        box = lax.rem(ring + step, 8)
        return ((2 * lax.rem(box, 4) + odd) * 8 + xc, lax.div(box, 4) * 4 + y)

    def owner_device(o):
        return ((2 * y + odd) * 8 + xc, o)

    def source_device(s):
        return ((2 * lax.rem(s, 4) + odd) * 8 + xc, lax.div(s, 4) * 4 + pair)

    my_source = z_hi * 4 + pair
    at_home = pair == y

    barrier = pltpu.get_barrier_semaphore()

    def greet(slot, *offset):
        pl.semaphore_signal(barrier, inc=1, device_id=box_device(*offset)[1], device_id_type=MESH)

    each_partner(greet)
    for step in (1, 7):
        pl.semaphore_signal(barrier, inc=1, device_id=ring_device(step), device_id_type=MESH)

    def tell_ring():
        pl.semaphore_signal(ring_sem.at[0], inc=1, device_id=ring_device(1), device_id_type=MESH)
        pl.semaphore_signal(ring_sem.at[1], inc=1, device_id=ring_device(7), device_id_type=MESH)

    def hear_ring():
        pl.semaphore_wait(ring_sem.at[0], 1)
        pl.semaphore_wait(ring_sem.at[1], 1)

    def line_device(i):
        z2 = lax.rem(z_lo + i, 8)
        return z2, (z2 * 8 + xc, tile)

    load_weight.wait()
    load_rad.wait()
    pl.semaphore_wait(barrier, BOX - 1 + 2)
    tell_ring()

    def fill(h, block, out):
        pixels = pl.ds(pl.multiple_of(block * LANES, LANES), LANES)
        w = weight[:, pixels].astype(F32)
        twice = jnp.concatenate([w, w], axis=0).astype(BF16)
        if h == 0:
            first = jnp.concatenate([w, w * rad[0, :, pixels].astype(F32)], axis=0).astype(BF16)
            out[0:16, :] = first
            for j in range(2):
                out[16 * j + 16 : 16 * j + 32, :] = rad[2 * j + 1 : 2 * j + 3, :, pixels].reshape(16, LANES) * twice
        else:
            for j in range(2):
                out[16 * j : 16 * j + 16, :] = rad[2 * j + 5 : 2 * j + 7, :, pixels].reshape(16, LANES) * twice
            last = jnp.concatenate([w * rad[9, :, pixels].astype(F32), jnp.zeros_like(w)], axis=0).astype(BF16)
            out[32:48, :] = last

    def box_copy(h, slot, device):
        return pltpu.make_async_remote_copy(
            src_ref=send.at[h, slot], dst_ref=recv.at[h, slot],
            send_sem=send_sem.at[h, slot], recv_sem=recv_sem.at[h, slot],
            device_id=device, device_id_type=MESH,
        )

    other_core = box_device(0, 0, 1, 0)[1]

    for h in range(2):
        def send_box(slot, *offset, h=h):
            block, device = box_device(*offset)
            fill(h, block, send.at[h, slot])
            box_copy(h, slot, device).start()

        each_partner(send_box)
        fill(h, (2 * y + odd) * 8 + xc, recv.at[h, BOX - 1])
        hear_ring()
        tell_ring()

    load_foot.wait()
    lane = lax.broadcasted_iota(jnp.int32, (1, 16 * BOX), 1)
    slot = lane >> 4
    step = slot >> 2
    dx, dy = jnp.zeros_like(slot), jnp.zeros_like(slot)
    for n, (far_x, far_y) in enumerate(STEPS):
        dx = jnp.where(step == n, far_x, dx)
        dy = jnp.where(step == n, far_y, dy)
    source_row = (
        (((odd + 1 - ((slot >> 1) & 1)) & 1) << 6)
        + (((x - dx) & 3) << 4)
        + (((core + 1 - (slot & 1)) & 1) << 3)
        + ((y - dy) & 3)
        + z_hi * 4
    )
    pick = jnp.where(lax.broadcasted_iota(jnp.int32, (128, 16 * BOX), 0) == source_row, 1.0, 0.0).astype(BF16)
    named = jnp.dot(foot[...].astype(F32).astype(BF16), pick, preferred_element_type=F32)
    own = lax.broadcasted_iota(jnp.int32, (K, 16 * BOX), 0) == (lane & 7)
    target = jnp.sum(jnp.where(own, named, 0.0), axis=0, keepdims=True).astype(jnp.int32) + ((lane & 8) << 3)
    row = lax.broadcasted_iota(jnp.int32, (128, 16 * BOX), 0)
    assign[...] = jnp.where(row == target, 1.0, 0.0).astype(BF16)
    hear_ring()
    tell_ring()

    def stays(o):
        return jnp.logical_and(at_home, o == tile)

    def owner_copy(h, o):
        return pltpu.make_async_remote_copy(
            src_ref=send3.at[h, o], dst_ref=recv3.at[h, my_source],
            send_sem=send3_sem.at[h, o], recv_sem=recv3_sem.at[h, my_source],
            device_id=owner_device(o), device_id_type=MESH,
        )

    def reduce_box(h):
        def wait_box(i, _):
            box_copy(h, i, other_core).wait_recv()
            return 0

        for g in range(4):
            lax.fori_loop(16 * g, min(16 * g + 16, BOX - 1), wait_box, 0)
            left = assign[:, 256 * g : 256 * g + 256]
            right = jnp.concatenate(
                [recv[h, 16 * g : 16 * g + 16, 16 * j : 16 * j + 16, :].reshape(256, LANES) for j in range(3)], axis=1
            )
            part = jnp.dot(left, right, preferred_element_type=F32)
            if g == 0:
                acc[...] = part
            else:
                acc[...] += part

        for o in range(8):
            for j in range(3):
                lanes = slice(LANES * j, LANES * j + LANES)
                both = jnp.concatenate([acc[8 * o : 8 * o + 8, lanes], acc[64 + 8 * o : 72 + 8 * o, lanes]], axis=0)
                send3[h, o, 16 * j : 16 * j + 16, :] = both.astype(BF16)

        if h == 0:
            hear_ring()

        def send_owner(i, _):
            o = lax.rem(tile + i, 8)

            @pl.when(jnp.logical_not(stays(o)))
            def _():
                owner_copy(h, o).start()
            return 0

        lax.fori_loop(0, 8, send_owner, 0)

        @pl.when(at_home)
        def _():
            recv3[h, my_source] = send3[h, tile]

    def line_copy(h, i):
        return pltpu.make_async_remote_copy(
            src_ref=line.at[h, z_lo], dst_ref=line.at[h, z_lo], send_sem=sg1_sem.at[h, i], recv_sem=rg1_sem.at[h, z_lo],
            device_id=line_device(i)[1], device_id_type=MESH,
        )

    def finish_mean(h, scale):
        def wait_source(s, _):
            @pl.when(jnp.logical_not(jnp.logical_and(at_home, s == my_source)))
            def _():
                pltpu.make_async_remote_copy(
                    src_ref=send3.at[h, s], dst_ref=recv3.at[h, s],
                    send_sem=send3_sem.at[h, s], recv_sem=recv3_sem.at[h, s],
                    device_id=source_device(s), device_id_type=MESH,
                ).wait_recv()
            return 0

        lax.fori_loop(0, 8, wait_source, 0)
        total = recv3[h, 0].astype(F32)
        for s in range(1, 8):
            total = total + recv3[h, s].astype(F32)
        if h == 0:
            scale = jnp.maximum(total[0:8, :], 1.0)
            total = total[8:48, :]
        mean = [(total[8 * b : 8 * b + 8, :] / scale).astype(BF16).astype(F32) for b in range(5)]

        blank = jnp.zeros((8, LANES), F32)
        pixel = lax.broadcasted_iota(jnp.int32, (LANES, LANES), 0)
        spot = lax.broadcasted_iota(jnp.int32, (LANES, LANES), 1)
        pooled = None
        for g in range(4):
            left = jnp.concatenate([mean[g], mean[4] if g == 0 else blank], axis=0).astype(BF16)
            mix = jnp.where(spot == 32 * g + ((pixel & 63) >> 1), 0.25, 0.0).astype(BF16)
            part = jnp.dot(left, mix, preferred_element_type=F32)
            pooled = part if pooled is None else pooled + part
        line[h, z_lo] = pooled.astype(BF16)

        def send_line(i, _):
            line_copy(h, i).start()
            return 0

        lax.fori_loop(1, 8, send_line, 0)
        comp_ref[40 * h : 40 * h + 40, :] = jnp.concatenate(mean, axis=0)
        return scale

    def plane_device(i):
        xc2 = lax.rem(xc + i, 8)
        return xc2, (z_lo * 8 + xc2, tile)

    def plane_copy(h, i):
        return pltpu.make_async_remote_copy(
            src_ref=line.at[h], dst_ref=rows_ref.at[h, xc], send_sem=sg2_sem.at[h, i], recv_sem=rg2_sem.at[h, xc],
            device_id=plane_device(i)[1], device_id_type=MESH,
        )

    def spread_line(h):
        def wait_line(i, _):
            z2, device = line_device(i)
            pltpu.make_async_remote_copy(
                src_ref=line.at[h, z2], dst_ref=line.at[h, z2], send_sem=sg1_sem.at[h, i], recv_sem=rg1_sem.at[h, z2],
                device_id=device, device_id_type=MESH,
            ).wait_recv()
            return 0

        lax.fori_loop(1, 8, wait_line, 0)

        def send_plane(i, _):
            plane_copy(h, i).start()
            return 0

        lax.fori_loop(1, 8, send_plane, 0)
        rows_ref[h, xc] = line[h]

    reduce_box(0)
    reduce_box(1)
    scale = finish_mean(0, None)
    finish_mean(1, scale)
    spread_line(0)
    spread_line(1)

    for h in range(2):
        def drain_box(i, _, h=h):
            box_copy(h, i, other_core).wait_send()
            return 0

        lax.fori_loop(0, BOX - 1, drain_box, 0)

        def drain_owner(o, _, h=h):
            @pl.when(jnp.logical_not(stays(o)))
            def _():
                owner_copy(h, o).wait_send()
            return 0

        lax.fori_loop(0, 8, drain_owner, 0)

        def wait_plane(i, _, h=h):
            xc2, device = plane_device(i)
            pltpu.make_async_remote_copy(
                src_ref=line.at[h], dst_ref=rows_ref.at[h, xc2], send_sem=sg2_sem.at[h, i], recv_sem=rg2_sem.at[h, xc2],
                device_id=device, device_id_type=MESH,
            ).wait_recv()
            return 0

        lax.fori_loop(1, 8, wait_plane, 0)

        def drain_rows(i, _, h=h):
            line_copy(h, i).wait_send()
            plane_copy(h, i).wait_send()
            return 0

        lax.fori_loop(1, 8, drain_rows, 0)


def exchange(radiance, cloud_weight, footprint):
    any_space = pl.BlockSpec(memory_space=pl.ANY)
    vmem = pl.BlockSpec(memory_space=pltpu.VMEM)
    dma = pltpu.SemaphoreType.DMA
    return pl.pallas_call(
        exchange_kernel,
        out_shape=(
            jax.ShapeDtypeStruct((2, 8, 8, 16, LANES), BF16),
            jax.ShapeDtypeStruct((80, LANES), F32),
        ),
        in_specs=[any_space] * 3,
        out_specs=(vmem, vmem),
        scratch_shapes=[
            pltpu.VMEM((BANDS, K, PIX), BF16),
            pltpu.VMEM((K, PIX), jnp.int32),
            pltpu.VMEM((K, 128), jnp.int32),
            pltpu.VMEM((2, BOX, HALF, LANES), BF16),
            pltpu.VMEM((2, BOX, HALF, LANES), BF16),
            pltpu.VMEM((128, 16 * BOX), BF16),
            pltpu.VMEM((128, 3 * LANES), F32),
            pltpu.VMEM((2, 8, HALF, LANES), BF16),
            pltpu.VMEM((2, 8, HALF, LANES), BF16),
            pltpu.VMEM((2, 8, 16, LANES), BF16),
            pltpu.SemaphoreType.REGULAR((2,)),
            dma((3,)),
            dma((2, BOX)),
            dma((2, BOX)),
            dma((2, 8)),
            dma((2, 8)),
            dma((2, 8)),
            dma((2, 8)),
            dma((2, 8)),
            dma((2, 8)),
        ],
        compiler_params=pltpu.CompilerParams(
            collective_id=0, has_side_effects=True, vmem_limit_bytes=16 * 1024 * 1024
        ),
        name="exchange",
    )(*(pltpu.with_memory_space_constraint(a, pltpu.HBM) for a in (jnp.transpose(radiance, (0, 2, 1, 3)), cloud_weight, footprint.T)))


def pyramid_kernel(rows_ref, comp_ref, composite, one, two, three, four, five, t1, t2, t3):
    composite[...] = comp_ref[...].reshape(BANDS, 8, LANES).astype(BF16)

    before = lax.broadcasted_iota(jnp.int32, (LANES, LANES), 0)
    after = lax.broadcasted_iota(jnp.int32, (LANES, LANES), 1)
    same = (before >> 5) == (after >> 5)
    mix = jnp.where(
        jnp.logical_and(same, ((before & 31) >> 1) == (after & 31)), 0.25, 0.0
    ).astype(BF16)
    unit = jnp.where(before == after, 1.0, 0.0).astype(BF16)

    def halve(values):
        flat = values.reshape(-1, LANES)
        return jnp.dot(flat, mix, preferred_element_type=F32).reshape(values.shape)

    def keep(scratch, row, h, values):
        for i in range(8):
            at = row(i) * 32 + 16 * h
            scratch[at : at + 16, :] = values[i].astype(F32)

    fourth, fifth = [], []
    for h in range(2):
        level = [rows_ref[h, xc] for xc in range(8)]
        for xc in range(8):
            keep(t1, lambda i, xc=xc: i * 8 + xc, h, level[xc])
        for scratch, m in ((t2, 4), (t3, 2), (None, 1)):
            level = [(halve(level[2 * q]) + halve(level[2 * q + 1])).astype(BF16) for q in range(m)]
            if scratch is not None:
                for q in range(m):
                    keep(scratch, lambda i, q=q, m=m: i * m + q, h, level[q])
        fourth.append(level[0].astype(F32))
        last = halve(level[0]).reshape(4, 2, 16, LANES)
        fifth.append((last[:, 0] + last[:, 1]).astype(BF16).astype(F32))

    for scratch, out, height, width in ((t1, one, 64, 32), (t2, two, 32, 16), (t3, three, 16, 8)):
        for r in range(32):
            h, extra, t = r // 16, r // 8 % 2, r % 8
            lines = scratch[pl.ds(r, height, stride=32), :].astype(BF16)
            turned = lax.dot_general(
                unit[0:32] if extra else unit, lines, (((1,), (1,)), ((), ())), preferred_element_type=F32
            )
            for g in range(1 if extra else 4):
                out[t, 5 * h + 4 * extra + g] = turned[32 * g : 32 * g + width].astype(BF16)

    for values, out, height, width in ((fourth, four, 8, 4), (fifth, five, 4, 2)):
        columns = []
        for c in range(width):
            total = None
            for r in range(4):
                h, extra = r // 2, r % 2
                group = before >> 5
                band = 5 * h + 4 if extra else 5 * h + group
                spread = jnp.where(
                    jnp.logical_and(
                        jnp.logical_and((before & 31) == c, after == band), group == 0 if extra else group < 4
                    ),
                    1.0, 0.0,
                ).astype(BF16)
                left = values[h][:, 8 * extra : 8 * extra + 8, :].reshape(8 * height, LANES).astype(BF16)
                part = jnp.dot(left, spread, preferred_element_type=F32)
                total = part if total is None else total + part
            columns.append(total)
        stacked = jnp.concatenate(columns, axis=0).astype(BF16)
        shape = (64 * height, 8 * height * width)
        to = lax.broadcasted_iota(jnp.int32, shape, 0)
        of = lax.broadcasted_iota(jnp.int32, shape, 1)
        high = {8: 3, 4: 2}[height]
        t, r, c = to >> (3 + high), (to >> 3) & (height - 1), to & 7
        order = jnp.where(of == c * (8 * height) + r * 8 + t, 1.0, 0.0).astype(BF16)
        placed = jnp.dot(order, stacked, preferred_element_type=F32)
        for t in range(8):
            for r in range(height):
                at = 8 * (t * height + r)
                out[t, r] = placed[at : at + width, 0:BANDS].astype(BF16)


def pyramid(rows, comp):
    vmem = pl.BlockSpec(memory_space=pltpu.VMEM)
    shapes = [(BANDS, 8, LANES)] + [(8, BANDS, 32 >> i, 64 >> i) for i in range(3)] + [(8, 8, 4, BANDS), (8, 4, 2, BANDS)]
    outs = pl.pallas_call(
        pyramid_kernel,
        out_shape=[jax.ShapeDtypeStruct(s, BF16) for s in shapes],
        in_specs=[vmem] * 2,
        out_specs=[vmem] * 6,
        scratch_shapes=[pltpu.VMEM((32 * (64 >> i), LANES), F32) for i in range(3)],
        compiler_params=pltpu.CompilerParams(vmem_limit_bytes=16 * 1024 * 1024),
        name="pyramid",
    )(rows, comp)
    orders = [(1, 0, 2)] + [(0, 1, 3, 2)] * 3 + [(0, 3, 1, 2)] * 2
    return tuple(jnp.transpose(out, order) for out, order in zip(outs, orders))


def on_device(radiance, cloud_weight, footprint):
    rows, comp = exchange(radiance, cloud_weight, footprint)
    return pyramid(rows, comp)


def solution(mesh):
    in_specs = (P(("scene", "tile"), None, None, None), P(("scene", "tile"), None, None), P())
    out_specs = (
        P("tile", None, "scene"),
        P("tile", None, None, None),
        P("tile", None, None, None),
        P("tile", None, None, None),
        P("tile", None, None, None),
        P("tile", None, None, None),
    )
    return jax.shard_map(
        on_device, mesh=mesh, in_specs=in_specs, out_specs=out_specs, check_vma=False
    )
```

```python
import functools

import jax
import jax.numpy as jnp
from jax import lax
from jax.experimental import pallas as pl
from jax.experimental.pallas import tpu as pltpu
from jax.sharding import PartitionSpec as P

MESH = pl.DeviceIdType.MESH
K = 8
BANDS = 10
TILES = 64
PIX = 8192
LANES = 128
ROWS = (64, 32)
CHUNK = ((0, 7), (7, 10))
BOX = 64
F32 = jnp.float32
BF16 = jnp.bfloat16


STEPS = (
    (2, 2), (2, 1), (1, 2), (2, 3), (3, 2), (2, 0), (1, 1), (0, 2), (3, 3), (1, 3), (3, 1), (1, 0), (0, 1), (3, 0), (0, 3),
)
STEPS_X = sum(step[0] * 4**n for n, step in enumerate(STEPS))
STEPS_Y = sum(step[1] * 4**n for n, step in enumerate(STEPS))


def each_partner(visit):
    def inner(u, carry):
        n, dx, dy = carry
        visit(4 * n + u, dx, dy, 1 - lax.rem(u, 2), 1 - lax.div(u, 2))
        return carry

    def outer(n, carry):
        in_x, in_y = carry
        lax.fori_loop(0, 4, inner, (n, lax.rem(in_x, 4), lax.rem(in_y, 4)))
        return lax.div(in_x, 4), lax.div(in_y, 4)

    lax.fori_loop(0, 15, outer, (jnp.int32(STEPS_X), jnp.int32(STEPS_Y)))
    lax.fori_loop(0, 3, inner, (jnp.int32(15), jnp.int32(0), jnp.int32(0)))


def position():
    scene = lax.axis_index("scene")
    tile = lax.axis_index("tile")
    z_lo = lax.div(scene, 8)
    x = lax.rem(lax.div(scene, 2), 4)
    core = lax.rem(scene, 2)
    z_hi = lax.div(tile, 4)
    y = lax.rem(tile, 4)
    return z_lo, x, core, z_hi, y


def exchange_kernel(
    rad_ref, weight_ref, foot_ref, rows_ref, comp_a, comp_b,
    rad, weight, foot, send_a, send_b, recv_a, recv_b, assign, acc, send3_a, send3_b, recv3_a, recv3_b, mean_a, mean_b, pool, line,
    ring_sem, in_sem, send_sem, recv_sem, send3_sem, recv3_sem, sg1_sem, rg1_sem, sg2_sem, rg2_sem, sc_sem, rc_sem,
):
    send, recv, send3, recv3 = (send_a, send_b), (recv_a, recv_b), (send3_a, send3_b), (recv3_a, recv3_b)
    z_lo, x, core, z_hi, y = position()
    tile = z_hi * 4 + y
    xc = x * 2 + core
    pair = lax.div(z_lo, 2)
    odd = lax.rem(z_lo, 2)

    load_foot = pltpu.make_async_copy(foot_ref.at[:, pl.ds(pl.multiple_of(pair * 128, 128), 128)], foot, in_sem.at[2])
    load_weight = pltpu.make_async_copy(weight_ref.at[0], weight, in_sem.at[1])
    load_rad = pltpu.make_async_copy(rad_ref.at[0], rad, in_sem.at[0])
    load_weight.start()
    load_rad.start()
    load_foot.start()

    def box_device(dx, dy, dc, dz):
        x2 = lax.rem(x + dx, 4)
        y2 = lax.rem(y + dy, 4)
        c2 = lax.rem(core + dc, 2)
        o2 = lax.rem(odd + dz, 2)
        block = (2 * y2 + o2) * 8 + x2 * 2 + c2
        return block, ((2 * pair + o2) * 8 + x2 * 2 + c2, z_hi * 4 + y2)

    ring = z_hi * 4 + pair

    def ring_device(step):
        box = lax.rem(ring + step, 8)
        return ((2 * lax.rem(box, 4) + odd) * 8 + xc, lax.div(box, 4) * 4 + y)

    group = lax.rem(ring + 2, 8)
    home = lax.rem(tile + 6, 8)
    comp, means = (comp_a, comp_b), (mean_a, mean_b)

    def maker_device(j):
        return ((2 * lax.rem(home, 4) + lax.rem(j, 2)) * 8 + xc, lax.div(home, 4) * 4 + lax.div(j, 2))

    my_row = 2 * y + odd
    at_home = group == tile

    barrier = pltpu.get_barrier_semaphore()

    def greet(slot, *offset):
        pl.semaphore_signal(barrier, inc=1, device_id=box_device(*offset)[1], device_id_type=MESH)

    each_partner(greet)
    for step in (1, 7):
        pl.semaphore_signal(barrier, inc=1, device_id=ring_device(step), device_id_type=MESH)

    def tell_ring():
        pl.semaphore_signal(ring_sem.at[0], inc=1, device_id=ring_device(1), device_id_type=MESH)
        pl.semaphore_signal(ring_sem.at[1], inc=1, device_id=ring_device(7), device_id_type=MESH)

    def hear_ring():
        pl.semaphore_wait(ring_sem.at[0], 1)
        pl.semaphore_wait(ring_sem.at[1], 1)

    load_weight.wait()
    load_rad.wait()
    pl.semaphore_wait(barrier, BOX - 1 + 2)
    tell_ring()

    def fill(h, block, out):
        pixels = pl.ds(pl.multiple_of(block * LANES, LANES), LANES)
        w = weight[:, pixels].astype(F32)
        twice = jnp.concatenate([w, w], axis=0).astype(BF16)
        if h == 0:
            first = jnp.concatenate([w, w * rad[0, :, pixels].astype(F32)], axis=0).astype(BF16)
            out[0:16, :] = first
            for j in range(3):
                out[16 * j + 16 : 16 * j + 32, :] = rad[2 * j + 1 : 2 * j + 3, :, pixels].reshape(16, LANES) * twice
        else:
            out[0:16, :] = rad[7:9, :, pixels].reshape(16, LANES) * twice
            last = jnp.concatenate([w * rad[9, :, pixels].astype(F32), jnp.zeros_like(w)], axis=0).astype(BF16)
            out[16:32, :] = last

    def box_copy(h, slot, device):
        return pltpu.make_async_remote_copy(
            src_ref=send[h].at[slot], dst_ref=recv[h].at[slot],
            send_sem=send_sem.at[h, slot], recv_sem=recv_sem.at[h, slot],
            device_id=device, device_id_type=MESH,
        )

    other_core = box_device(0, 0, 1, 0)[1]

    for h in range(2):
        def send_box(slot, *offset, h=h):
            block, device = box_device(*offset)
            fill(h, block, send[h].at[slot])
            box_copy(h, slot, device).start()

        each_partner(send_box)
        fill(h, my_row * 8 + xc, recv[h].at[BOX - 1])
        hear_ring()
        tell_ring()

    load_foot.wait()
    lane = lax.broadcasted_iota(jnp.int32, (1, 16 * BOX), 1)
    slot = lane >> 4
    step = slot >> 2
    dx, dy = jnp.zeros_like(slot), jnp.zeros_like(slot)
    for n, (far_x, far_y) in enumerate(STEPS):
        dx = jnp.where(step == n, far_x, dx)
        dy = jnp.where(step == n, far_y, dy)
    source_row = (
        (((odd + 1 - ((slot >> 1) & 1)) & 1) << 6)
        + (((x - dx) & 3) << 4)
        + (((core + 1 - (slot & 1)) & 1) << 3)
        + ((y - dy) & 3)
        + z_hi * 4
    )
    pick = jnp.where(lax.broadcasted_iota(jnp.int32, (128, 16 * BOX), 0) == source_row, 1.0, 0.0).astype(BF16)
    named = jnp.dot(foot[...].astype(F32).astype(BF16), pick, preferred_element_type=F32)
    own = lax.broadcasted_iota(jnp.int32, (K, 16 * BOX), 0) == (lane & 7)
    target = jnp.sum(jnp.where(own, named, 0.0), axis=0, keepdims=True).astype(jnp.int32) + ((lane & 8) << 3)
    row = lax.broadcasted_iota(jnp.int32, (128, 16 * BOX), 0)
    assign[...] = jnp.where(row == target, 1.0, 0.0).astype(BF16)
    hear_ring()
    tell_ring()

    def ring_copy(h, i):
        return pltpu.make_async_remote_copy(
            src_ref=send3[h].at[lax.rem(group + i, 8)], dst_ref=recv3[h].at[ring],
            send_sem=send3_sem.at[h, i], recv_sem=recv3_sem.at[h, ring],
            device_id=ring_device(i), device_id_type=MESH,
        )

    def reduce_box(h):
        def wait_box(i, _):
            box_copy(h, i, other_core).wait_recv()
            return 0

        for g in range(4):
            lax.fori_loop(16 * g, min(16 * g + 16, BOX - 1), wait_box, 0)
            left = assign[:, 256 * g : 256 * g + 256]
            right = jnp.concatenate(
                [recv[h][16 * g : 16 * g + 16, 16 * j : 16 * j + 16, :].reshape(256, LANES) for j in range(ROWS[h] // 16)],
                axis=1,
            )
            part = jnp.dot(left, right, preferred_element_type=F32)
            if g == 0:
                acc[:, 0 : 8 * ROWS[h]] = part
            else:
                acc[:, 0 : 8 * ROWS[h]] += part

        for o in range(8):
            for j in range(ROWS[h] // 16):
                lanes = slice(LANES * j, LANES * j + LANES)
                both = jnp.concatenate([acc[8 * o : 8 * o + 8, lanes], acc[64 + 8 * o : 72 + 8 * o, lanes]], axis=0)
                send3[h][o, 16 * j : 16 * j + 16, :] = both.astype(BF16)

        if h == 0:
            hear_ring()

        def send_ring(i, _):
            ring_copy(h, i).start()
            return 0

        lax.fori_loop(1, 8, send_ring, 0)
        recv3[h][ring] = send3[h][group]

    def line_copy(h, z2):
        return pltpu.make_async_remote_copy(
            src_ref=pool.at[h], dst_ref=line.at[h, my_row], send_sem=sg1_sem.at[h, z2], recv_sem=rg1_sem.at[h, my_row],
            device_id=(z2 * 8 + xc, group), device_id_type=MESH,
        )

    def comp_copy(h):
        return pltpu.make_async_remote_copy(
            src_ref=means[h], dst_ref=comp[h], send_sem=sc_sem.at[h], recv_sem=rc_sem.at[h],
            device_id=(my_row * 8 + xc, group), device_id_type=MESH,
        )

    def stays(z2):
        return jnp.logical_and(at_home, z2 == z_lo)

    def finish_mean(h, scale):
        def wait_ring(i, _):
            s = lax.rem(ring + i, 8)
            pltpu.make_async_remote_copy(
                src_ref=send3[h].at[s], dst_ref=recv3[h].at[s],
                send_sem=send3_sem.at[h, i], recv_sem=recv3_sem.at[h, s],
                device_id=ring_device(i), device_id_type=MESH,
            ).wait_recv()
            return 0

        lax.fori_loop(1, 8, wait_ring, 0)
        total = recv3[h][0].astype(F32)
        for s in range(1, 8):
            total = total + recv3[h][s].astype(F32)
        if h == 0:
            scale = jnp.maximum(total[0:8, :], 1.0)
            total = total[8:64, :]
        first, end = CHUNK[h]
        bands = end - first
        mean = [(total[8 * b : 8 * b + 8, :] / scale).astype(BF16).astype(F32) for b in range(bands)]

        blank = jnp.zeros((8, LANES), F32)
        pixel = lax.broadcasted_iota(jnp.int32, (LANES, LANES), 0)
        spot = lax.broadcasted_iota(jnp.int32, (LANES, LANES), 1)
        pooled = None
        for g in range(min(4, bands)):
            left = jnp.concatenate([mean[g], mean[4 + g] if 4 + g < bands else blank], axis=0).astype(BF16)
            mix = jnp.where(spot == 32 * g + ((pixel & 63) >> 1), 0.25, 0.0).astype(BF16)
            part = jnp.dot(left, mix, preferred_element_type=F32)
            pooled = part if pooled is None else pooled + part
        pool[h] = pooled.astype(BF16)

        def send_line(z2, _):
            @pl.when(jnp.logical_not(stays(z2)))
            def _():
                line_copy(h, z2).start()
            return 0

        lax.fori_loop(0, 8, send_line, 0)
        means[h][...] = jnp.concatenate(mean[0:bands] + [blank], axis=0).astype(BF16)

        @pl.when(jnp.logical_not(stays(my_row)))
        def _():
            comp_copy(h).start()

        @pl.when(stays(my_row))
        def _():
            comp[h][...] = means[h][...]

        @pl.when(at_home)
        def _():
            line[h, my_row] = pool[h]
        return scale

    def plane_device(i):
        xc2 = lax.rem(xc + i, 8)
        return xc2, (z_lo * 8 + xc2, tile)

    def plane_copy(h, i):
        return pltpu.make_async_remote_copy(
            src_ref=line.at[h], dst_ref=rows_ref.at[h, xc], send_sem=sg2_sem.at[h, i], recv_sem=rg2_sem.at[h, xc],
            device_id=plane_device(i)[1], device_id_type=MESH,
        )

    def spread_line(h):
        def wait_line(j, _):
            @pl.when(jnp.logical_not(jnp.logical_and(at_home, j == my_row)))
            def _():
                pltpu.make_async_remote_copy(
                    src_ref=pool.at[h], dst_ref=line.at[h, j], send_sem=sg1_sem.at[h, j], recv_sem=rg1_sem.at[h, j],
                    device_id=maker_device(j), device_id_type=MESH,
                ).wait_recv()
            return 0

        lax.fori_loop(0, 8, wait_line, 0)

        def send_plane(i, _):
            plane_copy(h, i).start()
            return 0

        lax.fori_loop(1, 8, send_plane, 0)
        rows_ref[h, xc] = line[h]

    reduce_box(0)
    reduce_box(1)
    scale = finish_mean(0, None)
    finish_mean(1, scale)
    spread_line(0)
    spread_line(1)

    for h in range(2):
        def drain_box(i, _, h=h):
            box_copy(h, i, other_core).wait_send()
            return 0

        lax.fori_loop(0, BOX - 1, drain_box, 0)

        def drain_ring(i, _, h=h):
            ring_copy(h, i).wait_send()
            return 0

        lax.fori_loop(1, 8, drain_ring, 0)

        @pl.when(jnp.logical_not(stays(my_row)))
        def _(h=h):
            comp_copy(h).wait_send()

        @pl.when(jnp.logical_not(jnp.logical_and(at_home, my_row == z_lo)))
        def _(h=h):
            pltpu.make_async_remote_copy(
                src_ref=means[h], dst_ref=comp[h], send_sem=sc_sem.at[h], recv_sem=rc_sem.at[h],
                device_id=maker_device(z_lo), device_id_type=MESH,
            ).wait_recv()

        def drain_line(z2, _, h=h):
            @pl.when(jnp.logical_not(stays(z2)))
            def _():
                line_copy(h, z2).wait_send()
            return 0

        lax.fori_loop(0, 8, drain_line, 0)

        def wait_plane(i, _, h=h):
            xc2, device = plane_device(i)
            pltpu.make_async_remote_copy(
                src_ref=line.at[h], dst_ref=rows_ref.at[h, xc2], send_sem=sg2_sem.at[h, i], recv_sem=rg2_sem.at[h, xc2],
                device_id=device, device_id_type=MESH,
            ).wait_recv()
            return 0

        lax.fori_loop(1, 8, wait_plane, 0)

        def drain_rows(i, _, h=h):
            plane_copy(h, i).wait_send()
            return 0

        lax.fori_loop(1, 8, drain_rows, 0)


def exchange(radiance, cloud_weight, footprint):
    any_space = pl.BlockSpec(memory_space=pl.ANY)
    vmem = pl.BlockSpec(memory_space=pltpu.VMEM)
    dma = pltpu.SemaphoreType.DMA
    return pl.pallas_call(
        exchange_kernel,
        out_shape=(
            jax.ShapeDtypeStruct((2, 8, 8, 16, LANES), BF16),
            *(jax.ShapeDtypeStruct((rows, LANES), BF16) for rows in ROWS),
        ),
        in_specs=[any_space] * 3,
        out_specs=(vmem, vmem, vmem),
        scratch_shapes=[
            pltpu.VMEM((BANDS, K, PIX), BF16),
            pltpu.VMEM((K, PIX), jnp.int32),
            pltpu.VMEM((K, 128), jnp.int32),
            *(pltpu.VMEM((BOX, rows, LANES), BF16) for rows in ROWS * 2),
            pltpu.VMEM((128, 16 * BOX), BF16),
            pltpu.VMEM((128, 4 * LANES), F32),
            *(pltpu.VMEM((8, rows, LANES), BF16) for rows in ROWS * 2),
            *(pltpu.VMEM((rows, LANES), BF16) for rows in ROWS),
            pltpu.VMEM((2, 16, LANES), BF16),
            pltpu.VMEM((2, 8, 16, LANES), BF16),
            pltpu.SemaphoreType.REGULAR((2,)),
            dma((3,)),
            dma((2, BOX)),
            dma((2, BOX)),
            dma((2, 8)),
            dma((2, 8)),
            dma((2, 8)),
            dma((2, 8)),
            dma((2, 8)),
            dma((2, 8)),
            dma((2,)),
            dma((2,)),
        ],
        compiler_params=pltpu.CompilerParams(
            collective_id=0, has_side_effects=True, vmem_limit_bytes=16 * 1024 * 1024
        ),
        name="exchange",
    )(*(pltpu.with_memory_space_constraint(a, pltpu.HBM) for a in (jnp.transpose(radiance, (0, 2, 1, 3)), cloud_weight, footprint.T)))


GROUPS = ((0, 0, 0, 4), (0, 8, 4, 3), (1, 0, 7, 3))


def pyramid_kernel(rows_ref, comp_a, comp_b, *refs):
    outs, (composite, one, two, three, four, five), (t1, t2, t3), sems = refs[:6], refs[6:12], refs[12:15], refs[15]

    def put(i):
        return pltpu.make_async_copy(refs[6 + i], outs[i], sems.at[i])

    before = lax.broadcasted_iota(jnp.int32, (LANES, LANES), 0)
    after = lax.broadcasted_iota(jnp.int32, (LANES, LANES), 1)
    same = (before >> 5) == (after >> 5)
    mix = jnp.where(
        jnp.logical_and(same, ((before & 31) >> 1) == (after & 31)), 0.25, 0.0
    ).astype(BF16)
    unit = jnp.where(before == after, 1.0, 0.0).astype(BF16)

    def halve(values):
        flat = values.reshape(-1, LANES)
        return jnp.dot(flat, mix, preferred_element_type=F32).reshape(values.shape)

    def keep(scratch, row, h, values):
        for i in range(8):
            at = row(i) * 24 + 16 * h
            lines = 8 if h else 16
            scratch[at : at + lines, :] = values[i].astype(F32)[0:lines]

    def turn(scratch, out, height, width):
        for r in range(24):
            _, _, first, bands = GROUPS[r // 8]
            lines = scratch[pl.ds(r, height, stride=24), :].astype(BF16)
            turned = lax.dot_general(
                unit[0 : 32 * bands], lines, (((1,), (1,)), ((), ())), preferred_element_type=F32
            )
            for g in range(bands):
                out[r % 8, first + g] = turned[32 * g : 32 * g + width].astype(BF16)

    level = [[rows_ref[h, xc] for xc in range(8)] for h in range(2)]
    for h in range(2):
        for xc in range(8):
            keep(t1, lambda i, xc=xc: i * 8 + xc, h, level[h][xc])
    turn(t1, one, 64, 32)
    put(1).start()
    for comp, (first, end) in zip((comp_a, comp_b), CHUNK):
        lines = comp[...].astype(F32)[0 : 8 * (end - first)]
        composite[first:end] = lines.reshape(end - first, 8, LANES).astype(BF16)
    put(0).start()
    for scratch, out, m in ((t2, two, 4), (t3, three, 2), (None, None, 1)):
        for h in range(2):
            level[h] = [(halve(level[h][2 * q]) + halve(level[h][2 * q + 1])).astype(BF16) for q in range(m)]
            if scratch is not None:
                for q in range(m):
                    keep(scratch, lambda i, q=q, m=m: i * m + q, h, level[h][q])
        if scratch is not None:
            turn(scratch, out, 8 * m, 4 * m)
            put(2 if m == 4 else 3).start()
    fourth, fifth = [], []
    for h in range(2):
        fourth.append(level[h][0].astype(F32))
        last = halve(level[h][0]).reshape(4, 2, 16, LANES)
        fifth.append((last[:, 0] + last[:, 1]).astype(BF16).astype(F32))

    for values, out, height, width in ((fourth, four, 8, 4), (fifth, five, 4, 2)):
        columns = []
        for c in range(width):
            total = None
            for h, line, first, bands in GROUPS:
                group = before >> 5
                spread = jnp.where(
                    jnp.logical_and(
                        jnp.logical_and((before & 31) == c, after == first + group), group < bands
                    ),
                    1.0, 0.0,
                ).astype(BF16)
                left = values[h][:, line : line + 8, :].reshape(8 * height, LANES).astype(BF16)
                part = jnp.dot(left, spread, preferred_element_type=F32)
                total = part if total is None else total + part
            columns.append(total)
        stacked = jnp.concatenate(columns, axis=0).astype(BF16)
        shape = (64 * height, 8 * height * width)
        to = lax.broadcasted_iota(jnp.int32, shape, 0)
        of = lax.broadcasted_iota(jnp.int32, shape, 1)
        high = {8: 3, 4: 2}[height]
        t, r, c = to >> (3 + high), (to >> 3) & (height - 1), to & 7
        order = jnp.where(of == c * (8 * height) + r * 8 + t, 1.0, 0.0).astype(BF16)
        placed = jnp.dot(order, stacked, preferred_element_type=F32)
        for t in range(8):
            for r in range(height):
                at = 8 * (t * height + r)
                out[t, r] = placed[at : at + width, 0:BANDS].astype(BF16)
        put(4 if height == 8 else 5).start()
    for i in range(6):
        put(i).wait()


def pyramid(rows, comp_a, comp_b):
    vmem = pl.BlockSpec(memory_space=pltpu.VMEM)
    shapes = [(BANDS, 8, LANES)] + [(8, BANDS, 32 >> i, 64 >> i) for i in range(3)] + [(8, 8, 4, BANDS), (8, 4, 2, BANDS)]
    outs = pl.pallas_call(
        pyramid_kernel,
        out_shape=[jax.ShapeDtypeStruct(s, BF16) for s in shapes],
        in_specs=[vmem] * 3,
        out_specs=[pl.BlockSpec(memory_space=pl.ANY)] * 6,
        scratch_shapes=[pltpu.VMEM(s, BF16) for s in shapes]
        + [pltpu.VMEM((24 * (64 >> i), LANES), F32) for i in range(3)]
        + [pltpu.SemaphoreType.DMA((6,))],
        compiler_params=pltpu.CompilerParams(vmem_limit_bytes=16 * 1024 * 1024),
        name="pyramid",
    )(rows, comp_a, comp_b)
    orders = [(1, 0, 2)] + [(0, 1, 3, 2)] * 3 + [(0, 3, 1, 2)] * 2
    return tuple(jnp.transpose(out, order) for out, order in zip(outs, orders))


def on_device(radiance, cloud_weight, footprint):
    return pyramid(*exchange(radiance, cloud_weight, footprint))


def solution(mesh):
    in_specs = (P(("scene", "tile"), None, None, None), P(("scene", "tile"), None, None), P())
    out_specs = (
        P("tile", None, "scene"),
        P("tile", None, None, None),
        P("tile", None, None, None),
        P("tile", None, None, None),
        P("tile", None, None, None),
        P("tile", None, None, None),
    )
    return jax.shard_map(
        on_device, mesh=mesh, in_specs=in_specs, out_specs=out_specs, check_vma=False
    )
```

```python
import functools

import jax
import jax.numpy as jnp
from jax import lax
from jax.experimental import pallas as pl
from jax.experimental.pallas import tpu as pltpu
from jax.sharding import PartitionSpec as P

MESH = pl.DeviceIdType.MESH
K = 8
BANDS = 10
TILES = 64
PIX = 8192
LANES = 128
ROWS = (64, 32)
SHORT = 48
CHUNK = ((0, 6), (6, 10))
BOX = 64
F32 = jnp.float32
BF16 = jnp.bfloat16


STEPS = (
    (2, 2), (2, 1), (1, 2), (2, 3), (3, 2), (2, 0), (1, 1), (0, 2), (3, 3), (1, 3), (3, 1), (1, 0), (0, 1), (3, 0), (0, 3),
)
STEPS_X = sum(step[0] * 4**n for n, step in enumerate(STEPS))
STEPS_Y = sum(step[1] * 4**n for n, step in enumerate(STEPS))


GROUPS = (((0, 4), (4, 2)), ((6, 4),))


def matrices():
    before = lax.broadcasted_iota(jnp.int32, (LANES, LANES), 0)
    after = lax.broadcasted_iota(jnp.int32, (LANES, LANES), 1)
    same = (before >> 5) == (after >> 5)
    mix = jnp.where(jnp.logical_and(same, ((before & 31) >> 1) == (after & 31)), 0.25, 0.0).astype(BF16)
    unit = jnp.where(before == after, 1.0, 0.0).astype(BF16)
    return before, after, mix, unit


def halve(values, mix):
    flat = values.reshape(-1, LANES).astype(BF16)
    return jnp.dot(flat, mix, preferred_element_type=F32).reshape(values.shape)


def overviews(h, level, mix, unit, scratches, outs, done):
    lines = 8 * len(GROUPS[h])
    base = CHUNK[h][0]
    for depth in range(4):
        m = 8 >> depth
        if depth:
            level = [(halve(level[2 * q], mix) + halve(level[2 * q + 1], mix)).astype(BF16).astype(F32) for q in range(m)]
        if depth == 3:
            return level[0]
        scratch, out = scratches[depth], outs[depth]
        for q in range(m):
            for i in range(8):
                at = (i * m + q) * lines
                scratch[at : at + lines, :] = level[q][i]
        for r in range(lines):
            first, bands = GROUPS[h][r // 8]
            picked = scratch[pl.ds(r, 8 * m, stride=lines), :].astype(BF16)
            turned = lax.dot_general(
                unit[0 : 32 * bands], picked, (((1,), (1,)), ((), ())), preferred_element_type=F32
            )
            for g in range(bands):
                out[r % 8, first - base + g] = turned[32 * g : 32 * g + 4 * m].astype(BF16)
        done(depth)


def position():
    scene = lax.axis_index("scene")
    tile = lax.axis_index("tile")
    z_lo = lax.div(scene, 8)
    x = lax.rem(lax.div(scene, 2), 4)
    core = lax.rem(scene, 2)
    z_hi = lax.div(tile, 4)
    y = lax.rem(tile, 4)
    return z_lo, x, core, z_hi, y


def exchange_kernel(
    rad_ref, weight_ref, foot_ref, rows_b, one, two, three, fourth, comp_a, comp_b,
    rad, weight, foot, send_a, send_b, recv_a, recv_b, assign, acc, send3_a, send3_b, recv3_a, recv3_b, mean_a, mean_b, pool, swap_out, swap_in, line, packed, rows_a, t1, t2, t3,
    ring_sem, in_sem, send_sem, recv_sem, send3_sem, recv3_sem, sg1_sem, rg1_sem, sg2_sem, rg2_sem, sc_sem, rc_sem, swap_sem,
):
    send, recv, send3, recv3 = (send_a, send_b), (recv_a, recv_b), (send3_a, send3_b), (recv3_a, recv3_b)
    z_lo, x, core, z_hi, y = position()
    tile = z_hi * 4 + y
    xc = x * 2 + core
    pair = lax.div(z_lo, 2)
    odd = lax.rem(z_lo, 2)

    load_foot = pltpu.make_async_copy(foot_ref.at[:, pl.ds(pl.multiple_of(pair * 128, 128), 128)], foot, in_sem.at[2])
    load_weight = pltpu.make_async_copy(weight_ref.at[0], weight, in_sem.at[1])
    load_rad = pltpu.make_async_copy(rad_ref.at[0], rad, in_sem.at[0])
    load_weight.start()
    load_rad.start()
    load_foot.start()

    def box_device(x2, y2, c2, o2):
        block = (2 * y2 + o2) * 8 + x2 * 2 + c2
        return block, ((2 * pair + o2) * 8 + x2 * 2 + c2, z_hi * 4 + y2)

    def each_partner(visit):
        def four(n, x2, y2, count):
            for u in range(count):
                visit(4 * n + u, u % 2, x2, y2, core if u % 2 else 1 - core, odd if u // 2 else 1 - odd)

        def outer(n, carry):
            in_x, in_y = carry
            four(n, lax.rem(x + lax.rem(in_x, 4), 4), lax.rem(y + lax.rem(in_y, 4), 4), 4)
            return lax.div(in_x, 4), lax.div(in_y, 4)

        lax.fori_loop(0, 15, outer, (jnp.int32(STEPS_X), jnp.int32(STEPS_Y)))
        four(15, x, y, 3)

    ring = z_hi * 4 + pair

    def ring_device(step):
        box = lax.rem(ring + step, 8)
        return ((2 * lax.rem(box, 4) + odd) * 8 + xc, lax.div(box, 4) * 4 + y)

    group = lax.rem(ring + 2, 8)
    home = lax.rem(tile + 6, 8)
    comp, means = (comp_a, comp_b), (mean_a, mean_b)
    whole_line, rows = (line.at[0], packed), (rows_a, rows_b)

    def maker_device(j):
        return ((2 * lax.rem(home, 4) + lax.rem(j, 2)) * 8 + xc, lax.div(home, 4) * 4 + lax.div(j, 2))

    my_row = 2 * y + odd
    at_home = group == tile

    barrier = pltpu.get_barrier_semaphore()

    def greet(slot, same, *offset):
        pl.semaphore_signal(barrier, inc=1, device_id=box_device(*offset)[1], device_id_type=MESH)

    each_partner(greet)

    def clear(n, _):
        recv_a[2 * n, SHORT:64] = jnp.zeros((16, LANES), BF16)
        return 0

    lax.fori_loop(0, BOX // 2, clear, 0)
    for step in (1, 7):
        pl.semaphore_signal(barrier, inc=1, device_id=ring_device(step), device_id_type=MESH)

    def tell_ring():
        pl.semaphore_signal(ring_sem.at[0], inc=1, device_id=ring_device(1), device_id_type=MESH)
        pl.semaphore_signal(ring_sem.at[1], inc=1, device_id=ring_device(7), device_id_type=MESH)

    def hear_ring():
        pl.semaphore_wait(ring_sem.at[0], 1)
        pl.semaphore_wait(ring_sem.at[1], 1)

    load_weight.wait()
    load_rad.wait()
    pl.semaphore_wait(barrier, BOX - 1 + 2)
    tell_ring()

    def fill(h, same, block, out):
        pixels = pl.ds(pl.multiple_of(block * LANES, LANES), LANES)
        w = weight[:, pixels].astype(F32)
        twice = jnp.concatenate([w, w], axis=0).astype(BF16)
        if h == 1:
            for j in range(2):
                out[16 * j : 16 * j + 16, :] = rad[2 * j + 6 : 2 * j + 8, :, pixels].reshape(16, LANES) * twice
            return
        first = jnp.concatenate([w, w * rad[0, :, pixels].astype(F32)], axis=0).astype(BF16)
        out[0:16, :] = first
        for j in range(2):
            out[16 * j + 16 : 16 * j + 32, :] = rad[2 * j + 1 : 2 * j + 3, :, pixels].reshape(16, LANES) * twice
        if same:
            beside = pl.ds(pl.multiple_of((block + 1 - 2 * core) * LANES, LANES), LANES)
            mine = w * rad[5, :, pixels].astype(F32)
            theirs = weight[:, beside].astype(F32) * rad[5, :, beside].astype(F32)
            out[48:64, :] = jnp.concatenate([mine, theirs], axis=0).astype(BF16)

    def box_copy(h, same, slot, device):
        source, target = send[h].at[slot], recv[h].at[slot]
        if h == 0 and not same:
            source, target = send[h].at[slot, 0:SHORT], recv[h].at[slot, 0:SHORT]
        return pltpu.make_async_remote_copy(
            src_ref=source, dst_ref=target,
            send_sem=send_sem.at[h, slot], recv_sem=recv_sem.at[h, slot],
            device_id=device, device_id_type=MESH,
        )

    def each_pair(first, end, visit):
        def pair_of(n, _):
            visit(2 * n, 0)
            visit(2 * n + 1, 1)
            return 0

        lax.fori_loop(first // 2, end // 2, pair_of, 0)
        if end % 2:
            visit(end - 1, 0)

    other_core = box_device(x, y, 1 - core, odd)[1]

    for h in range(2):
        def send_box(slot, same, *offset, h=h):
            block, device = box_device(*offset)
            fill(h, same, block, send[h].at[slot])
            box_copy(h, same, slot, device).start()

        each_partner(send_box)
        fill(h, 1, my_row * 8 + xc, recv[h].at[BOX - 1])
        hear_ring()
        tell_ring()

    load_foot.wait()
    lane = lax.broadcasted_iota(jnp.int32, (1, 16 * BOX), 1)
    slot = lane >> 4
    step = slot >> 2
    dx, dy = jnp.zeros_like(slot), jnp.zeros_like(slot)
    for n, (far_x, far_y) in enumerate(STEPS):
        dx = jnp.where(step == n, far_x, dx)
        dy = jnp.where(step == n, far_y, dy)
    source_row = (
        (((odd + 1 - ((slot >> 1) & 1)) & 1) << 6)
        + (((x - dx) & 3) << 4)
        + (((core + 1 - (slot & 1)) & 1) << 3)
        + ((y - dy) & 3)
        + z_hi * 4
    )
    pick = jnp.where(lax.broadcasted_iota(jnp.int32, (128, 16 * BOX), 0) == source_row, 1.0, 0.0).astype(BF16)
    named = jnp.dot(foot[...].astype(F32).astype(BF16), pick, preferred_element_type=F32)
    own = lax.broadcasted_iota(jnp.int32, (K, 16 * BOX), 0) == (lane & 7)
    target = jnp.sum(jnp.where(own, named, 0.0), axis=0, keepdims=True).astype(jnp.int32) + ((lane & 8) << 3)
    row = lax.broadcasted_iota(jnp.int32, (128, 16 * BOX), 0)
    assign[...] = jnp.where(row == target, 1.0, 0.0).astype(BF16)
    hear_ring()
    tell_ring()

    def ring_copy(h, i):
        return pltpu.make_async_remote_copy(
            src_ref=send3[h].at[lax.rem(group + i, 8)], dst_ref=recv3[h].at[ring],
            send_sem=send3_sem.at[h, i], recv_sem=recv3_sem.at[h, ring],
            device_id=ring_device(i), device_id_type=MESH,
        )

    def reduce_box(h):
        def wait_box(slot, same):
            box_copy(h, same, slot, other_core).wait_recv()

        for g in range(4):
            each_pair(16 * g, min(16 * g + 16, BOX - 1), wait_box)
            left = assign[:, 256 * g : 256 * g + 256]
            right = jnp.concatenate(
                [recv[h][16 * g : 16 * g + 16, 16 * j : 16 * j + 16, :].reshape(256, LANES) for j in range(ROWS[h] // 16)],
                axis=1,
            )
            part = jnp.dot(left, right, preferred_element_type=F32)
            if g == 0:
                acc[:, 0 : 8 * ROWS[h]] = part
            else:
                acc[:, 0 : 8 * ROWS[h]] += part

        for o in range(8):
            for j in range(ROWS[h] // 16):
                lanes = slice(LANES * j, LANES * j + LANES)
                both = jnp.concatenate([acc[8 * o : 8 * o + 8, lanes], acc[64 + 8 * o : 72 + 8 * o, lanes]], axis=0)
                send3[h][o, 16 * j : 16 * j + 16, :] = both.astype(BF16)

        if h == 0:
            hear_ring()

        def send_ring(i, _):
            ring_copy(h, i).start()
            return 0

        lax.fori_loop(1, 8, send_ring, 0)
        recv3[h][ring] = send3[h][group]

    def line_copy(h, z2):
        return pltpu.make_async_remote_copy(
            src_ref=pool.at[h], dst_ref=line.at[h, my_row], send_sem=sg1_sem.at[h, z2], recv_sem=rg1_sem.at[h, my_row],
            device_id=(z2 * 8 + xc, group), device_id_type=MESH,
        )

    def comp_copy(h):
        return pltpu.make_async_remote_copy(
            src_ref=means[h], dst_ref=comp[h], send_sem=sc_sem.at[h], recv_sem=rc_sem.at[h],
            device_id=(my_row * 8 + xc, group), device_id_type=MESH,
        )

    def swap_copy():
        return pltpu.make_async_remote_copy(
            src_ref=swap_out, dst_ref=swap_in, send_sem=swap_sem.at[0], recv_sem=swap_sem.at[1],
            device_id=other_core, device_id_type=MESH,
        )

    def stays(z2):
        return jnp.logical_and(at_home, z2 == z_lo)

    def finish_mean(h, scale):
        def wait_ring(i, _):
            s = lax.rem(ring + i, 8)
            pltpu.make_async_remote_copy(
                src_ref=send3[h].at[s], dst_ref=recv3[h].at[s],
                send_sem=send3_sem.at[h, i], recv_sem=recv3_sem.at[h, s],
                device_id=ring_device(i), device_id_type=MESH,
            ).wait_recv()
            return 0

        lax.fori_loop(1, 8, wait_ring, 0)
        total = recv3[h][0].astype(F32)
        for s in range(1, 8):
            total = total + recv3[h][s].astype(F32)
        if h == 0:
            swap_out[...] = jnp.concatenate([total[56:64], jnp.zeros((8, LANES), F32)], axis=0).astype(BF16)
            swap_copy().start()
            scale = jnp.maximum(total[0:8, :], 1.0)
            swap_copy().wait_recv()
            split = total[48:56, :] + swap_in[...].astype(F32)[0:8]
            total = jnp.concatenate([total[8:48, :], split], axis=0)
        first, end = CHUNK[h]
        bands = end - first
        mean = [(total[8 * b : 8 * b + 8, :] / scale).astype(BF16).astype(F32) for b in range(bands)]

        blank = jnp.zeros((8, LANES), F32)
        pixel = lax.broadcasted_iota(jnp.int32, (LANES, LANES), 0)
        spot = lax.broadcasted_iota(jnp.int32, (LANES, LANES), 1)
        pooled = None
        for g in range(min(4, bands)):
            left = jnp.concatenate([mean[g], mean[4 + g] if 4 + g < bands else blank], axis=0).astype(BF16)
            mix = jnp.where(spot == 32 * g + ((pixel & 63) >> 1), 0.25, 0.0).astype(BF16)
            part = jnp.dot(left, mix, preferred_element_type=F32)
            pooled = part if pooled is None else pooled + part
        pool[h] = pooled.astype(BF16)

        def send_line(z2, _):
            @pl.when(jnp.logical_not(stays(z2)))
            def _():
                line_copy(h, z2).start()
            return 0

        lax.fori_loop(0, 8, send_line, 0)
        spare = ROWS[h] // 8 - bands
        means[h][...] = jnp.concatenate(mean[0:bands] + [blank] * spare, axis=0).astype(BF16)

        @pl.when(jnp.logical_not(stays(my_row)))
        def _():
            comp_copy(h).start()

        @pl.when(stays(my_row))
        def _():
            comp[h][...] = means[h][...]

        @pl.when(at_home)
        def _():
            line[h, my_row] = pool[h]
        return scale

    def plane_device(i):
        xc2 = lax.rem(xc + i, 8)
        return xc2, (z_lo * 8 + xc2, tile)

    def plane_copy(h, i):
        return pltpu.make_async_remote_copy(
            src_ref=whole_line[h], dst_ref=rows[h].at[xc], send_sem=sg2_sem.at[h, i], recv_sem=rg2_sem.at[h, xc],
            device_id=plane_device(i)[1], device_id_type=MESH,
        )

    def spread_line(h):
        def wait_line(j, _):
            @pl.when(jnp.logical_not(jnp.logical_and(at_home, j == my_row)))
            def _():
                pltpu.make_async_remote_copy(
                    src_ref=pool.at[h], dst_ref=line.at[h, j], send_sem=sg1_sem.at[h, j], recv_sem=rg1_sem.at[h, j],
                    device_id=maker_device(j), device_id_type=MESH,
                ).wait_recv()
            return 0

        lax.fori_loop(0, 8, wait_line, 0)
        if h == 1:
            for q in range(4):
                both = [line[1, 2 * q + i].astype(F32)[0:8] for i in range(2)]
                packed[16 * q : 16 * q + 16, :] = jnp.concatenate(both, axis=0).astype(BF16)

        def send_plane(i, _):
            plane_copy(h, i).start()
            return 0

        lax.fori_loop(1, 8, send_plane, 0)
        rows[h][xc] = whole_line[h][...]

    reduce_box(0)
    reduce_box(1)
    scale = finish_mean(0, None)
    finish_mean(1, scale)
    spread_line(0)
    spread_line(1)

    for h in range(2):
        def wait_plane(i, _, h=h):
            xc2, device = plane_device(i)
            pltpu.make_async_remote_copy(
                src_ref=whole_line[h], dst_ref=rows[h].at[xc2], send_sem=sg2_sem.at[h, i], recv_sem=rg2_sem.at[h, xc2],
                device_id=device, device_id_type=MESH,
            ).wait_recv()
            return 0

        lax.fori_loop(1, 8, wait_plane, 0)
        if h == 0:
            _, _, mix, unit = matrices()
            level = [rows_a[i].astype(F32) for i in range(8)]
            fourth[...] = overviews(0, level, mix, unit, (t1, t2, t3), (one, two, three), lambda depth: None)

    swap_copy().wait_send()
    for h in range(2):
        def drain_box(slot, same, h=h):
            box_copy(h, same, slot, other_core).wait_send()

        each_pair(0, BOX - 1, drain_box)

        def drain_ring(i, _, h=h):
            ring_copy(h, i).wait_send()
            return 0

        lax.fori_loop(1, 8, drain_ring, 0)

        @pl.when(jnp.logical_not(stays(my_row)))
        def _(h=h):
            comp_copy(h).wait_send()

        @pl.when(jnp.logical_not(jnp.logical_and(at_home, my_row == z_lo)))
        def _(h=h):
            pltpu.make_async_remote_copy(
                src_ref=means[h], dst_ref=comp[h], send_sem=sc_sem.at[h], recv_sem=rc_sem.at[h],
                device_id=maker_device(z_lo), device_id_type=MESH,
            ).wait_recv()

        def drain_line(z2, _, h=h):
            @pl.when(jnp.logical_not(stays(z2)))
            def _():
                line_copy(h, z2).wait_send()
            return 0

        lax.fori_loop(0, 8, drain_line, 0)

        def drain_rows(i, _, h=h):
            plane_copy(h, i).wait_send()
            return 0

        lax.fori_loop(1, 8, drain_rows, 0)


def exchange(radiance, cloud_weight, footprint):
    any_space = pl.BlockSpec(memory_space=pl.ANY)
    vmem = pl.BlockSpec(memory_space=pltpu.VMEM)
    dma = pltpu.SemaphoreType.DMA
    return pl.pallas_call(
        exchange_kernel,
        out_shape=(
            jax.ShapeDtypeStruct((8, 64, LANES), BF16),
            *(jax.ShapeDtypeStruct((8, CHUNK[0][1], 32 >> i, 64 >> i), BF16) for i in range(3)),
            jax.ShapeDtypeStruct((8, 16, LANES), F32),
            *(jax.ShapeDtypeStruct((rows, LANES), BF16) for rows in ROWS),
        ),
        in_specs=[any_space] * 3,
        out_specs=(vmem,) * 7,
        scratch_shapes=[
            pltpu.VMEM((BANDS, K, PIX), BF16),
            pltpu.VMEM((K, PIX), jnp.int32),
            pltpu.VMEM((K, 128), jnp.int32),
            *(pltpu.VMEM((BOX, rows, LANES), BF16) for rows in ROWS * 2),
            pltpu.VMEM((128, 16 * BOX), BF16),
            pltpu.VMEM((128, 4 * LANES), F32),
            *(pltpu.VMEM((8, rows, LANES), BF16) for rows in ROWS * 2),
            *(pltpu.VMEM((rows, LANES), BF16) for rows in ROWS),
            *(pltpu.VMEM(shape, BF16) for shape in ((2, 16, LANES), (16, LANES), (16, LANES))),
            pltpu.VMEM((2, 8, 16, LANES), BF16),
            pltpu.VMEM((64, LANES), BF16),
            pltpu.VMEM((8, 8, 16, LANES), BF16),
            *(pltpu.VMEM((16 * (64 >> i), LANES), F32) for i in range(3)),
            pltpu.SemaphoreType.REGULAR((2,)),
            dma((3,)),
            dma((2, BOX)),
            dma((2, BOX)),
            dma((2, 8)),
            dma((2, 8)),
            dma((2, 8)),
            dma((2, 8)),
            dma((2, 8)),
            dma((2, 8)),
            dma((2,)),
            dma((2,)),
            dma((2,)),
        ],
        compiler_params=pltpu.CompilerParams(
            collective_id=0, has_side_effects=True, vmem_limit_bytes=16 * 1024 * 1024
        ),
        name="exchange",
    )(*(pltpu.with_memory_space_constraint(a, pltpu.HBM) for a in (jnp.transpose(radiance, (0, 2, 1, 3)), cloud_weight, footprint.T)))


def pyramid_kernel(rows_b, one_a, two_a, three_a, fourth_a, comp_a, comp_b, *refs):
    outs, (composite, four, five), parts, scratches, sems = refs[:6], refs[6:9], refs[9:12], refs[12:15], refs[15]
    early = [
        pltpu.make_async_copy(part, outs[1 + i].at[:, 0 : CHUNK[0][1]], sems.at[i]) for i, part in enumerate((one_a, two_a, three_a))
    ]
    late = [pltpu.make_async_copy(part, outs[1 + i].at[:, CHUNK[1][0] : BANDS], sems.at[3 + i]) for i, part in enumerate(parts)]
    rest = [pltpu.make_async_copy(part, outs[i], sems.at[6 + k]) for k, (part, i) in enumerate(((composite, 0), (four, 4), (five, 5)))]
    for copy in early:
        copy.start()
    for comp, (first, end) in zip((comp_a, comp_b), CHUNK):
        lines = comp[...].astype(F32)[0 : 8 * (end - first)]
        composite[first:end] = lines.reshape(end - first, 8, LANES).astype(BF16)
    rest[0].start()

    before, after, mix, unit = matrices()
    level = [rows_b[i].astype(F32).reshape(8, 8, LANES) for i in range(8)]
    fourth_b = overviews(1, level, mix, unit, scratches, parts, lambda depth: late[depth].start())
    fourth, fifth = [fourth_a[...], fourth_b], []
    for values in fourth:
        last = halve(values, mix).reshape(4, 2, -1, LANES)
        fifth.append((last[:, 0] + last[:, 1]).astype(BF16).astype(F32))

    for values, out, height, width in ((fourth, four, 8, 4), (fifth, five, 4, 2)):
        columns = []
        for c in range(width):
            total = None
            for h, line, (first, bands) in ((0, 0, GROUPS[0][0]), (0, 8, GROUPS[0][1]), (1, 0, GROUPS[1][0])):
                group = before >> 5
                spread = jnp.where(
                    jnp.logical_and(
                        jnp.logical_and((before & 31) == c, after == first + group), group < bands
                    ),
                    1.0, 0.0,
                ).astype(BF16)
                left = values[h][:, line : line + 8, :].reshape(8 * height, LANES).astype(BF16)
                part = jnp.dot(left, spread, preferred_element_type=F32)
                total = part if total is None else total + part
            columns.append(total)
        stacked = jnp.concatenate(columns, axis=0).astype(BF16)
        shape = (64 * height, 8 * height * width)
        to = lax.broadcasted_iota(jnp.int32, shape, 0)
        of = lax.broadcasted_iota(jnp.int32, shape, 1)
        high = {8: 3, 4: 2}[height]
        t, r, c = to >> (3 + high), (to >> 3) & (height - 1), to & 7
        order = jnp.where(of == c * (8 * height) + r * 8 + t, 1.0, 0.0).astype(BF16)
        placed = jnp.dot(order, stacked, preferred_element_type=F32)
        for t in range(8):
            for r in range(height):
                at = 8 * (t * height + r)
                out[t, r] = placed[at : at + width, 0:BANDS].astype(BF16)
        rest[1 if height == 8 else 2].start()
    for copy in early + late + rest:
        copy.wait()


def pyramid(*parts):
    vmem = pl.BlockSpec(memory_space=pltpu.VMEM)
    shapes = [(BANDS, 8, LANES)] + [(8, BANDS, 32 >> i, 64 >> i) for i in range(3)] + [(8, 8, 4, BANDS), (8, 4, 2, BANDS)]
    outs = pl.pallas_call(
        pyramid_kernel,
        out_shape=[jax.ShapeDtypeStruct(s, BF16) for s in shapes],
        in_specs=[vmem] * 7,
        out_specs=[pl.BlockSpec(memory_space=pl.ANY)] * 6,
        scratch_shapes=[pltpu.VMEM(shapes[i], BF16) for i in (0, 4, 5)]
        + [pltpu.VMEM((8, BANDS - CHUNK[1][0], 32 >> i, 64 >> i), BF16) for i in range(3)]
        + [pltpu.VMEM((8 * (64 >> i), LANES), F32) for i in range(3)]
        + [pltpu.SemaphoreType.DMA((9,))],
        compiler_params=pltpu.CompilerParams(vmem_limit_bytes=16 * 1024 * 1024),
        name="pyramid",
    )(*parts)
    orders = [(1, 0, 2)] + [(0, 1, 3, 2)] * 3 + [(0, 3, 1, 2)] * 2
    return tuple(jnp.transpose(out, order) for out, order in zip(outs, orders))


def on_device(radiance, cloud_weight, footprint):
    return pyramid(*exchange(radiance, cloud_weight, footprint))


def solution(mesh):
    in_specs = (P(("scene", "tile"), None, None, None), P(("scene", "tile"), None, None), P())
    out_specs = (
        P("tile", None, "scene"),
        P("tile", None, None, None),
        P("tile", None, None, None),
        P("tile", None, None, None),
        P("tile", None, None, None),
        P("tile", None, None, None),
    )
    return jax.shard_map(
        on_device, mesh=mesh, in_specs=in_specs, out_specs=out_specs, check_vma=False
    )
```

```python
import functools

import jax
import jax.numpy as jnp
from jax import lax
from jax.experimental import pallas as pl
from jax.experimental.pallas import tpu as pltpu
from jax.sharding import PartitionSpec as P

MESH = pl.DeviceIdType.MESH
K = 8
BANDS = 10
TILES = 64
PIX = 8192
LANES = 128
ROWS = (64, 32)
SHORT = 48
CHUNK = ((0, 6), (6, 10))
BOX = 64
F32 = jnp.float32
BF16 = jnp.bfloat16


STEPS = (
    (2, 2), (2, 1), (1, 2), (2, 3), (3, 2), (2, 0), (1, 1), (0, 2), (3, 3), (1, 3), (3, 1), (1, 0), (0, 1), (3, 0), (0, 3),
)
STEPS_X = sum(step[0] * 4**n for n, step in enumerate(STEPS))
STEPS_Y = sum(step[1] * 4**n for n, step in enumerate(STEPS))


GROUPS = (((0, 4), (4, 2)), ((6, 4),))


def matrices():
    before = lax.broadcasted_iota(jnp.int32, (LANES, LANES), 0)
    after = lax.broadcasted_iota(jnp.int32, (LANES, LANES), 1)
    same = (before >> 5) == (after >> 5)
    mix = jnp.where(jnp.logical_and(same, ((before & 31) >> 1) == (after & 31)), 0.25, 0.0).astype(BF16)
    unit = jnp.where(before == after, 1.0, 0.0).astype(BF16)
    return before, after, mix, unit


def halve(values, mix):
    flat = values.reshape(-1, LANES).astype(BF16)
    return jnp.dot(flat, mix, preferred_element_type=F32).reshape(values.shape)


def overviews(h, level, mix, unit, scratches, outs, done):
    lines = 8 * len(GROUPS[h])
    base = CHUNK[h][0]
    for depth in range(4):
        m = 8 >> depth
        if depth:
            level = [(halve(level[2 * q], mix) + halve(level[2 * q + 1], mix)).astype(BF16).astype(F32) for q in range(m)]
        if depth == 3:
            return level[0]
        scratch, out = scratches[depth], outs[depth]
        for q in range(m):
            for i in range(8):
                at = (i * m + q) * lines
                scratch[at : at + lines, :] = level[q][i]
        for r in range(lines):
            first, bands = GROUPS[h][r // 8]
            picked = scratch[pl.ds(r, 8 * m, stride=lines), :].astype(BF16)
            turned = lax.dot_general(
                unit[0 : 32 * bands], picked, (((1,), (1,)), ((), ())), preferred_element_type=F32
            )
            for g in range(bands):
                out[r % 8, first - base + g] = turned[32 * g : 32 * g + 4 * m].astype(BF16)
        done(depth)


def position():
    scene = lax.axis_index("scene")
    tile = lax.axis_index("tile")
    z_lo = lax.div(scene, 8)
    x = lax.rem(lax.div(scene, 2), 4)
    core = lax.rem(scene, 2)
    z_hi = lax.div(tile, 4)
    y = lax.rem(tile, 4)
    return z_lo, x, core, z_hi, y


def exchange_kernel(
    rad_ref, weight_ref, foot_ref, rows_b, one, two, three, fourth, comp_a, comp_b,
    rad, weight, foot, send_a, send_b, recv_a, recv_b, assign, acc, send3_a, send3_b, recv3_a, recv3_b, mean_a, mean_b, pool, swap_out, swap_in, line, packed, rows_a, t1, t2, t3,
    ring_sem, in_sem, send_sem, recv_sem, send3_sem, recv3_sem, sg1_sem, rg1_sem, sg2_sem, rg2_sem, sc_sem, rc_sem, swap_sem,
):
    send, recv, send3, recv3 = (send_a, send_b), (recv_a, recv_b), (send3_a, send3_b), (recv3_a, recv3_b)
    z_lo, x, core, z_hi, y = position()
    tile = z_hi * 4 + y
    xc = x * 2 + core
    pair = lax.div(z_lo, 2)
    odd = lax.rem(z_lo, 2)

    load_foot = pltpu.make_async_copy(foot_ref.at[:, pl.ds(pl.multiple_of(pair * 128, 128), 128)], foot, in_sem.at[2])
    load_weight = pltpu.make_async_copy(weight_ref.at[0], weight, in_sem.at[1])
    load_rad = pltpu.make_async_copy(rad_ref.at[0], rad, in_sem.at[0])
    load_weight.start()
    load_rad.start()
    load_foot.start()

    def box_device(x2, y2, c2, o2):
        block = (2 * y2 + o2) * 8 + x2 * 2 + c2
        return block, ((2 * pair + o2) * 8 + x2 * 2 + c2, z_hi * 4 + y2)

    def each_partner(visit):
        def four(n, x2, y2, count):
            for u in range(count):
                visit(4 * n + u, u % 2, x2, y2, core if u % 2 else 1 - core, odd if u // 2 else 1 - odd)

        def outer(n, carry):
            in_x, in_y = carry
            four(n, lax.rem(x + lax.rem(in_x, 4), 4), lax.rem(y + lax.rem(in_y, 4), 4), 4)
            return lax.div(in_x, 4), lax.div(in_y, 4)

        lax.fori_loop(0, 15, outer, (jnp.int32(STEPS_X), jnp.int32(STEPS_Y)))
        four(15, x, y, 3)

    ring = z_hi * 4 + pair

    def ring_device(step):
        box = lax.rem(ring + step, 8)
        return ((2 * lax.rem(box, 4) + odd) * 8 + xc, lax.div(box, 4) * 4 + y)

    group = lax.rem(ring + 2, 8)
    home = lax.rem(tile + 6, 8)
    comp, means = (comp_a, comp_b), (mean_a, mean_b)
    whole_line, rows = (line.at[0], packed), (rows_a, rows_b)

    def maker_device(j):
        return ((2 * lax.rem(home, 4) + lax.rem(j, 2)) * 8 + xc, lax.div(home, 4) * 4 + lax.div(j, 2))

    my_row = 2 * y + odd
    at_home = group == tile

    barrier = pltpu.get_barrier_semaphore()

    def greet(slot, same, *offset):
        pl.semaphore_signal(barrier, inc=1, device_id=box_device(*offset)[1], device_id_type=MESH)

    each_partner(greet)

    def clear(n, _):
        recv_a[2 * n, SHORT:64] = jnp.zeros((16, LANES), BF16)
        return 0

    lax.fori_loop(0, BOX // 2, clear, 0)
    for step in (1, 7):
        pl.semaphore_signal(barrier, inc=1, device_id=ring_device(step), device_id_type=MESH)

    def tell_ring():
        pl.semaphore_signal(ring_sem.at[0], inc=1, device_id=ring_device(1), device_id_type=MESH)
        pl.semaphore_signal(ring_sem.at[1], inc=1, device_id=ring_device(7), device_id_type=MESH)

    def hear_ring():
        pl.semaphore_wait(ring_sem.at[0], 1)
        pl.semaphore_wait(ring_sem.at[1], 1)

    load_weight.wait()
    load_rad.wait()
    pl.semaphore_wait(barrier, BOX - 1 + 2)
    tell_ring()

    def fill(h, same, block, out):
        pixels = pl.ds(pl.multiple_of(block * LANES, LANES), LANES)
        w = weight[:, pixels].astype(F32)
        twice = jnp.concatenate([w, w], axis=0).astype(BF16)
        if h == 1:
            for j in range(2):
                out[16 * j : 16 * j + 16, :] = rad[2 * j + 6 : 2 * j + 8, :, pixels].reshape(16, LANES) * twice
            return
        first = jnp.concatenate([w, w * rad[0, :, pixels].astype(F32)], axis=0).astype(BF16)
        out[0:16, :] = first
        for j in range(2):
            out[16 * j + 16 : 16 * j + 32, :] = rad[2 * j + 1 : 2 * j + 3, :, pixels].reshape(16, LANES) * twice
        if same:
            beside = pl.ds(pl.multiple_of((block + 1 - 2 * core) * LANES, LANES), LANES)
            mine = w * rad[5, :, pixels].astype(F32)
            theirs = weight[:, beside].astype(F32) * rad[5, :, beside].astype(F32)
            out[48:64, :] = jnp.concatenate([mine, theirs], axis=0).astype(BF16)

    def box_copy(h, same, slot, device):
        source, target = send[h].at[slot], recv[h].at[slot]
        if h == 0 and not same:
            source, target = send[h].at[slot, 0:SHORT], recv[h].at[slot, 0:SHORT]
        return pltpu.make_async_remote_copy(
            src_ref=source, dst_ref=target,
            send_sem=send_sem.at[h, slot], recv_sem=recv_sem.at[h, slot],
            device_id=device, device_id_type=MESH,
        )

    def each_pair(first, end, visit):
        def pair_of(n, _):
            visit(2 * n, 0)
            visit(2 * n + 1, 1)
            return 0

        lax.fori_loop(first // 2, end // 2, pair_of, 0)
        if end % 2:
            visit(end - 1, 0)

    other_core = box_device(x, y, 1 - core, odd)[1]

    for h in range(2):
        def send_box(slot, same, *offset, h=h):
            block, device = box_device(*offset)
            fill(h, same, block, send[h].at[slot])
            box_copy(h, same, slot, device).start()

        each_partner(send_box)
        fill(h, 1, my_row * 8 + xc, recv[h].at[BOX - 1])
        hear_ring()
        tell_ring()

    load_foot.wait()
    lane = lax.broadcasted_iota(jnp.int32, (1, 16 * BOX), 1)
    slot = lane >> 4
    step = slot >> 2
    dx, dy = jnp.zeros_like(slot), jnp.zeros_like(slot)
    for n, (far_x, far_y) in enumerate(STEPS):
        dx = jnp.where(step == n, far_x, dx)
        dy = jnp.where(step == n, far_y, dy)
    source_row = (
        (((odd + 1 - ((slot >> 1) & 1)) & 1) << 6)
        + (((x - dx) & 3) << 4)
        + (((core + 1 - (slot & 1)) & 1) << 3)
        + ((y - dy) & 3)
        + z_hi * 4
    )
    pick = jnp.where(lax.broadcasted_iota(jnp.int32, (128, 16 * BOX), 0) == source_row, 1.0, 0.0).astype(BF16)
    named = jnp.dot(foot[...].astype(F32).astype(BF16), pick, preferred_element_type=F32)
    own = lax.broadcasted_iota(jnp.int32, (K, 16 * BOX), 0) == (lane & 7)
    target = jnp.sum(jnp.where(own, named, 0.0), axis=0, keepdims=True).astype(jnp.int32) + ((lane & 8) << 3)
    row = lax.broadcasted_iota(jnp.int32, (128, 16 * BOX), 0)
    assign[...] = jnp.where(row == target, 1.0, 0.0).astype(BF16)
    hear_ring()
    tell_ring()

    def ring_copy(h, i):
        return pltpu.make_async_remote_copy(
            src_ref=send3[h].at[lax.rem(group + i, 8)], dst_ref=recv3[h].at[ring],
            send_sem=send3_sem.at[h, i], recv_sem=recv3_sem.at[h, ring],
            device_id=ring_device(i), device_id_type=MESH,
        )

    def reduce_box(h):
        def wait_box(slot, same):
            box_copy(h, same, slot, other_core).wait_recv()

        for g in range(4):
            each_pair(16 * g, min(16 * g + 16, BOX - 1), wait_box)
            left = assign[:, 256 * g : 256 * g + 256]
            right = jnp.concatenate(
                [recv[h][16 * g : 16 * g + 16, 16 * j : 16 * j + 16, :].reshape(256, LANES) for j in range(ROWS[h] // 16)],
                axis=1,
            )
            part = jnp.dot(left, right, preferred_element_type=F32)
            if g == 0:
                acc[:, 0 : 8 * ROWS[h]] = part
            else:
                acc[:, 0 : 8 * ROWS[h]] += part

        for o in range(8):
            for j in range(ROWS[h] // 16):
                lanes = slice(LANES * j, LANES * j + LANES)
                both = jnp.concatenate([acc[8 * o : 8 * o + 8, lanes], acc[64 + 8 * o : 72 + 8 * o, lanes]], axis=0)
                send3[h][o, 16 * j : 16 * j + 16, :] = both.astype(BF16)

        if h == 0:
            hear_ring()

        def send_ring(i, _):
            ring_copy(h, i).start()
            return 0

        lax.fori_loop(1, 8, send_ring, 0)
        recv3[h][ring] = send3[h][group]

    def line_copy(h, z2):
        return pltpu.make_async_remote_copy(
            src_ref=pool.at[h], dst_ref=line.at[h, my_row], send_sem=sg1_sem.at[h, z2], recv_sem=rg1_sem.at[h, my_row],
            device_id=(z2 * 8 + xc, group), device_id_type=MESH,
        )

    def comp_copy(h):
        return pltpu.make_async_remote_copy(
            src_ref=means[h], dst_ref=comp[h], send_sem=sc_sem.at[h], recv_sem=rc_sem.at[h],
            device_id=(my_row * 8 + xc, group), device_id_type=MESH,
        )

    def swap_copy():
        return pltpu.make_async_remote_copy(
            src_ref=swap_out, dst_ref=swap_in, send_sem=swap_sem.at[0], recv_sem=swap_sem.at[1],
            device_id=other_core, device_id_type=MESH,
        )

    def stays(z2):
        return jnp.logical_and(at_home, z2 == z_lo)

    def finish_mean(h, scale):
        def wait_ring(i, _):
            s = lax.rem(ring + i, 8)
            pltpu.make_async_remote_copy(
                src_ref=send3[h].at[s], dst_ref=recv3[h].at[s],
                send_sem=send3_sem.at[h, i], recv_sem=recv3_sem.at[h, s],
                device_id=ring_device(i), device_id_type=MESH,
            ).wait_recv()
            return 0

        lax.fori_loop(1, 8, wait_ring, 0)
        total = recv3[h][0].astype(F32)
        for s in range(1, 8):
            total = total + recv3[h][s].astype(F32)
        if h == 0:
            swap_out[...] = jnp.concatenate([total[56:64], jnp.zeros((8, LANES), F32)], axis=0).astype(BF16)
            swap_copy().start()
            scale = jnp.maximum(total[0:8, :], 1.0)
            swap_copy().wait_recv()
            split = total[48:56, :] + swap_in[...].astype(F32)[0:8]
            total = jnp.concatenate([total[8:48, :], split], axis=0)
        first, end = CHUNK[h]
        bands = end - first
        mean = [(total[8 * b : 8 * b + 8, :] / scale).astype(BF16).astype(F32) for b in range(bands)]

        blank = jnp.zeros((8, LANES), F32)
        pixel = lax.broadcasted_iota(jnp.int32, (LANES, LANES), 0)
        spot = lax.broadcasted_iota(jnp.int32, (LANES, LANES), 1)
        lefts, mixes = [], []
        for g in range(min(4, bands)):
            lefts.append(jnp.concatenate([mean[g], mean[4 + g] if 4 + g < bands else blank], axis=0).astype(BF16))
            mixes.append(jnp.where(spot == 32 * g + ((pixel & 63) >> 1), 0.25, 0.0).astype(BF16))
        pooled = jnp.dot(
            jnp.concatenate(lefts, axis=1), jnp.concatenate(mixes, axis=0), preferred_element_type=F32
        )
        pool[h] = pooled.astype(BF16)

        def send_line(z2, _):
            @pl.when(jnp.logical_not(stays(z2)))
            def _():
                line_copy(h, z2).start()
            return 0

        lax.fori_loop(0, 8, send_line, 0)
        spare = ROWS[h] // 8 - bands
        means[h][...] = jnp.concatenate(mean[0:bands] + [blank] * spare, axis=0).astype(BF16)

        @pl.when(jnp.logical_not(stays(my_row)))
        def _():
            comp_copy(h).start()

        @pl.when(stays(my_row))
        def _():
            comp[h][...] = means[h][...]

        @pl.when(at_home)
        def _():
            line[h, my_row] = pool[h]
        return scale

    def plane_device(i):
        xc2 = lax.rem(xc + i, 8)
        return xc2, (z_lo * 8 + xc2, tile)

    def plane_copy(h, i):
        return pltpu.make_async_remote_copy(
            src_ref=whole_line[h], dst_ref=rows[h].at[xc], send_sem=sg2_sem.at[h, i], recv_sem=rg2_sem.at[h, xc],
            device_id=plane_device(i)[1], device_id_type=MESH,
        )

    def spread_line(h):
        def wait_line(j, _):
            @pl.when(jnp.logical_not(jnp.logical_and(at_home, j == my_row)))
            def _():
                pltpu.make_async_remote_copy(
                    src_ref=pool.at[h], dst_ref=line.at[h, j], send_sem=sg1_sem.at[h, j], recv_sem=rg1_sem.at[h, j],
                    device_id=maker_device(j), device_id_type=MESH,
                ).wait_recv()
            return 0

        lax.fori_loop(0, 8, wait_line, 0)
        if h == 1:
            for q in range(4):
                both = [line[1, 2 * q + i].astype(F32)[0:8] for i in range(2)]
                packed[16 * q : 16 * q + 16, :] = jnp.concatenate(both, axis=0).astype(BF16)

        def send_plane(i, _):
            plane_copy(h, i).start()
            return 0

        lax.fori_loop(1, 8, send_plane, 0)
        rows[h][xc] = whole_line[h][...]

    def drain_box(h):
        def drain(slot, same):
            box_copy(h, same, slot, other_core).wait_send()

        each_pair(0, BOX - 1, drain)

    def drain_ring(h):
        def drain(i, _):
            ring_copy(h, i).wait_send()
            return 0

        lax.fori_loop(1, 8, drain, 0)

    def drain_line(h):
        @pl.when(jnp.logical_not(stays(my_row)))
        def _():
            comp_copy(h).wait_send()

        @pl.when(jnp.logical_not(jnp.logical_and(at_home, my_row == z_lo)))
        def _():
            pltpu.make_async_remote_copy(
                src_ref=means[h], dst_ref=comp[h], send_sem=sc_sem.at[h], recv_sem=rc_sem.at[h],
                device_id=maker_device(z_lo), device_id_type=MESH,
            ).wait_recv()

        def drain(z2, _):
            @pl.when(jnp.logical_not(stays(z2)))
            def _():
                line_copy(h, z2).wait_send()
            return 0

        lax.fori_loop(0, 8, drain, 0)

    def wait_plane(h):
        def wait(i, _):
            xc2, device = plane_device(i)
            pltpu.make_async_remote_copy(
                src_ref=whole_line[h], dst_ref=rows[h].at[xc2], send_sem=sg2_sem.at[h, i], recv_sem=rg2_sem.at[h, xc2],
                device_id=device, device_id_type=MESH,
            ).wait_recv()
            return 0

        lax.fori_loop(1, 8, wait, 0)

    def drain_plane(h):
        def drain(i, _):
            plane_copy(h, i).wait_send()
            return 0

        lax.fori_loop(1, 8, drain, 0)

    reduce_box(0)
    drain_box(0)
    reduce_box(1)
    drain_box(1)
    scale = finish_mean(0, None)
    drain_ring(0)
    finish_mean(1, scale)
    drain_ring(1)
    swap_copy().wait_send()
    spread_line(0)
    spread_line(1)
    wait_plane(0)
    _, _, mix, unit = matrices()
    level = [rows_a[i].astype(F32) for i in range(8)]
    fourth[...] = overviews(0, level, mix, unit, (t1, t2, t3), (one, two, three), lambda depth: None)
    for h in range(2):
        drain_line(h)
    drain_plane(0)
    wait_plane(1)
    drain_plane(1)


def exchange(radiance, cloud_weight, footprint):
    any_space = pl.BlockSpec(memory_space=pl.ANY)
    vmem = pl.BlockSpec(memory_space=pltpu.VMEM)
    dma = pltpu.SemaphoreType.DMA
    return pl.pallas_call(
        exchange_kernel,
        out_shape=(
            jax.ShapeDtypeStruct((8, 64, LANES), BF16),
            *(jax.ShapeDtypeStruct((8, CHUNK[0][1], 32 >> i, 64 >> i), BF16) for i in range(3)),
            jax.ShapeDtypeStruct((8, 16, LANES), F32),
            *(jax.ShapeDtypeStruct((rows, LANES), BF16) for rows in ROWS),
        ),
        in_specs=[any_space] * 3,
        out_specs=(vmem,) * 7,
        scratch_shapes=[
            pltpu.VMEM((BANDS, K, PIX), BF16),
            pltpu.VMEM((K, PIX), jnp.int32),
            pltpu.VMEM((K, 128), jnp.int32),
            *(pltpu.VMEM((BOX, rows, LANES), BF16) for rows in ROWS * 2),
            pltpu.VMEM((128, 16 * BOX), BF16),
            pltpu.VMEM((128, 4 * LANES), F32),
            *(pltpu.VMEM((8, rows, LANES), BF16) for rows in ROWS * 2),
            *(pltpu.VMEM((rows, LANES), BF16) for rows in ROWS),
            *(pltpu.VMEM(shape, BF16) for shape in ((2, 16, LANES), (16, LANES), (16, LANES))),
            pltpu.VMEM((2, 8, 16, LANES), BF16),
            pltpu.VMEM((64, LANES), BF16),
            pltpu.VMEM((8, 8, 16, LANES), BF16),
            *(pltpu.VMEM((16 * (64 >> i), LANES), F32) for i in range(3)),
            pltpu.SemaphoreType.REGULAR((2,)),
            dma((3,)),
            dma((2, BOX)),
            dma((2, BOX)),
            dma((2, 8)),
            dma((2, 8)),
            dma((2, 8)),
            dma((2, 8)),
            dma((2, 8)),
            dma((2, 8)),
            dma((2,)),
            dma((2,)),
            dma((2,)),
        ],
        compiler_params=pltpu.CompilerParams(
            collective_id=0, has_side_effects=True, vmem_limit_bytes=16 * 1024 * 1024
        ),
        name="exchange",
    )(*(pltpu.with_memory_space_constraint(a, pltpu.HBM) for a in (jnp.transpose(radiance, (0, 2, 1, 3)), cloud_weight, footprint.T)))


def pyramid_kernel(rows_b, one_a, two_a, three_a, fourth_a, comp_a, comp_b, *refs):
    outs, (composite, four, five), parts, scratches, sems = refs[:6], refs[6:9], refs[9:12], refs[12:15], refs[15]
    early = [
        pltpu.make_async_copy(part, outs[1 + i].at[:, 0 : CHUNK[0][1]], sems.at[i]) for i, part in enumerate((one_a, two_a, three_a))
    ]
    late = [pltpu.make_async_copy(part, outs[1 + i].at[:, CHUNK[1][0] : BANDS], sems.at[3 + i]) for i, part in enumerate(parts)]
    rest = [pltpu.make_async_copy(part, outs[i], sems.at[6 + k]) for k, (part, i) in enumerate(((composite, 0), (four, 4), (five, 5)))]
    for copy in early:
        copy.start()
    for comp, (first, end) in zip((comp_a, comp_b), CHUNK):
        lines = comp[...].astype(F32)[0 : 8 * (end - first)]
        composite[first:end] = lines.reshape(end - first, 8, LANES).astype(BF16)
    rest[0].start()

    before, after, mix, unit = matrices()
    level = [rows_b[i].astype(F32).reshape(8, 8, LANES) for i in range(8)]
    fourth_b = overviews(1, level, mix, unit, scratches, parts, lambda depth: None)
    for copy in late:
        copy.start()
    fourth, fifth = [fourth_a[...], fourth_b], []
    for values in fourth:
        last = halve(values, mix).reshape(4, 2, -1, LANES)
        fifth.append((last[:, 0] + last[:, 1]).astype(BF16).astype(F32))

    for values, out, height, width in ((fourth, four, 8, 4), (fifth, five, 4, 2)):
        columns = []
        for c in range(width):
            total = None
            for h, line, (first, bands) in ((0, 0, GROUPS[0][0]), (0, 8, GROUPS[0][1]), (1, 0, GROUPS[1][0])):
                group = before >> 5
                spread = jnp.where(
                    jnp.logical_and(
                        jnp.logical_and((before & 31) == c, after == first + group), group < bands
                    ),
                    1.0, 0.0,
                ).astype(BF16)
                left = values[h][:, line : line + 8, :].reshape(8 * height, LANES).astype(BF16)
                part = jnp.dot(left, spread, preferred_element_type=F32)
                total = part if total is None else total + part
            columns.append(total)
        stacked = jnp.concatenate(columns, axis=0).astype(BF16)
        shape = (64 * height, 8 * height * width)
        to = lax.broadcasted_iota(jnp.int32, shape, 0)
        of = lax.broadcasted_iota(jnp.int32, shape, 1)
        high = {8: 3, 4: 2}[height]
        t, r, c = to >> (3 + high), (to >> 3) & (height - 1), to & 7
        order = jnp.where(of == c * (8 * height) + r * 8 + t, 1.0, 0.0).astype(BF16)
        placed = jnp.dot(order, stacked, preferred_element_type=F32)
        for t in range(8):
            for r in range(height):
                at = 8 * (t * height + r)
                out[t, r] = placed[at : at + width, 0:BANDS].astype(BF16)
        rest[1 if height == 8 else 2].start()
    for copy in early + late + rest:
        copy.wait()


def pyramid(*parts):
    vmem = pl.BlockSpec(memory_space=pltpu.VMEM)
    shapes = [(BANDS, 8, LANES)] + [(8, BANDS, 32 >> i, 64 >> i) for i in range(3)] + [(8, 8, 4, BANDS), (8, 4, 2, BANDS)]
    outs = pl.pallas_call(
        pyramid_kernel,
        out_shape=[jax.ShapeDtypeStruct(s, BF16) for s in shapes],
        in_specs=[vmem] * 7,
        out_specs=[pl.BlockSpec(memory_space=pl.ANY)] * 6,
        scratch_shapes=[pltpu.VMEM(shapes[i], BF16) for i in (0, 4, 5)]
        + [pltpu.VMEM((8, BANDS - CHUNK[1][0], 32 >> i, 64 >> i), BF16) for i in range(3)]
        + [pltpu.VMEM((8 * (64 >> i), LANES), F32) for i in range(3)]
        + [pltpu.SemaphoreType.DMA((9,))],
        compiler_params=pltpu.CompilerParams(vmem_limit_bytes=16 * 1024 * 1024),
        name="pyramid",
    )(*parts)
    orders = [(1, 0, 2)] + [(0, 1, 3, 2)] * 3 + [(0, 3, 1, 2)] * 2
    return tuple(jnp.transpose(out, order) for out, order in zip(outs, orders))


def on_device(radiance, cloud_weight, footprint):
    return pyramid(*exchange(radiance, cloud_weight, footprint))


def solution(mesh):
    in_specs = (P(("scene", "tile"), None, None, None), P(("scene", "tile"), None, None), P())
    out_specs = (
        P("tile", None, "scene"),
        P("tile", None, None, None),
        P("tile", None, None, None),
        P("tile", None, None, None),
        P("tile", None, None, None),
        P("tile", None, None, None),
    )
    return jax.shard_map(
        on_device, mesh=mesh, in_specs=in_specs, out_specs=out_specs, check_vma=False
    )
```

```python
import functools

import jax
import jax.numpy as jnp
from jax import lax
from jax.experimental import pallas as pl
from jax.experimental.pallas import tpu as pltpu
from jax.sharding import PartitionSpec as P

MESH = pl.DeviceIdType.MESH
K = 8
BANDS = 10
TILES = 64
PIX = 8192
LANES = 128
ROWS = (64, 32)
SHORT = 48
CHUNK = ((0, 6), (6, 10))
BOX = 64
F32 = jnp.float32
BF16 = jnp.bfloat16


STEPS = (
    (2, 2), (2, 1), (1, 2), (2, 3), (3, 2), (2, 0), (1, 1), (0, 2), (3, 3), (1, 3), (3, 1), (1, 0), (0, 1), (3, 0), (0, 3),
)
STEPS_X = sum(step[0] * 4**n for n, step in enumerate(STEPS))
STEPS_Y = sum(step[1] * 4**n for n, step in enumerate(STEPS))


GROUPS = (((0, 4), (4, 2)), ((6, 4),))


def matrices():
    before = lax.broadcasted_iota(jnp.int32, (LANES, LANES), 0)
    after = lax.broadcasted_iota(jnp.int32, (LANES, LANES), 1)
    same = (before >> 5) == (after >> 5)
    mix = jnp.where(jnp.logical_and(same, ((before & 31) >> 1) == (after & 31)), 0.25, 0.0).astype(BF16)
    unit = jnp.where(before == after, 1.0, 0.0).astype(BF16)
    return before, after, mix, unit


def halve(values, mix):
    flat = values.reshape(-1, LANES).astype(BF16)
    return jnp.dot(flat, mix, preferred_element_type=F32).reshape(values.shape)


def overviews(h, level, mix, unit, scratches, outs, done):
    lines = 8 * len(GROUPS[h])
    base = CHUNK[h][0]
    for depth in range(4):
        m = 8 >> depth
        if depth:
            level = [(halve(level[2 * q], mix) + halve(level[2 * q + 1], mix)).astype(BF16).astype(F32) for q in range(m)]
        if depth == 3:
            return level[0]
        scratch, out = scratches[depth], outs[depth]
        for q in range(m):
            for i in range(8):
                at = (i * m + q) * lines
                scratch[at : at + lines, :] = level[q][i]
        for r in range(lines):
            first, bands = GROUPS[h][r // 8]
            picked = scratch[pl.ds(r, 8 * m, stride=lines), :].astype(BF16)
            turned = lax.dot_general(
                unit[0 : 32 * bands], picked, (((1,), (1,)), ((), ())), preferred_element_type=F32
            )
            for g in range(bands):
                out[r % 8, first - base + g] = turned[32 * g : 32 * g + 4 * m].astype(BF16)
        done(depth)


def fifth_of(fourth, mix):
    last = halve(fourth, mix).reshape(4, 2, -1, LANES)
    return (last[:, 0] + last[:, 1]).astype(BF16).astype(F32)


def bands_to_lanes(values, groups, height, width):
    before, after, _, _ = matrices()
    group = before >> 5
    columns = []
    for c in range(width):
        total = None
        for k, (first, bands) in enumerate(groups):
            spread = jnp.where(
                jnp.logical_and(jnp.logical_and((before & 31) == c, after == first + group), group < bands), 1.0, 0.0
            ).astype(BF16)
            left = values[:, 8 * k : 8 * k + 8, :].reshape(8 * height, LANES).astype(BF16)
            part = jnp.dot(left, spread, preferred_element_type=F32)
            total = part if total is None else total + part
        columns.append(total)
    return jnp.concatenate(columns, axis=0)


def row_order(height, width):
    shape = (64 * height, 8 * height * width)
    to = lax.broadcasted_iota(jnp.int32, shape, 0)
    of = lax.broadcasted_iota(jnp.int32, shape, 1)
    high = {8: 3, 4: 2}[height]
    t, r, c = to >> (3 + high), (to >> 3) & (height - 1), to & 7
    return jnp.where(of == c * (8 * height) + r * 8 + t, 1.0, 0.0).astype(BF16)


def position():
    scene = lax.axis_index("scene")
    tile = lax.axis_index("tile")
    z_lo = lax.div(scene, 8)
    x = lax.rem(lax.div(scene, 2), 4)
    core = lax.rem(scene, 2)
    z_hi = lax.div(tile, 4)
    y = lax.rem(tile, 4)
    return z_lo, x, core, z_hi, y


def exchange_kernel(
    rad_ref, weight_ref, foot_ref, rows_b, one, two, three, lanes_4, lanes_5, order_4, order_5, comp_a, comp_b,
    rad, weight, foot, send_a, send_b, recv_a, recv_b, assign, acc, send3_a, send3_b, recv3_a, recv3_b, mean_a, mean_b, pool, swap_out, swap_in, line, packed, rows_a, t1, t2, t3,
    ring_sem, in_sem, send_sem, recv_sem, send3_sem, recv3_sem, sg1_sem, rg1_sem, sg2_sem, rg2_sem, sc_sem, rc_sem, swap_sem,
):
    send, recv, send3, recv3 = (send_a, send_b), (recv_a, recv_b), (send3_a, send3_b), (recv3_a, recv3_b)
    z_lo, x, core, z_hi, y = position()
    tile = z_hi * 4 + y
    xc = x * 2 + core
    pair = lax.div(z_lo, 2)
    odd = lax.rem(z_lo, 2)

    load_foot = pltpu.make_async_copy(foot_ref.at[:, pl.ds(pl.multiple_of(pair * 128, 128), 128)], foot, in_sem.at[2])
    load_weight = pltpu.make_async_copy(weight_ref.at[0], weight, in_sem.at[1])
    load_rad = pltpu.make_async_copy(rad_ref.at[0], rad, in_sem.at[0])
    load_weight.start()
    load_rad.start()
    load_foot.start()

    def box_device(x2, y2, c2, o2):
        block = (2 * y2 + o2) * 8 + x2 * 2 + c2
        return block, ((2 * pair + o2) * 8 + x2 * 2 + c2, z_hi * 4 + y2)

    def each_partner(visit):
        def four(n, x2, y2, count):
            for u in range(count):
                visit(4 * n + u, u % 2, x2, y2, core if u % 2 else 1 - core, odd if u // 2 else 1 - odd)

        def outer(n, carry):
            in_x, in_y = carry
            four(n, lax.rem(x + lax.rem(in_x, 4), 4), lax.rem(y + lax.rem(in_y, 4), 4), 4)
            return lax.div(in_x, 4), lax.div(in_y, 4)

        lax.fori_loop(0, 15, outer, (jnp.int32(STEPS_X), jnp.int32(STEPS_Y)))
        four(15, x, y, 3)

    ring = z_hi * 4 + pair

    def ring_device(step):
        box = lax.rem(ring + step, 8)
        return ((2 * lax.rem(box, 4) + odd) * 8 + xc, lax.div(box, 4) * 4 + y)

    group = lax.rem(ring + 2, 8)
    home = lax.rem(tile + 6, 8)
    comp, means = (comp_a, comp_b), (mean_a, mean_b)
    whole_line, rows = (line.at[0], packed), (rows_a, rows_b)

    def maker_device(j):
        return ((2 * lax.rem(home, 4) + lax.rem(j, 2)) * 8 + xc, lax.div(home, 4) * 4 + lax.div(j, 2))

    my_row = 2 * y + odd
    at_home = group == tile

    barrier = pltpu.get_barrier_semaphore()

    def greet(slot, same, *offset):
        pl.semaphore_signal(barrier, inc=1, device_id=box_device(*offset)[1], device_id_type=MESH)

    each_partner(greet)

    def clear(n, _):
        recv_a[2 * n, SHORT:64] = jnp.zeros((16, LANES), BF16)
        return 0

    lax.fori_loop(0, BOX // 2, clear, 0)
    for step in (1, 7):
        pl.semaphore_signal(barrier, inc=1, device_id=ring_device(step), device_id_type=MESH)

    def tell_ring():
        pl.semaphore_signal(ring_sem.at[0], inc=1, device_id=ring_device(1), device_id_type=MESH)
        pl.semaphore_signal(ring_sem.at[1], inc=1, device_id=ring_device(7), device_id_type=MESH)

    def hear_ring():
        pl.semaphore_wait(ring_sem.at[0], 1)
        pl.semaphore_wait(ring_sem.at[1], 1)

    load_weight.wait()
    load_rad.wait()
    pl.semaphore_wait(barrier, BOX - 1 + 2)
    tell_ring()

    def fill(h, same, block, out):
        pixels = pl.ds(pl.multiple_of(block * LANES, LANES), LANES)
        w = weight[:, pixels].astype(F32)
        twice = jnp.concatenate([w, w], axis=0).astype(BF16)
        if h == 1:
            for j in range(2):
                out[16 * j : 16 * j + 16, :] = rad[2 * j + 6 : 2 * j + 8, :, pixels].reshape(16, LANES) * twice
            return
        first = jnp.concatenate([w, w * rad[0, :, pixels].astype(F32)], axis=0).astype(BF16)
        out[0:16, :] = first
        for j in range(2):
            out[16 * j + 16 : 16 * j + 32, :] = rad[2 * j + 1 : 2 * j + 3, :, pixels].reshape(16, LANES) * twice
        if same:
            beside = pl.ds(pl.multiple_of((block + 1 - 2 * core) * LANES, LANES), LANES)
            mine = w * rad[5, :, pixels].astype(F32)
            theirs = weight[:, beside].astype(F32) * rad[5, :, beside].astype(F32)
            out[48:64, :] = jnp.concatenate([mine, theirs], axis=0).astype(BF16)

    def box_copy(h, same, slot, device):
        source, target = send[h].at[slot], recv[h].at[slot]
        if h == 0 and not same:
            source, target = send[h].at[slot, 0:SHORT], recv[h].at[slot, 0:SHORT]
        return pltpu.make_async_remote_copy(
            src_ref=source, dst_ref=target,
            send_sem=send_sem.at[h, slot], recv_sem=recv_sem.at[h, slot],
            device_id=device, device_id_type=MESH,
        )

    def each_pair(first, end, visit):
        def pair_of(n, _):
            visit(2 * n, 0)
            visit(2 * n + 1, 1)
            return 0

        lax.fori_loop(first // 2, end // 2, pair_of, 0)
        if end % 2:
            visit(end - 1, 0)

    other_core = box_device(x, y, 1 - core, odd)[1]

    for h in range(2):
        def send_box(slot, same, *offset, h=h):
            block, device = box_device(*offset)
            fill(h, same, block, send[h].at[slot])
            box_copy(h, same, slot, device).start()

        each_partner(send_box)
        fill(h, 1, my_row * 8 + xc, recv[h].at[BOX - 1])
        hear_ring()
        tell_ring()

    load_foot.wait()
    lane = lax.broadcasted_iota(jnp.int32, (1, 16 * BOX), 1)
    slot = lane >> 4
    step = slot >> 2
    dx, dy = jnp.zeros_like(slot), jnp.zeros_like(slot)
    for n, (far_x, far_y) in enumerate(STEPS):
        dx = jnp.where(step == n, far_x, dx)
        dy = jnp.where(step == n, far_y, dy)
    source_row = (
        (((odd + 1 - ((slot >> 1) & 1)) & 1) << 6)
        + (((x - dx) & 3) << 4)
        + (((core + 1 - (slot & 1)) & 1) << 3)
        + ((y - dy) & 3)
        + z_hi * 4
    )
    pick = jnp.where(lax.broadcasted_iota(jnp.int32, (128, 16 * BOX), 0) == source_row, 1.0, 0.0).astype(BF16)
    named = jnp.dot(foot[...].astype(F32).astype(BF16), pick, preferred_element_type=F32)
    own = lax.broadcasted_iota(jnp.int32, (K, 16 * BOX), 0) == (lane & 7)
    target = jnp.sum(jnp.where(own, named, 0.0), axis=0, keepdims=True).astype(jnp.int32) + ((lane & 8) << 3)
    row = lax.broadcasted_iota(jnp.int32, (128, 16 * BOX), 0)
    assign[...] = jnp.where(row == target, 1.0, 0.0).astype(BF16)
    order_4[...] = row_order(8, 4)
    order_5[...] = row_order(4, 2)
    hear_ring()
    tell_ring()

    def ring_copy(h, i):
        return pltpu.make_async_remote_copy(
            src_ref=send3[h].at[lax.rem(group + i, 8)], dst_ref=recv3[h].at[ring],
            send_sem=send3_sem.at[h, i], recv_sem=recv3_sem.at[h, ring],
            device_id=ring_device(i), device_id_type=MESH,
        )

    def reduce_box(h):
        def wait_box(slot, same):
            box_copy(h, same, slot, other_core).wait_recv()

        for g in range(4):
            each_pair(16 * g, min(16 * g + 16, BOX - 1), wait_box)
            left = assign[:, 256 * g : 256 * g + 256]
            right = jnp.concatenate(
                [recv[h][16 * g : 16 * g + 16, 16 * j : 16 * j + 16, :].reshape(256, LANES) for j in range(ROWS[h] // 16)],
                axis=1,
            )
            part = jnp.dot(left, right, preferred_element_type=F32)
            if g == 0:
                acc[:, 0 : 8 * ROWS[h]] = part
            else:
                acc[:, 0 : 8 * ROWS[h]] += part

        for o in range(8):
            for j in range(ROWS[h] // 16):
                lanes = slice(LANES * j, LANES * j + LANES)
                both = jnp.concatenate([acc[8 * o : 8 * o + 8, lanes], acc[64 + 8 * o : 72 + 8 * o, lanes]], axis=0)
                send3[h][o, 16 * j : 16 * j + 16, :] = both.astype(BF16)

        if h == 0:
            hear_ring()

        def send_ring(i, _):
            ring_copy(h, i).start()
            return 0

        lax.fori_loop(1, 8, send_ring, 0)
        recv3[h][ring] = send3[h][group]

    def line_copy(h, z2):
        return pltpu.make_async_remote_copy(
            src_ref=pool.at[h], dst_ref=line.at[h, my_row], send_sem=sg1_sem.at[h, z2], recv_sem=rg1_sem.at[h, my_row],
            device_id=(z2 * 8 + xc, group), device_id_type=MESH,
        )

    def comp_copy(h):
        return pltpu.make_async_remote_copy(
            src_ref=means[h], dst_ref=comp[h], send_sem=sc_sem.at[h], recv_sem=rc_sem.at[h],
            device_id=(my_row * 8 + xc, group), device_id_type=MESH,
        )

    def swap_copy():
        return pltpu.make_async_remote_copy(
            src_ref=swap_out, dst_ref=swap_in, send_sem=swap_sem.at[0], recv_sem=swap_sem.at[1],
            device_id=other_core, device_id_type=MESH,
        )

    def stays(z2):
        return jnp.logical_and(at_home, z2 == z_lo)

    def finish_mean(h, scale):
        def wait_ring(i, _):
            s = lax.rem(ring + i, 8)
            pltpu.make_async_remote_copy(
                src_ref=send3[h].at[s], dst_ref=recv3[h].at[s],
                send_sem=send3_sem.at[h, i], recv_sem=recv3_sem.at[h, s],
                device_id=ring_device(i), device_id_type=MESH,
            ).wait_recv()
            return 0

        lax.fori_loop(1, 8, wait_ring, 0)
        total = recv3[h][0].astype(F32)
        for s in range(1, 8):
            total = total + recv3[h][s].astype(F32)
        if h == 0:
            swap_out[...] = jnp.concatenate([total[56:64], jnp.zeros((8, LANES), F32)], axis=0).astype(BF16)
            swap_copy().start()
            scale = jnp.maximum(total[0:8, :], 1.0)
            swap_copy().wait_recv()
            split = total[48:56, :] + swap_in[...].astype(F32)[0:8]
            total = jnp.concatenate([total[8:48, :], split], axis=0)
        first, end = CHUNK[h]
        bands = end - first
        mean = [(total[8 * b : 8 * b + 8, :] / scale).astype(BF16).astype(F32) for b in range(bands)]

        blank = jnp.zeros((8, LANES), F32)
        pixel = lax.broadcasted_iota(jnp.int32, (LANES, LANES), 0)
        spot = lax.broadcasted_iota(jnp.int32, (LANES, LANES), 1)
        lefts, mixes = [], []
        for g in range(min(4, bands)):
            lefts.append(jnp.concatenate([mean[g], mean[4 + g] if 4 + g < bands else blank], axis=0).astype(BF16))
            mixes.append(jnp.where(spot == 32 * g + ((pixel & 63) >> 1), 0.25, 0.0).astype(BF16))
        pooled = jnp.dot(
            jnp.concatenate(lefts, axis=1), jnp.concatenate(mixes, axis=0), preferred_element_type=F32
        )
        pool[h] = pooled.astype(BF16)

        def send_line(z2, _):
            @pl.when(jnp.logical_not(stays(z2)))
            def _():
                line_copy(h, z2).start()
            return 0

        lax.fori_loop(0, 8, send_line, 0)
        spare = ROWS[h] // 8 - bands
        means[h][...] = jnp.concatenate(mean[0:bands] + [blank] * spare, axis=0).astype(BF16)

        @pl.when(jnp.logical_not(stays(my_row)))
        def _():
            comp_copy(h).start()

        @pl.when(stays(my_row))
        def _():
            comp[h][...] = means[h][...]

        @pl.when(at_home)
        def _():
            line[h, my_row] = pool[h]
        return scale

    def plane_device(i):
        xc2 = lax.rem(xc + i, 8)
        return xc2, (z_lo * 8 + xc2, tile)

    def plane_copy(h, i):
        return pltpu.make_async_remote_copy(
            src_ref=whole_line[h], dst_ref=rows[h].at[xc], send_sem=sg2_sem.at[h, i], recv_sem=rg2_sem.at[h, xc],
            device_id=plane_device(i)[1], device_id_type=MESH,
        )

    def spread_line(h):
        def wait_line(j, _):
            @pl.when(jnp.logical_not(jnp.logical_and(at_home, j == my_row)))
            def _():
                pltpu.make_async_remote_copy(
                    src_ref=pool.at[h], dst_ref=line.at[h, j], send_sem=sg1_sem.at[h, j], recv_sem=rg1_sem.at[h, j],
                    device_id=maker_device(j), device_id_type=MESH,
                ).wait_recv()
            return 0

        lax.fori_loop(0, 8, wait_line, 0)
        if h == 1:
            for q in range(4):
                both = [line[1, 2 * q + i].astype(F32)[0:8] for i in range(2)]
                packed[16 * q : 16 * q + 16, :] = jnp.concatenate(both, axis=0).astype(BF16)

        def send_plane(i, _):
            plane_copy(h, i).start()
            return 0

        lax.fori_loop(1, 8, send_plane, 0)
        rows[h][xc] = whole_line[h][...]

    def drain_box(h):
        def drain(slot, same):
            box_copy(h, same, slot, other_core).wait_send()

        each_pair(0, BOX - 1, drain)

    def drain_ring(h):
        def drain(i, _):
            ring_copy(h, i).wait_send()
            return 0

        lax.fori_loop(1, 8, drain, 0)

    def drain_line(h):
        @pl.when(jnp.logical_not(stays(my_row)))
        def _():
            comp_copy(h).wait_send()

        @pl.when(jnp.logical_not(jnp.logical_and(at_home, my_row == z_lo)))
        def _():
            pltpu.make_async_remote_copy(
                src_ref=means[h], dst_ref=comp[h], send_sem=sc_sem.at[h], recv_sem=rc_sem.at[h],
                device_id=maker_device(z_lo), device_id_type=MESH,
            ).wait_recv()

        def drain(z2, _):
            @pl.when(jnp.logical_not(stays(z2)))
            def _():
                line_copy(h, z2).wait_send()
            return 0

        lax.fori_loop(0, 8, drain, 0)

    def wait_plane(h):
        def wait(i, _):
            xc2, device = plane_device(i)
            pltpu.make_async_remote_copy(
                src_ref=whole_line[h], dst_ref=rows[h].at[xc2], send_sem=sg2_sem.at[h, i], recv_sem=rg2_sem.at[h, xc2],
                device_id=device, device_id_type=MESH,
            ).wait_recv()
            return 0

        lax.fori_loop(1, 8, wait, 0)

    def drain_plane(h):
        def drain(i, _):
            plane_copy(h, i).wait_send()
            return 0

        lax.fori_loop(1, 8, drain, 0)

    reduce_box(0)
    drain_box(0)
    reduce_box(1)
    drain_box(1)
    scale = finish_mean(0, None)
    drain_ring(0)
    finish_mean(1, scale)
    drain_ring(1)
    swap_copy().wait_send()
    spread_line(0)
    spread_line(1)
    wait_plane(0)
    _, _, mix, unit = matrices()
    level = [rows_a[i].astype(F32) for i in range(8)]
    fourth = overviews(0, level, mix, unit, (t1, t2, t3), (one, two, three), lambda depth: None)
    lanes_4[...] = bands_to_lanes(fourth, GROUPS[0], 8, 4)
    lanes_5[...] = bands_to_lanes(fifth_of(fourth, mix), GROUPS[0], 4, 2)
    for h in range(2):
        drain_line(h)
    drain_plane(0)
    wait_plane(1)
    drain_plane(1)


def exchange(radiance, cloud_weight, footprint):
    any_space = pl.BlockSpec(memory_space=pl.ANY)
    vmem = pl.BlockSpec(memory_space=pltpu.VMEM)
    dma = pltpu.SemaphoreType.DMA
    return pl.pallas_call(
        exchange_kernel,
        out_shape=(
            jax.ShapeDtypeStruct((8, 64, LANES), BF16),
            *(jax.ShapeDtypeStruct((8, CHUNK[0][1], 32 >> i, 64 >> i), BF16) for i in range(3)),
            jax.ShapeDtypeStruct((256, LANES), F32),
            jax.ShapeDtypeStruct((64, LANES), F32),
            jax.ShapeDtypeStruct((512, 256), BF16),
            jax.ShapeDtypeStruct((256, 64), BF16),
            *(jax.ShapeDtypeStruct((rows, LANES), BF16) for rows in ROWS),
        ),
        in_specs=[any_space] * 3,
        out_specs=(vmem,) * 10,
        scratch_shapes=[
            pltpu.VMEM((BANDS, K, PIX), BF16),
            pltpu.VMEM((K, PIX), jnp.int32),
            pltpu.VMEM((K, 128), jnp.int32),
            *(pltpu.VMEM((BOX, rows, LANES), BF16) for rows in ROWS * 2),
            pltpu.VMEM((128, 16 * BOX), BF16),
            pltpu.VMEM((128, 4 * LANES), F32),
            *(pltpu.VMEM((8, rows, LANES), BF16) for rows in ROWS * 2),
            *(pltpu.VMEM((rows, LANES), BF16) for rows in ROWS),
            *(pltpu.VMEM(shape, BF16) for shape in ((2, 16, LANES), (16, LANES), (16, LANES))),
            pltpu.VMEM((2, 8, 16, LANES), BF16),
            pltpu.VMEM((64, LANES), BF16),
            pltpu.VMEM((8, 8, 16, LANES), BF16),
            *(pltpu.VMEM((16 * (64 >> i), LANES), F32) for i in range(3)),
            pltpu.SemaphoreType.REGULAR((2,)),
            dma((3,)),
            dma((2, BOX)),
            dma((2, BOX)),
            dma((2, 8)),
            dma((2, 8)),
            dma((2, 8)),
            dma((2, 8)),
            dma((2, 8)),
            dma((2, 8)),
            dma((2,)),
            dma((2,)),
            dma((2,)),
        ],
        compiler_params=pltpu.CompilerParams(
            collective_id=0, has_side_effects=True, vmem_limit_bytes=16 * 1024 * 1024
        ),
        name="exchange",
    )(*(pltpu.with_memory_space_constraint(a, pltpu.HBM) for a in (jnp.transpose(radiance, (0, 2, 1, 3)), cloud_weight, footprint.T)))


def pyramid_kernel(rows_b, one_a, two_a, three_a, lanes_4, lanes_5, order_4, order_5, comp_a, comp_b, *refs):
    outs, (composite, four, five), parts, scratches, sems = refs[:6], refs[6:9], refs[9:12], refs[12:15], refs[15]
    early = [
        pltpu.make_async_copy(part, outs[1 + i].at[:, 0 : CHUNK[0][1]], sems.at[i]) for i, part in enumerate((one_a, two_a, three_a))
    ]
    late = [pltpu.make_async_copy(part, outs[1 + i].at[:, CHUNK[1][0] : BANDS], sems.at[3 + i]) for i, part in enumerate(parts)]
    rest = [pltpu.make_async_copy(part, outs[i], sems.at[6 + k]) for k, (part, i) in enumerate(((composite, 0), (four, 4), (five, 5)))]
    for copy in early:
        copy.start()
    for comp, (first, end) in zip((comp_a, comp_b), CHUNK):
        lines = comp[...].astype(F32)[0 : 8 * (end - first)]
        composite[first:end] = lines.reshape(end - first, 8, LANES).astype(BF16)
    rest[0].start()

    _, _, mix, unit = matrices()
    level = [rows_b[i].astype(F32).reshape(8, 8, LANES) for i in range(8)]
    fourth_b = overviews(1, level, mix, unit, scratches, parts, lambda depth: None)
    for copy in late:
        copy.start()
    fifth_b = fifth_of(fourth_b, mix)

    for values, lanes, order, out, height, width in (
        (fourth_b, lanes_4, order_4, four, 8, 4), (fifth_b, lanes_5, order_5, five, 4, 2)
    ):
        stacked = (lanes[...] + bands_to_lanes(values, GROUPS[1], height, width)).astype(BF16)
        placed = jnp.dot(order[...], stacked, preferred_element_type=F32)
        for t in range(8):
            for r in range(height):
                at = 8 * (t * height + r)
                out[t, r] = placed[at : at + width, 0:BANDS].astype(BF16)
        rest[1 if height == 8 else 2].start()
    for copy in early + late + rest:
        copy.wait()


def pyramid(*parts):
    vmem = pl.BlockSpec(memory_space=pltpu.VMEM)
    shapes = [(BANDS, 8, LANES)] + [(8, BANDS, 32 >> i, 64 >> i) for i in range(3)] + [(8, 8, 4, BANDS), (8, 4, 2, BANDS)]
    outs = pl.pallas_call(
        pyramid_kernel,
        out_shape=[jax.ShapeDtypeStruct(s, BF16) for s in shapes],
        in_specs=[vmem] * 10,
        out_specs=[pl.BlockSpec(memory_space=pl.ANY)] * 6,
        scratch_shapes=[pltpu.VMEM(shapes[i], BF16) for i in (0, 4, 5)]
        + [pltpu.VMEM((8, BANDS - CHUNK[1][0], 32 >> i, 64 >> i), BF16) for i in range(3)]
        + [pltpu.VMEM((8 * (64 >> i), LANES), F32) for i in range(3)]
        + [pltpu.SemaphoreType.DMA((9,))],
        compiler_params=pltpu.CompilerParams(vmem_limit_bytes=16 * 1024 * 1024),
        name="pyramid",
    )(*parts)
    orders = [(1, 0, 2)] + [(0, 1, 3, 2)] * 3 + [(0, 3, 1, 2)] * 2
    return tuple(jnp.transpose(out, order) for out, order in zip(outs, orders))


def on_device(radiance, cloud_weight, footprint):
    return pyramid(*exchange(radiance, cloud_weight, footprint))


def solution(mesh):
    in_specs = (P(("scene", "tile"), None, None, None), P(("scene", "tile"), None, None), P())
    out_specs = (
        P("tile", None, "scene"),
        P("tile", None, None, None),
        P("tile", None, None, None),
        P("tile", None, None, None),
        P("tile", None, None, None),
        P("tile", None, None, None),
    )
    return jax.shard_map(
        on_device, mesh=mesh, in_specs=in_specs, out_specs=out_specs, check_vma=False
    )
```

```python
import functools

import jax
import jax.numpy as jnp
from jax import lax
from jax.experimental import pallas as pl
from jax.experimental.pallas import tpu as pltpu
from jax.sharding import PartitionSpec as P

MESH = pl.DeviceIdType.MESH
K = 8
BANDS = 10
TILES = 64
PIX = 8192
LANES = 128
ROWS = (64, 32)
SHORT = 48
CHUNK = ((0, 6), (6, 10))
BOX = 64
F32 = jnp.float32
BF16 = jnp.bfloat16


STEPS = (
    (2, 2), (2, 1), (1, 2), (2, 3), (3, 2), (2, 0), (1, 1), (0, 2), (3, 3), (1, 3), (3, 1), (1, 0), (0, 1), (3, 0), (0, 3),
)
STEPS_X = sum(step[0] * 4**n for n, step in enumerate(STEPS))
STEPS_Y = sum(step[1] * 4**n for n, step in enumerate(STEPS))


GROUPS = (((0, 4), (4, 2)), ((6, 4),))


def matrices():
    before = lax.broadcasted_iota(jnp.int32, (LANES, LANES), 0)
    after = lax.broadcasted_iota(jnp.int32, (LANES, LANES), 1)
    same = (before >> 5) == (after >> 5)
    mix = jnp.where(jnp.logical_and(same, ((before & 31) >> 1) == (after & 31)), 0.25, 0.0).astype(BF16)
    unit = jnp.where(before == after, 1.0, 0.0).astype(BF16)
    return before, after, mix, unit


def halve(values, mix):
    flat = values.reshape(-1, LANES).astype(BF16)
    return jnp.dot(flat, mix, preferred_element_type=F32).reshape(values.shape)


def overviews(h, level, mix, unit, scratches, outs, done):
    lines = 8 * len(GROUPS[h])
    base = CHUNK[h][0]
    for depth in range(4):
        m = 8 >> depth
        if depth:
            level = [(halve(level[2 * q], mix) + halve(level[2 * q + 1], mix)).astype(BF16).astype(F32) for q in range(m)]
        if depth == 3:
            return level[0]
        scratch, out = scratches[depth], outs[depth]
        for q in range(m):
            for i in range(8):
                at = (i * m + q) * lines
                scratch[at : at + lines, :] = level[q][i]
        for r in range(lines):
            first, bands = GROUPS[h][r // 8]
            picked = scratch[pl.ds(r, 8 * m, stride=lines), :].astype(BF16)
            turned = lax.dot_general(
                unit[0 : 32 * bands], picked, (((1,), (1,)), ((), ())), preferred_element_type=F32
            )
            for g in range(bands):
                out[r % 8, first - base + g] = turned[32 * g : 32 * g + 4 * m].astype(BF16)
        done(depth)


def position():
    scene = lax.axis_index("scene")
    tile = lax.axis_index("tile")
    z_lo = lax.div(scene, 8)
    x = lax.rem(lax.div(scene, 2), 4)
    core = lax.rem(scene, 2)
    z_hi = lax.div(tile, 4)
    y = lax.rem(tile, 4)
    return z_lo, x, core, z_hi, y


def exchange_kernel(
    rad_ref, weight_ref, foot_ref, rows_b, one, two, three, fourth, comp_a, comp_b,
    rad, weight, foot, send_a, send_b, recv_a, recv_b, assign, acc, send3_a, send3_b, recv3_a, recv3_b, mean_a, mean_b, pool, swap_out, swap_in, line, packed, rows_a, t1, t2, t3,
    ring_sem, in_sem, send_sem, recv_sem, send3_sem, recv3_sem, sg1_sem, rg1_sem, sg2_sem, rg2_sem, sc_sem, rc_sem, swap_sem,
):
    send, recv, send3, recv3 = (send_a, send_b), (recv_a, recv_b), (send3_a, send3_b), (recv3_a, recv3_b)
    z_lo, x, core, z_hi, y = position()
    tile = z_hi * 4 + y
    xc = x * 2 + core
    pair = lax.div(z_lo, 2)
    odd = lax.rem(z_lo, 2)

    load_foot = pltpu.make_async_copy(foot_ref.at[:, pl.ds(pl.multiple_of(pair * 128, 128), 128)], foot, in_sem.at[2])
    load_weight = pltpu.make_async_copy(weight_ref.at[0], weight, in_sem.at[1])
    load_rad = pltpu.make_async_copy(rad_ref.at[0], rad, in_sem.at[0])
    load_weight.start()
    load_rad.start()
    load_foot.start()

    def box_device(x2, y2, c2, o2):
        block = (2 * y2 + o2) * 8 + x2 * 2 + c2
        return block, ((2 * pair + o2) * 8 + x2 * 2 + c2, z_hi * 4 + y2)

    def each_partner(visit):
        def four(n, x2, y2, count):
            for u in range(count):
                visit(4 * n + u, u % 2, x2, y2, core if u % 2 else 1 - core, odd if u // 2 else 1 - odd)

        def outer(n, carry):
            in_x, in_y = carry
            four(n, lax.rem(x + lax.rem(in_x, 4), 4), lax.rem(y + lax.rem(in_y, 4), 4), 4)
            return lax.div(in_x, 4), lax.div(in_y, 4)

        lax.fori_loop(0, 15, outer, (jnp.int32(STEPS_X), jnp.int32(STEPS_Y)))
        four(15, x, y, 3)

    ring = z_hi * 4 + pair

    def ring_device(step):
        box = lax.rem(ring + step, 8)
        return ((2 * lax.rem(box, 4) + odd) * 8 + xc, lax.div(box, 4) * 4 + y)

    group = lax.rem(ring + 2, 8)
    home = lax.rem(tile + 6, 8)
    comp, means = (comp_a, comp_b), (mean_a, mean_b)
    whole_line, rows = (line.at[0], packed), (rows_a, rows_b)

    def maker_device(j):
        return ((2 * lax.rem(home, 4) + lax.rem(j, 2)) * 8 + xc, lax.div(home, 4) * 4 + lax.div(j, 2))

    my_row = 2 * y + odd
    at_home = group == tile

    barrier = pltpu.get_barrier_semaphore()

    def greet(slot, same, *offset):
        pl.semaphore_signal(barrier, inc=1, device_id=box_device(*offset)[1], device_id_type=MESH)

    each_partner(greet)

    def clear(n, _):
        recv_a[2 * n, SHORT:64] = jnp.zeros((16, LANES), BF16)
        return 0

    lax.fori_loop(0, BOX // 2, clear, 0)
    for step in (1, 7):
        pl.semaphore_signal(barrier, inc=1, device_id=ring_device(step), device_id_type=MESH)

    def tell_ring():
        pl.semaphore_signal(ring_sem.at[0], inc=1, device_id=ring_device(1), device_id_type=MESH)
        pl.semaphore_signal(ring_sem.at[1], inc=1, device_id=ring_device(7), device_id_type=MESH)

    def hear_ring():
        pl.semaphore_wait(ring_sem.at[0], 1)
        pl.semaphore_wait(ring_sem.at[1], 1)

    load_weight.wait()
    load_rad.wait()
    pl.semaphore_wait(barrier, BOX - 1 + 2)
    tell_ring()

    def fill(h, same, block, out):
        pixels = pl.ds(pl.multiple_of(block * LANES, LANES), LANES)
        w = weight[:, pixels].astype(F32)
        twice = jnp.concatenate([w, w], axis=0).astype(BF16)
        if h == 1:
            for j in range(2):
                out[16 * j : 16 * j + 16, :] = rad[2 * j + 6 : 2 * j + 8, :, pixels].reshape(16, LANES) * twice
            return
        first = jnp.concatenate([w, w * rad[0, :, pixels].astype(F32)], axis=0).astype(BF16)
        out[0:16, :] = first
        for j in range(2):
            out[16 * j + 16 : 16 * j + 32, :] = rad[2 * j + 1 : 2 * j + 3, :, pixels].reshape(16, LANES) * twice
        if same:
            beside = pl.ds(pl.multiple_of((block + 1 - 2 * core) * LANES, LANES), LANES)
            mine = w * rad[5, :, pixels].astype(F32)
            theirs = weight[:, beside].astype(F32) * rad[5, :, beside].astype(F32)
            out[48:64, :] = jnp.concatenate([mine, theirs], axis=0).astype(BF16)

    def box_copy(h, same, slot, device):
        source, target = send[h].at[slot], recv[h].at[slot]
        if h == 0 and not same:
            source, target = send[h].at[slot, 0:SHORT], recv[h].at[slot, 0:SHORT]
        return pltpu.make_async_remote_copy(
            src_ref=source, dst_ref=target,
            send_sem=send_sem.at[h, slot], recv_sem=recv_sem.at[h, slot],
            device_id=device, device_id_type=MESH,
        )

    def each_pair(first, end, visit):
        def pair_of(n, _):
            visit(2 * n, 0)
            visit(2 * n + 1, 1)
            return 0

        lax.fori_loop(first // 2, end // 2, pair_of, 0)
        if end % 2:
            visit(end - 1, 0)

    other_core = box_device(x, y, 1 - core, odd)[1]

    for h in range(2):
        def send_box(slot, same, *offset, h=h):
            block, device = box_device(*offset)
            fill(h, same, block, send[h].at[slot])
            box_copy(h, same, slot, device).start()

        each_partner(send_box)
        fill(h, 1, my_row * 8 + xc, recv[h].at[BOX - 1])
        hear_ring()
        tell_ring()

    load_foot.wait()
    lane = lax.broadcasted_iota(jnp.int32, (1, 16 * BOX), 1)
    slot = lane >> 4
    step = slot >> 2
    dx, dy = jnp.zeros_like(slot), jnp.zeros_like(slot)
    for n, (far_x, far_y) in enumerate(STEPS):
        dx = jnp.where(step == n, far_x, dx)
        dy = jnp.where(step == n, far_y, dy)
    source_row = (
        (((odd + 1 - ((slot >> 1) & 1)) & 1) << 6)
        + (((x - dx) & 3) << 4)
        + (((core + 1 - (slot & 1)) & 1) << 3)
        + ((y - dy) & 3)
        + z_hi * 4
    )
    pick = jnp.where(lax.broadcasted_iota(jnp.int32, (128, 16 * BOX), 0) == source_row, 1.0, 0.0).astype(BF16)
    named = jnp.dot(foot[...].astype(F32).astype(BF16), pick, preferred_element_type=F32)
    own = lax.broadcasted_iota(jnp.int32, (K, 16 * BOX), 0) == (lane & 7)
    target = jnp.sum(jnp.where(own, named, 0.0), axis=0, keepdims=True).astype(jnp.int32) + ((lane & 8) << 3)
    row = lax.broadcasted_iota(jnp.int32, (128, 16 * BOX), 0)
    assign[...] = jnp.where(row == target, 1.0, 0.0).astype(BF16)
    hear_ring()
    tell_ring()

    def ring_copy(h, i):
        return pltpu.make_async_remote_copy(
            src_ref=send3[h].at[lax.rem(group + i, 8)], dst_ref=recv3[h].at[ring],
            send_sem=send3_sem.at[h, i], recv_sem=recv3_sem.at[h, ring],
            device_id=ring_device(i), device_id_type=MESH,
        )

    def reduce_box(h):
        def wait_box(slot, same):
            box_copy(h, same, slot, other_core).wait_recv()

        for g in range(4):
            each_pair(16 * g, min(16 * g + 16, BOX - 1), wait_box)
            left = assign[:, 256 * g : 256 * g + 256]
            right = jnp.concatenate(
                [recv[h][16 * g : 16 * g + 16, 16 * j : 16 * j + 16, :].reshape(256, LANES) for j in range(ROWS[h] // 16)],
                axis=1,
            )
            part = jnp.dot(left, right, preferred_element_type=F32)
            if g == 0:
                acc[:, 0 : 8 * ROWS[h]] = part
            else:
                acc[:, 0 : 8 * ROWS[h]] += part

        for o in range(8):
            for j in range(ROWS[h] // 16):
                lanes = slice(LANES * j, LANES * j + LANES)
                both = jnp.concatenate([acc[8 * o : 8 * o + 8, lanes], acc[64 + 8 * o : 72 + 8 * o, lanes]], axis=0)
                send3[h][o, 16 * j : 16 * j + 16, :] = both.astype(BF16)

        if h == 0:
            hear_ring()

        def send_ring(i, _):
            ring_copy(h, 4 + lax.div(i, 2) * (1 - 2 * lax.rem(i, 2))).start()
            return 0

        lax.fori_loop(1, 8, send_ring, 0)
        recv3[h][ring] = send3[h][group]

    def line_copy(h, z2):
        return pltpu.make_async_remote_copy(
            src_ref=pool.at[h], dst_ref=line.at[h, my_row], send_sem=sg1_sem.at[h, z2], recv_sem=rg1_sem.at[h, my_row],
            device_id=(z2 * 8 + xc, group), device_id_type=MESH,
        )

    def comp_copy(h):
        return pltpu.make_async_remote_copy(
            src_ref=means[h], dst_ref=comp[h], send_sem=sc_sem.at[h], recv_sem=rc_sem.at[h],
            device_id=(my_row * 8 + xc, group), device_id_type=MESH,
        )

    def swap_copy():
        return pltpu.make_async_remote_copy(
            src_ref=swap_out, dst_ref=swap_in, send_sem=swap_sem.at[0], recv_sem=swap_sem.at[1],
            device_id=other_core, device_id_type=MESH,
        )

    def stays(z2):
        return jnp.logical_and(at_home, z2 == z_lo)

    def finish_mean(h, scale):
        def wait_ring(i, _):
            s = lax.rem(ring + i, 8)
            pltpu.make_async_remote_copy(
                src_ref=send3[h].at[s], dst_ref=recv3[h].at[s],
                send_sem=send3_sem.at[h, i], recv_sem=recv3_sem.at[h, s],
                device_id=ring_device(i), device_id_type=MESH,
            ).wait_recv()
            return 0

        lax.fori_loop(1, 8, wait_ring, 0)
        total = recv3[h][0].astype(F32)
        for s in range(1, 8):
            total = total + recv3[h][s].astype(F32)
        if h == 0:
            swap_out[...] = jnp.concatenate([total[56:64], jnp.zeros((8, LANES), F32)], axis=0).astype(BF16)
            swap_copy().start()
            scale = jnp.maximum(total[0:8, :], 1.0)
            swap_copy().wait_recv()
            split = total[48:56, :] + swap_in[...].astype(F32)[0:8]
            total = jnp.concatenate([total[8:48, :], split], axis=0)
        first, end = CHUNK[h]
        bands = end - first
        mean = [(total[8 * b : 8 * b + 8, :] / scale).astype(BF16).astype(F32) for b in range(bands)]

        blank = jnp.zeros((8, LANES), F32)
        pixel = lax.broadcasted_iota(jnp.int32, (LANES, LANES), 0)
        spot = lax.broadcasted_iota(jnp.int32, (LANES, LANES), 1)
        lefts, mixes = [], []
        for g in range(min(4, bands)):
            lefts.append(jnp.concatenate([mean[g], mean[4 + g] if 4 + g < bands else blank], axis=0).astype(BF16))
            mixes.append(jnp.where(spot == 32 * g + ((pixel & 63) >> 1), 0.25, 0.0).astype(BF16))
        pooled = jnp.dot(
            jnp.concatenate(lefts, axis=1), jnp.concatenate(mixes, axis=0), preferred_element_type=F32
        )
        pool[h] = pooled.astype(BF16)

        def send_line(z2, _):
            @pl.when(jnp.logical_not(stays(z2)))
            def _():
                line_copy(h, z2).start()
            return 0

        lax.fori_loop(0, 8, send_line, 0)
        spare = ROWS[h] // 8 - bands
        means[h][...] = jnp.concatenate(mean[0:bands] + [blank] * spare, axis=0).astype(BF16)

        @pl.when(jnp.logical_not(stays(my_row)))
        def _():
            comp_copy(h).start()

        @pl.when(stays(my_row))
        def _():
            comp[h][...] = means[h][...]

        @pl.when(at_home)
        def _():
            line[h, my_row] = pool[h]
        return scale

    def plane_device(i):
        xc2 = lax.rem(xc + i, 8)
        return xc2, (z_lo * 8 + xc2, tile)

    def plane_copy(h, i):
        return pltpu.make_async_remote_copy(
            src_ref=whole_line[h], dst_ref=rows[h].at[xc], send_sem=sg2_sem.at[h, i], recv_sem=rg2_sem.at[h, xc],
            device_id=plane_device(i)[1], device_id_type=MESH,
        )

    def spread_line(h):
        def wait_line(j, _):
            @pl.when(jnp.logical_not(jnp.logical_and(at_home, j == my_row)))
            def _():
                pltpu.make_async_remote_copy(
                    src_ref=pool.at[h], dst_ref=line.at[h, j], send_sem=sg1_sem.at[h, j], recv_sem=rg1_sem.at[h, j],
                    device_id=maker_device(j), device_id_type=MESH,
                ).wait_recv()
            return 0

        lax.fori_loop(0, 8, wait_line, 0)
        if h == 1:
            for q in range(4):
                both = [line[1, 2 * q + i].astype(F32)[0:8] for i in range(2)]
                packed[16 * q : 16 * q + 16, :] = jnp.concatenate(both, axis=0).astype(BF16)

        def send_plane(i, _):
            plane_copy(h, i).start()
            return 0

        lax.fori_loop(1, 8, send_plane, 0)
        rows[h][xc] = whole_line[h][...]

    def drain_box(h):
        def drain(slot, same):
            box_copy(h, same, slot, other_core).wait_send()

        each_pair(0, BOX - 1, drain)

    def drain_ring(h):
        def drain(i, _):
            ring_copy(h, i).wait_send()
            return 0

        lax.fori_loop(1, 8, drain, 0)

    def drain_line(h):
        @pl.when(jnp.logical_not(stays(my_row)))
        def _():
            comp_copy(h).wait_send()

        @pl.when(jnp.logical_not(jnp.logical_and(at_home, my_row == z_lo)))
        def _():
            pltpu.make_async_remote_copy(
                src_ref=means[h], dst_ref=comp[h], send_sem=sc_sem.at[h], recv_sem=rc_sem.at[h],
                device_id=maker_device(z_lo), device_id_type=MESH,
            ).wait_recv()

        def drain(z2, _):
            @pl.when(jnp.logical_not(stays(z2)))
            def _():
                line_copy(h, z2).wait_send()
            return 0

        lax.fori_loop(0, 8, drain, 0)

    def wait_plane(h):
        def wait(i, _):
            xc2, device = plane_device(i)
            pltpu.make_async_remote_copy(
                src_ref=whole_line[h], dst_ref=rows[h].at[xc2], send_sem=sg2_sem.at[h, i], recv_sem=rg2_sem.at[h, xc2],
                device_id=device, device_id_type=MESH,
            ).wait_recv()
            return 0

        lax.fori_loop(1, 8, wait, 0)

    def drain_plane(h):
        def drain(i, _):
            plane_copy(h, i).wait_send()
            return 0

        lax.fori_loop(1, 8, drain, 0)

    reduce_box(0)
    drain_box(0)
    reduce_box(1)
    drain_box(1)
    scale = finish_mean(0, None)
    drain_ring(0)
    finish_mean(1, scale)
    drain_ring(1)
    swap_copy().wait_send()
    spread_line(0)
    spread_line(1)
    wait_plane(0)
    _, _, mix, unit = matrices()
    level = [rows_a[i].astype(F32) for i in range(8)]
    fourth[...] = overviews(0, level, mix, unit, (t1, t2, t3), (one, two, three), lambda depth: None)
    for h in range(2):
        drain_line(h)
    drain_plane(0)
    wait_plane(1)
    drain_plane(1)


def exchange(radiance, cloud_weight, footprint):
    any_space = pl.BlockSpec(memory_space=pl.ANY)
    vmem = pl.BlockSpec(memory_space=pltpu.VMEM)
    dma = pltpu.SemaphoreType.DMA
    return pl.pallas_call(
        exchange_kernel,
        out_shape=(
            jax.ShapeDtypeStruct((8, 64, LANES), BF16),
            *(jax.ShapeDtypeStruct((8, CHUNK[0][1], 32 >> i, 64 >> i), BF16) for i in range(3)),
            jax.ShapeDtypeStruct((8, 16, LANES), F32),
            *(jax.ShapeDtypeStruct((rows, LANES), BF16) for rows in ROWS),
        ),
        in_specs=[any_space] * 3,
        out_specs=(vmem,) * 7,
        scratch_shapes=[
            pltpu.VMEM((BANDS, K, PIX), BF16),
            pltpu.VMEM((K, PIX), jnp.int32),
            pltpu.VMEM((K, 128), jnp.int32),
            *(pltpu.VMEM((BOX, rows, LANES), BF16) for rows in ROWS * 2),
            pltpu.VMEM((128, 16 * BOX), BF16),
            pltpu.VMEM((128, 4 * LANES), F32),
            *(pltpu.VMEM((8, rows, LANES), BF16) for rows in ROWS * 2),
            *(pltpu.VMEM((rows, LANES), BF16) for rows in ROWS),
            *(pltpu.VMEM(shape, BF16) for shape in ((2, 16, LANES), (16, LANES), (16, LANES))),
            pltpu.VMEM((2, 8, 16, LANES), BF16),
            pltpu.VMEM((64, LANES), BF16),
            pltpu.VMEM((8, 8, 16, LANES), BF16),
            *(pltpu.VMEM((16 * (64 >> i), LANES), F32) for i in range(3)),
            pltpu.SemaphoreType.REGULAR((2,)),
            dma((3,)),
            dma((2, BOX)),
            dma((2, BOX)),
            dma((2, 8)),
            dma((2, 8)),
            dma((2, 8)),
            dma((2, 8)),
            dma((2, 8)),
            dma((2, 8)),
            dma((2,)),
            dma((2,)),
            dma((2,)),
        ],
        compiler_params=pltpu.CompilerParams(
            collective_id=0, has_side_effects=True, vmem_limit_bytes=16 * 1024 * 1024
        ),
        name="exchange",
    )(*(pltpu.with_memory_space_constraint(a, pltpu.HBM) for a in (jnp.transpose(radiance, (0, 2, 1, 3)), cloud_weight, footprint.T)))


def pyramid_kernel(rows_b, one_a, two_a, three_a, fourth_a, comp_a, comp_b, *refs):
    outs, (composite, four, five), parts, scratches, sems = refs[:6], refs[6:9], refs[9:12], refs[12:15], refs[15]
    early = [
        pltpu.make_async_copy(part, outs[1 + i].at[:, 0 : CHUNK[0][1]], sems.at[i]) for i, part in enumerate((one_a, two_a, three_a))
    ]
    late = [pltpu.make_async_copy(part, outs[1 + i].at[:, CHUNK[1][0] : BANDS], sems.at[3 + i]) for i, part in enumerate(parts)]
    rest = [pltpu.make_async_copy(part, outs[i], sems.at[6 + k]) for k, (part, i) in enumerate(((composite, 0), (four, 4), (five, 5)))]
    for copy in early:
        copy.start()
    for comp, (first, end) in zip((comp_a, comp_b), CHUNK):
        lines = comp[...].astype(F32)[0 : 8 * (end - first)]
        composite[first:end] = lines.reshape(end - first, 8, LANES).astype(BF16)
    rest[0].start()

    before, after, mix, unit = matrices()
    level = [rows_b[i].astype(F32).reshape(8, 8, LANES) for i in range(8)]
    fourth_b = overviews(1, level, mix, unit, scratches, parts, lambda depth: None)
    for copy in late:
        copy.start()
    fourth, fifth = [fourth_a[...], fourth_b], []
    for values in fourth:
        last = halve(values, mix).reshape(4, 2, -1, LANES)
        fifth.append((last[:, 0] + last[:, 1]).astype(BF16).astype(F32))

    for values, out, height, width in ((fourth, four, 8, 4), (fifth, five, 4, 2)):
        columns = []
        for c in range(width):
            total = None
            for h, line, (first, bands) in ((0, 0, GROUPS[0][0]), (0, 8, GROUPS[0][1]), (1, 0, GROUPS[1][0])):
                group = before >> 5
                spread = jnp.where(
                    jnp.logical_and(
                        jnp.logical_and((before & 31) == c, after == first + group), group < bands
                    ),
                    1.0, 0.0,
                ).astype(BF16)
                left = values[h][:, line : line + 8, :].reshape(8 * height, LANES).astype(BF16)
                part = jnp.dot(left, spread, preferred_element_type=F32)
                total = part if total is None else total + part
            columns.append(total)
        stacked = jnp.concatenate(columns, axis=0).astype(BF16)
        shape = (64 * height, 8 * height * width)
        to = lax.broadcasted_iota(jnp.int32, shape, 0)
        of = lax.broadcasted_iota(jnp.int32, shape, 1)
        high = {8: 3, 4: 2}[height]
        t, r, c = to >> (3 + high), (to >> 3) & (height - 1), to & 7
        order = jnp.where(of == c * (8 * height) + r * 8 + t, 1.0, 0.0).astype(BF16)
        placed = jnp.dot(order, stacked, preferred_element_type=F32)
        for t in range(8):
            for r in range(height):
                at = 8 * (t * height + r)
                out[t, r] = placed[at : at + width, 0:BANDS].astype(BF16)
        rest[1 if height == 8 else 2].start()
    for copy in early + late + rest:
        copy.wait()


def pyramid(*parts):
    vmem = pl.BlockSpec(memory_space=pltpu.VMEM)
    shapes = [(BANDS, 8, LANES)] + [(8, BANDS, 32 >> i, 64 >> i) for i in range(3)] + [(8, 8, 4, BANDS), (8, 4, 2, BANDS)]
    outs = pl.pallas_call(
        pyramid_kernel,
        out_shape=[jax.ShapeDtypeStruct(s, BF16) for s in shapes],
        in_specs=[vmem] * 7,
        out_specs=[pl.BlockSpec(memory_space=pl.ANY)] * 6,
        scratch_shapes=[pltpu.VMEM(shapes[i], BF16) for i in (0, 4, 5)]
        + [pltpu.VMEM((8, BANDS - CHUNK[1][0], 32 >> i, 64 >> i), BF16) for i in range(3)]
        + [pltpu.VMEM((8 * (64 >> i), LANES), F32) for i in range(3)]
        + [pltpu.SemaphoreType.DMA((9,))],
        compiler_params=pltpu.CompilerParams(vmem_limit_bytes=16 * 1024 * 1024),
        name="pyramid",
    )(*parts)
    orders = [(1, 0, 2)] + [(0, 1, 3, 2)] * 3 + [(0, 3, 1, 2)] * 2
    return tuple(jnp.transpose(out, order) for out, order in zip(outs, orders))


def on_device(radiance, cloud_weight, footprint):
    return pyramid(*exchange(radiance, cloud_weight, footprint))


def solution(mesh):
    in_specs = (P(("scene", "tile"), None, None, None), P(("scene", "tile"), None, None), P())
    out_specs = (
        P("tile", None, "scene"),
        P("tile", None, None, None),
        P("tile", None, None, None),
        P("tile", None, None, None),
        P("tile", None, None, None),
        P("tile", None, None, None),
    )
    return jax.shard_map(
        on_device, mesh=mesh, in_specs=in_specs, out_specs=out_specs, check_vma=False
    )
```

```python
import functools

import jax
import jax.numpy as jnp
from jax import lax
from jax.experimental import pallas as pl
from jax.experimental.pallas import tpu as pltpu
from jax.sharding import PartitionSpec as P

MESH = pl.DeviceIdType.MESH
K = 8
BANDS = 10
TILES = 64
PIX = 8192
LANES = 128
ROWS = (64, 32)
SHORT = 48
CHUNK = ((0, 6), (6, 10))
BOX = 64
F32 = jnp.float32
BF16 = jnp.bfloat16


STEPS = (
    (2, 2), (2, 1), (1, 2), (2, 3), (3, 2), (2, 0), (1, 1), (0, 2), (3, 3), (1, 3), (3, 1), (1, 0), (0, 1), (3, 0), (0, 3),
)
STEPS_X = sum(step[0] * 4**n for n, step in enumerate(STEPS))
STEPS_Y = sum(step[1] * 4**n for n, step in enumerate(STEPS))


GROUPS = (((0, 4), (4, 2)), ((6, 4),))


def matrices():
    before = lax.broadcasted_iota(jnp.int32, (LANES, LANES), 0)
    after = lax.broadcasted_iota(jnp.int32, (LANES, LANES), 1)
    same = (before >> 5) == (after >> 5)
    mix = jnp.where(jnp.logical_and(same, ((before & 31) >> 1) == (after & 31)), 0.25, 0.0).astype(BF16)
    unit = jnp.where(before == after, 1.0, 0.0).astype(BF16)
    return before, after, mix, unit


def halve(values, mix):
    flat = values.reshape(-1, LANES).astype(BF16)
    return jnp.dot(flat, mix, preferred_element_type=F32).reshape(values.shape)


def overviews(h, level, mix, unit, scratches, outs, done):
    lines = 8 * len(GROUPS[h])
    base = CHUNK[h][0]
    for depth in range(4):
        m = 8 >> depth
        if depth:
            level = [(halve(level[2 * q], mix) + halve(level[2 * q + 1], mix)).astype(BF16).astype(F32) for q in range(m)]
        if depth == 3:
            return level[0]
        scratch, out = scratches[depth], outs[depth]
        for q in range(m):
            for i in range(8):
                at = (i * m + q) * lines
                scratch[at : at + lines, :] = level[q][i]
        for r in range(lines):
            first, bands = GROUPS[h][r // 8]
            picked = scratch[pl.ds(r, 8 * m, stride=lines), :].astype(BF16)
            turned = lax.dot_general(
                unit[0 : 32 * bands], picked, (((1,), (1,)), ((), ())), preferred_element_type=F32
            )
            for g in range(bands):
                out[r % 8, first - base + g] = turned[32 * g : 32 * g + 4 * m].astype(BF16)
        done(depth)


def position():
    scene = lax.axis_index("scene")
    tile = lax.axis_index("tile")
    z_lo = lax.div(scene, 8)
    x = lax.rem(lax.div(scene, 2), 4)
    core = lax.rem(scene, 2)
    z_hi = lax.div(tile, 4)
    y = lax.rem(tile, 4)
    return z_lo, x, core, z_hi, y


def exchange_kernel(
    rad_ref, weight_ref, foot_ref, rows_b, one, two, three, fourth, comp_a, comp_b,
    rad, weight, foot, send_a, send_b, recv_a, recv_b, assign, acc, send3_a, send3_b, recv3_a, recv3_b, mean_a, mean_b, pool, swap_out, swap_in, line, packed, rows_a, t1, t2, t3,
    ring_sem, in_sem, send_sem, recv_sem, send3_sem, recv3_sem, sg1_sem, rg1_sem, sg2_sem, rg2_sem, sc_sem, rc_sem, swap_sem,
):
    send, recv, send3, recv3 = (send_a, send_b), (recv_a, recv_b), (send3_a, send3_b), (recv3_a, recv3_b)
    z_lo, x, core, z_hi, y = position()
    tile = z_hi * 4 + y
    xc = x * 2 + core
    pair = lax.div(z_lo, 2)
    odd = lax.rem(z_lo, 2)

    load_foot = pltpu.make_async_copy(foot_ref.at[:, pl.ds(pl.multiple_of(pair * 128, 128), 128)], foot, in_sem.at[2])
    load_weight = pltpu.make_async_copy(weight_ref.at[0], weight, in_sem.at[1])
    load_rad = pltpu.make_async_copy(rad_ref.at[0], rad, in_sem.at[0])
    load_weight.start()
    load_rad.start()
    load_foot.start()

    def box_device(x2, y2, c2, o2):
        block = (2 * y2 + o2) * 8 + x2 * 2 + c2
        return block, ((2 * pair + o2) * 8 + x2 * 2 + c2, z_hi * 4 + y2)

    def each_partner(visit):
        def four(n, x2, y2, count):
            for u in range(count):
                visit(4 * n + u, u % 2, x2, y2, core if u % 2 else 1 - core, odd if u // 2 else 1 - odd)

        def outer(n, carry):
            in_x, in_y = carry
            four(n, lax.rem(x + lax.rem(in_x, 4), 4), lax.rem(y + lax.rem(in_y, 4), 4), 4)
            return lax.div(in_x, 4), lax.div(in_y, 4)

        lax.fori_loop(0, 15, outer, (jnp.int32(STEPS_X), jnp.int32(STEPS_Y)))
        four(15, x, y, 3)

    ring = z_hi * 4 + pair

    def ring_device(step):
        box = lax.rem(ring + step, 8)
        return ((2 * lax.rem(box, 4) + odd) * 8 + xc, lax.div(box, 4) * 4 + y)

    group = lax.rem(ring + 2, 8)
    home = lax.rem(tile + 6, 8)
    comp, means = (comp_a, comp_b), (mean_a, mean_b)
    whole_line, rows = (line.at[0], packed), (rows_a, rows_b)

    def maker_device(j):
        return ((2 * lax.rem(home, 4) + lax.rem(j, 2)) * 8 + xc, lax.div(home, 4) * 4 + lax.div(j, 2))

    my_row = 2 * y + odd
    at_home = group == tile

    barrier = pltpu.get_barrier_semaphore()

    def greet(slot, same, *offset):
        pl.semaphore_signal(barrier, inc=1, device_id=box_device(*offset)[1], device_id_type=MESH)

    each_partner(greet)

    def clear(n, _):
        recv_a[2 * n, SHORT:64] = jnp.zeros((16, LANES), BF16)
        return 0

    lax.fori_loop(0, BOX // 2, clear, 0)
    for step in (1, 7):
        pl.semaphore_signal(barrier, inc=1, device_id=ring_device(step), device_id_type=MESH)

    def tell_ring():
        pl.semaphore_signal(ring_sem.at[0], inc=1, device_id=ring_device(1), device_id_type=MESH)
        pl.semaphore_signal(ring_sem.at[1], inc=1, device_id=ring_device(7), device_id_type=MESH)

    def hear_ring():
        pl.semaphore_wait(ring_sem.at[0], 1)
        pl.semaphore_wait(ring_sem.at[1], 1)

    load_weight.wait()
    load_rad.wait()
    pl.semaphore_wait(barrier, BOX - 1 + 2)
    tell_ring()

    def fill(h, same, block, out):
        pixels = pl.ds(pl.multiple_of(block * LANES, LANES), LANES)
        w = weight[:, pixels].astype(F32)
        twice = jnp.concatenate([w, w], axis=0).astype(BF16)
        if h == 1:
            for j in range(2):
                out[16 * j : 16 * j + 16, :] = rad[2 * j + 6 : 2 * j + 8, :, pixels].reshape(16, LANES) * twice
            return
        first = jnp.concatenate([w, w * rad[0, :, pixels].astype(F32)], axis=0).astype(BF16)
        out[0:16, :] = first
        for j in range(2):
            out[16 * j + 16 : 16 * j + 32, :] = rad[2 * j + 1 : 2 * j + 3, :, pixels].reshape(16, LANES) * twice
        if same:
            beside = pl.ds(pl.multiple_of((block + 1 - 2 * core) * LANES, LANES), LANES)
            mine = w * rad[5, :, pixels].astype(F32)
            theirs = weight[:, beside].astype(F32) * rad[5, :, beside].astype(F32)
            out[48:64, :] = jnp.concatenate([mine, theirs], axis=0).astype(BF16)

    def box_copy(h, same, slot, device):
        source, target = send[h].at[slot], recv[h].at[slot]
        if h == 0 and not same:
            source, target = send[h].at[slot, 0:SHORT], recv[h].at[slot, 0:SHORT]
        return pltpu.make_async_remote_copy(
            src_ref=source, dst_ref=target,
            send_sem=send_sem.at[h, slot], recv_sem=recv_sem.at[h, slot],
            device_id=device, device_id_type=MESH,
        )

    def each_pair(first, end, visit):
        def pair_of(n, _):
            visit(2 * n, 0)
            visit(2 * n + 1, 1)
            return 0

        lax.fori_loop(first // 2, end // 2, pair_of, 0)
        if end % 2:
            visit(end - 1, 0)

    other_core = box_device(x, y, 1 - core, odd)[1]

    for h in range(2):
        def send_box(slot, same, *offset, h=h):
            block, device = box_device(*offset)
            fill(h, same, block, send[h].at[slot])
            box_copy(h, same, slot, device).start()

        each_partner(send_box)
        fill(h, 1, my_row * 8 + xc, recv[h].at[BOX - 1])
        hear_ring()
        tell_ring()

    load_foot.wait()
    lane = lax.broadcasted_iota(jnp.int32, (1, 16 * BOX), 1)
    slot = lane >> 4
    step = slot >> 2
    dx, dy = jnp.zeros_like(slot), jnp.zeros_like(slot)
    for n, (far_x, far_y) in enumerate(STEPS):
        dx = jnp.where(step == n, far_x, dx)
        dy = jnp.where(step == n, far_y, dy)
    source_row = (
        (((odd + 1 - ((slot >> 1) & 1)) & 1) << 6)
        + (((x - dx) & 3) << 4)
        + (((core + 1 - (slot & 1)) & 1) << 3)
        + ((y - dy) & 3)
        + z_hi * 4
    )
    pick = jnp.where(lax.broadcasted_iota(jnp.int32, (128, 16 * BOX), 0) == source_row, 1.0, 0.0).astype(BF16)
    named = jnp.dot(foot[...].astype(F32).astype(BF16), pick, preferred_element_type=F32)
    own = lax.broadcasted_iota(jnp.int32, (K, 16 * BOX), 0) == (lane & 7)
    target = jnp.sum(jnp.where(own, named, 0.0), axis=0, keepdims=True).astype(jnp.int32) + ((lane & 8) << 3)
    row = lax.broadcasted_iota(jnp.int32, (128, 16 * BOX), 0)
    assign[...] = jnp.where(row == target, 1.0, 0.0).astype(BF16)
    hear_ring()
    tell_ring()

    def ring_copy(h, i):
        return pltpu.make_async_remote_copy(
            src_ref=send3[h].at[lax.rem(group + i, 8)], dst_ref=recv3[h].at[ring],
            send_sem=send3_sem.at[h, i], recv_sem=recv3_sem.at[h, ring],
            device_id=ring_device(i), device_id_type=MESH,
        )

    def reduce_box(h):
        def wait_box(slot, same):
            box_copy(h, same, slot, other_core).wait_recv()

        for g in range(4):
            each_pair(16 * g, min(16 * g + 16, BOX - 1), wait_box)
            left = assign[:, 256 * g : 256 * g + 256]
            right = jnp.concatenate(
                [recv[h][16 * g : 16 * g + 16, 16 * j : 16 * j + 16, :].reshape(256, LANES) for j in range(ROWS[h] // 16)],
                axis=1,
            )
            part = jnp.dot(left, right, preferred_element_type=F32)
            if g == 0:
                acc[:, 0 : 8 * ROWS[h]] = part
            else:
                acc[:, 0 : 8 * ROWS[h]] += part

        for o in range(8):
            for j in range(ROWS[h] // 16):
                lanes = slice(LANES * j, LANES * j + LANES)
                both = jnp.concatenate([acc[8 * o : 8 * o + 8, lanes], acc[64 + 8 * o : 72 + 8 * o, lanes]], axis=0)
                send3[h][o, 16 * j : 16 * j + 16, :] = both.astype(BF16)

        if h == 0:
            hear_ring()

        def send_ring(i, _):
            ring_copy(h, 4 + lax.div(i, 2) * (1 - 2 * lax.rem(i, 2))).start()
            return 0

        lax.fori_loop(1, 8, send_ring, 0)
        recv3[h][ring] = send3[h][group]

    def line_copy(h, z2):
        return pltpu.make_async_remote_copy(
            src_ref=pool.at[h], dst_ref=line.at[h, my_row], send_sem=sg1_sem.at[h, z2], recv_sem=rg1_sem.at[h, my_row],
            device_id=(z2 * 8 + xc, group), device_id_type=MESH,
        )

    def comp_copy(h):
        return pltpu.make_async_remote_copy(
            src_ref=means[h], dst_ref=comp[h], send_sem=sc_sem.at[h], recv_sem=rc_sem.at[h],
            device_id=(my_row * 8 + xc, group), device_id_type=MESH,
        )

    def swap_copy():
        return pltpu.make_async_remote_copy(
            src_ref=swap_out, dst_ref=swap_in, send_sem=swap_sem.at[0], recv_sem=swap_sem.at[1],
            device_id=other_core, device_id_type=MESH,
        )

    def stays(z2):
        return jnp.logical_and(at_home, z2 == z_lo)

    def finish_mean(h, scale):
        def wait_ring(i, _):
            s = lax.rem(ring + i, 8)
            pltpu.make_async_remote_copy(
                src_ref=send3[h].at[s], dst_ref=recv3[h].at[s],
                send_sem=send3_sem.at[h, i], recv_sem=recv3_sem.at[h, s],
                device_id=ring_device(i), device_id_type=MESH,
            ).wait_recv()
            return 0

        lax.fori_loop(1, 8, wait_ring, 0)
        total = recv3[h][0].astype(F32)
        for s in range(1, 8):
            total = total + recv3[h][s].astype(F32)
        if h == 0:
            swap_out[...] = jnp.concatenate([total[56:64], jnp.zeros((8, LANES), F32)], axis=0).astype(BF16)
            swap_copy().start()
            scale = jnp.maximum(total[0:8, :], 1.0)
            swap_copy().wait_recv()
            split = total[48:56, :] + swap_in[...].astype(F32)[0:8]
            total = jnp.concatenate([total[8:48, :], split], axis=0)
        first, end = CHUNK[h]
        bands = end - first
        mean = [(total[8 * b : 8 * b + 8, :] / scale).astype(BF16).astype(F32) for b in range(bands)]

        blank = jnp.zeros((8, LANES), F32)
        pixel = lax.broadcasted_iota(jnp.int32, (LANES, LANES), 0)
        spot = lax.broadcasted_iota(jnp.int32, (LANES, LANES), 1)
        lefts, mixes = [], []
        for g in range(min(4, bands)):
            lefts.append(jnp.concatenate([mean[g], mean[4 + g] if 4 + g < bands else blank], axis=0).astype(BF16))
            mixes.append(jnp.where(spot == 32 * g + ((pixel & 63) >> 1), 0.25, 0.0).astype(BF16))
        pooled = jnp.dot(
            jnp.concatenate(lefts, axis=1), jnp.concatenate(mixes, axis=0), preferred_element_type=F32
        )
        pool[h] = pooled.astype(BF16)

        def send_line(z2, _):
            @pl.when(jnp.logical_not(stays(z2)))
            def _():
                line_copy(h, z2).start()
            return 0

        lax.fori_loop(0, 8, send_line, 0)
        spare = ROWS[h] // 8 - bands
        means[h][...] = jnp.concatenate(mean[0:bands] + [blank] * spare, axis=0).astype(BF16)

        @pl.when(jnp.logical_not(stays(my_row)))
        def _():
            comp_copy(h).start()

        @pl.when(stays(my_row))
        def _():
            comp[h][...] = means[h][...]

        @pl.when(at_home)
        def _():
            line[h, my_row] = pool[h]
        return scale

    def plane_device(i):
        xc2 = lax.rem(xc + i, 8)
        return xc2, (z_lo * 8 + xc2, tile)

    def plane_copy(h, i):
        return pltpu.make_async_remote_copy(
            src_ref=whole_line[h], dst_ref=rows[h].at[xc], send_sem=sg2_sem.at[h, i], recv_sem=rg2_sem.at[h, xc],
            device_id=plane_device(i)[1], device_id_type=MESH,
        )

    def spread_line(h):
        def wait_line(j, _):
            @pl.when(jnp.logical_not(jnp.logical_and(at_home, j == my_row)))
            def _():
                pltpu.make_async_remote_copy(
                    src_ref=pool.at[h], dst_ref=line.at[h, j], send_sem=sg1_sem.at[h, j], recv_sem=rg1_sem.at[h, j],
                    device_id=maker_device(j), device_id_type=MESH,
                ).wait_recv()
            return 0

        lax.fori_loop(0, 8, wait_line, 0)
        if h == 1:
            for q in range(4):
                both = [line[1, 2 * q + i].astype(F32)[0:8] for i in range(2)]
                packed[16 * q : 16 * q + 16, :] = jnp.concatenate(both, axis=0).astype(BF16)

        def send_plane(i, _):
            plane_copy(h, 4 + lax.div(i, 2) * (1 - 2 * lax.rem(i, 2))).start()
            return 0

        lax.fori_loop(1, 8, send_plane, 0)
        rows[h][xc] = whole_line[h][...]

    def drain_box(h):
        def drain(slot, same):
            box_copy(h, same, slot, other_core).wait_send()

        each_pair(0, BOX - 1, drain)

    def drain_ring(h):
        def drain(i, _):
            ring_copy(h, i).wait_send()
            return 0

        lax.fori_loop(1, 8, drain, 0)

    def drain_line(h):
        @pl.when(jnp.logical_not(stays(my_row)))
        def _():
            comp_copy(h).wait_send()

        @pl.when(jnp.logical_not(jnp.logical_and(at_home, my_row == z_lo)))
        def _():
            pltpu.make_async_remote_copy(
                src_ref=means[h], dst_ref=comp[h], send_sem=sc_sem.at[h], recv_sem=rc_sem.at[h],
                device_id=maker_device(z_lo), device_id_type=MESH,
            ).wait_recv()

        def drain(z2, _):
            @pl.when(jnp.logical_not(stays(z2)))
            def _():
                line_copy(h, z2).wait_send()
            return 0

        lax.fori_loop(0, 8, drain, 0)

    def wait_plane(h):
        def wait(i, _):
            xc2, device = plane_device(i)
            pltpu.make_async_remote_copy(
                src_ref=whole_line[h], dst_ref=rows[h].at[xc2], send_sem=sg2_sem.at[h, i], recv_sem=rg2_sem.at[h, xc2],
                device_id=device, device_id_type=MESH,
            ).wait_recv()
            return 0

        lax.fori_loop(1, 8, wait, 0)

    def drain_plane(h):
        def drain(i, _):
            plane_copy(h, i).wait_send()
            return 0

        lax.fori_loop(1, 8, drain, 0)

    reduce_box(0)
    drain_box(0)
    reduce_box(1)
    drain_box(1)
    scale = finish_mean(0, None)
    drain_ring(0)
    finish_mean(1, scale)
    drain_ring(1)
    swap_copy().wait_send()
    spread_line(0)
    spread_line(1)
    wait_plane(0)
    _, _, mix, unit = matrices()
    level = [rows_a[i].astype(F32) for i in range(8)]
    fourth[...] = overviews(0, level, mix, unit, (t1, t2, t3), (one, two, three), lambda depth: None)
    for h in range(2):
        drain_line(h)
    drain_plane(0)
    wait_plane(1)
    drain_plane(1)


def exchange(radiance, cloud_weight, footprint):
    any_space = pl.BlockSpec(memory_space=pl.ANY)
    vmem = pl.BlockSpec(memory_space=pltpu.VMEM)
    dma = pltpu.SemaphoreType.DMA
    return pl.pallas_call(
        exchange_kernel,
        out_shape=(
            jax.ShapeDtypeStruct((8, 64, LANES), BF16),
            *(jax.ShapeDtypeStruct((8, CHUNK[0][1], 32 >> i, 64 >> i), BF16) for i in range(3)),
            jax.ShapeDtypeStruct((8, 16, LANES), F32),
            *(jax.ShapeDtypeStruct((rows, LANES), BF16) for rows in ROWS),
        ),
        in_specs=[any_space] * 3,
        out_specs=(vmem,) * 7,
        scratch_shapes=[
            pltpu.VMEM((BANDS, K, PIX), BF16),
            pltpu.VMEM((K, PIX), jnp.int32),
            pltpu.VMEM((K, 128), jnp.int32),
            *(pltpu.VMEM((BOX, rows, LANES), BF16) for rows in ROWS * 2),
            pltpu.VMEM((128, 16 * BOX), BF16),
            pltpu.VMEM((128, 4 * LANES), F32),
            *(pltpu.VMEM((8, rows, LANES), BF16) for rows in ROWS * 2),
            *(pltpu.VMEM((rows, LANES), BF16) for rows in ROWS),
            *(pltpu.VMEM(shape, BF16) for shape in ((2, 16, LANES), (16, LANES), (16, LANES))),
            pltpu.VMEM((2, 8, 16, LANES), BF16),
            pltpu.VMEM((64, LANES), BF16),
            pltpu.VMEM((8, 8, 16, LANES), BF16),
            *(pltpu.VMEM((16 * (64 >> i), LANES), F32) for i in range(3)),
            pltpu.SemaphoreType.REGULAR((2,)),
            dma((3,)),
            dma((2, BOX)),
            dma((2, BOX)),
            dma((2, 8)),
            dma((2, 8)),
            dma((2, 8)),
            dma((2, 8)),
            dma((2, 8)),
            dma((2, 8)),
            dma((2,)),
            dma((2,)),
            dma((2,)),
        ],
        compiler_params=pltpu.CompilerParams(
            collective_id=0, has_side_effects=True, vmem_limit_bytes=16 * 1024 * 1024
        ),
        name="exchange",
    )(*(pltpu.with_memory_space_constraint(a, pltpu.HBM) for a in (jnp.transpose(radiance, (0, 2, 1, 3)), cloud_weight, footprint.T)))


def pyramid_kernel(rows_b, one_a, two_a, three_a, fourth_a, comp_a, comp_b, *refs):
    outs, (composite, four, five), parts, scratches, sems = refs[:6], refs[6:9], refs[9:12], refs[12:15], refs[15]
    early = [
        pltpu.make_async_copy(part, outs[1 + i].at[:, 0 : CHUNK[0][1]], sems.at[i]) for i, part in enumerate((one_a, two_a, three_a))
    ]
    late = [pltpu.make_async_copy(part, outs[1 + i].at[:, CHUNK[1][0] : BANDS], sems.at[3 + i]) for i, part in enumerate(parts)]
    rest = [pltpu.make_async_copy(part, outs[i], sems.at[6 + k]) for k, (part, i) in enumerate(((composite, 0), (four, 4), (five, 5)))]
    for copy in early:
        copy.start()
    for comp, (first, end) in zip((comp_a, comp_b), CHUNK):
        lines = comp[...].astype(F32)[0 : 8 * (end - first)]
        composite[first:end] = lines.reshape(end - first, 8, LANES).astype(BF16)
    rest[0].start()

    before, after, mix, unit = matrices()
    level = [rows_b[i].astype(F32).reshape(8, 8, LANES) for i in range(8)]
    fourth_b = overviews(1, level, mix, unit, scratches, parts, lambda depth: None)
    for copy in late:
        copy.start()
    fourth, fifth = [fourth_a[...], fourth_b], []
    for values in fourth:
        last = halve(values, mix).reshape(4, 2, -1, LANES)
        fifth.append((last[:, 0] + last[:, 1]).astype(BF16).astype(F32))

    for values, out, height, width in ((fourth, four, 8, 4), (fifth, five, 4, 2)):
        columns = []
        for c in range(width):
            total = None
            for h, line, (first, bands) in ((0, 0, GROUPS[0][0]), (0, 8, GROUPS[0][1]), (1, 0, GROUPS[1][0])):
                group = before >> 5
                spread = jnp.where(
                    jnp.logical_and(
                        jnp.logical_and((before & 31) == c, after == first + group), group < bands
                    ),
                    1.0, 0.0,
                ).astype(BF16)
                left = values[h][:, line : line + 8, :].reshape(8 * height, LANES).astype(BF16)
                part = jnp.dot(left, spread, preferred_element_type=F32)
                total = part if total is None else total + part
            columns.append(total)
        stacked = jnp.concatenate(columns, axis=0).astype(BF16)
        shape = (64 * height, 8 * height * width)
        to = lax.broadcasted_iota(jnp.int32, shape, 0)
        of = lax.broadcasted_iota(jnp.int32, shape, 1)
        high = {8: 3, 4: 2}[height]
        t, r, c = to >> (3 + high), (to >> 3) & (height - 1), to & 7
        order = jnp.where(of == c * (8 * height) + r * 8 + t, 1.0, 0.0).astype(BF16)
        placed = jnp.dot(order, stacked, preferred_element_type=F32)
        for t in range(8):
            for r in range(height):
                at = 8 * (t * height + r)
                out[t, r] = placed[at : at + width, 0:BANDS].astype(BF16)
        rest[1 if height == 8 else 2].start()
    for copy in early + late + rest:
        copy.wait()


def pyramid(*parts):
    vmem = pl.BlockSpec(memory_space=pltpu.VMEM)
    shapes = [(BANDS, 8, LANES)] + [(8, BANDS, 32 >> i, 64 >> i) for i in range(3)] + [(8, 8, 4, BANDS), (8, 4, 2, BANDS)]
    outs = pl.pallas_call(
        pyramid_kernel,
        out_shape=[jax.ShapeDtypeStruct(s, BF16) for s in shapes],
        in_specs=[vmem] * 7,
        out_specs=[pl.BlockSpec(memory_space=pl.ANY)] * 6,
        scratch_shapes=[pltpu.VMEM(shapes[i], BF16) for i in (0, 4, 5)]
        + [pltpu.VMEM((8, BANDS - CHUNK[1][0], 32 >> i, 64 >> i), BF16) for i in range(3)]
        + [pltpu.VMEM((8 * (64 >> i), LANES), F32) for i in range(3)]
        + [pltpu.SemaphoreType.DMA((9,))],
        compiler_params=pltpu.CompilerParams(vmem_limit_bytes=16 * 1024 * 1024),
        name="pyramid",
    )(*parts)
    orders = [(1, 0, 2)] + [(0, 1, 3, 2)] * 3 + [(0, 3, 1, 2)] * 2
    return tuple(jnp.transpose(out, order) for out, order in zip(outs, orders))


def on_device(radiance, cloud_weight, footprint):
    return pyramid(*exchange(radiance, cloud_weight, footprint))


def solution(mesh):
    in_specs = (P(("scene", "tile"), None, None, None), P(("scene", "tile"), None, None), P())
    out_specs = (
        P("tile", None, "scene"),
        P("tile", None, None, None),
        P("tile", None, None, None),
        P("tile", None, None, None),
        P("tile", None, None, None),
        P("tile", None, None, None),
    )
    return jax.shard_map(
        on_device, mesh=mesh, in_specs=in_specs, out_specs=out_specs, check_vma=False
    )
```
